32 devices in a mesh: wide: 8 (over z, y), section: 4 (over x, core).
Axes of the slice: x: 2, y: 2, z: 4, core: 2. Of those that a mesh axis runs over, the one named last changes fastest.
Arguments:
- tokens: bfloat16 [64, 200, 768], P('wide'), may hold values from -6 to 6
- cotangent: bfloat16 [64, 200, 768], P('wide'), may hold values from -6 to 6
- patch_grids: int32 [64, 2], P('wide'), may hold values from 8 to 24, as said below
- attention_gain: float32 [2, 768], replicated, may hold values from 0.1 to 1.9
- attention_shift: float32 [2, 768], replicated, may hold values from -3 to 3
- input_projection: bfloat16 [2, 768, 2304], replicated, may hold values from -0.21875 to 0.21875
- query_bias: float32 [2, 768], replicated, may hold values from -3 to 3
- value_bias: float32 [2, 768], replicated, may hold values from -3 to 3
- relative_table: float32 [2, 1269, 12], replicated, may hold values from -4 to 4
- output_projection: bfloat16 [2, 768, 768], replicated, may hold values from -0.875 to 0.875
- output_bias: float32 [2, 768], replicated, may hold values from -2 to 2
- attention_scale: float32 [2, 768], replicated, may hold values from 0.1 to 1.9
- forward_gain: float32 [2, 768], replicated, may hold values from 0.1 to 1.9
- forward_shift: float32 [2, 768], replicated, may hold values from -3 to 3
- hidden_weight: bfloat16 [2, 768, 3072], replicated, may hold values from -0.21875 to 0.21875
- hidden_bias: float32 [2, 3072], replicated, may hold values from -3 to 3
- return_weight: bfloat16 [2, 3072, 768], replicated, may hold values from -0.109375 to 0.109375
- return_bias: float32 [2, 768], replicated, may hold values from -2 to 2
- forward_scale: float32 [2, 768], replicated, may hold values from 0.1 to 1.9
Outputs:
- layer_output: bfloat16 [64, 200, 768], P('wide', None, 'section')
- input_grad: bfloat16 [64, 200, 768], P('wide', None, 'section')
- attention_gain_grad: float32 [2, 768], P(None, 'section')
- attention_shift_grad: float32 [2, 768], P(None, 'section')
- input_projection_grad: float32 [2, 768, 2304], P(None, 'wide', 'section')
- query_bias_grad: float32 [2, 768], P(None, 'section')
- value_bias_grad: float32 [2, 768], P(None, 'section')
- relative_table_grad: float32 [2, 1269, 12], P(None, None, 'section')
- output_projection_grad: float32 [2, 768, 768], P(None, 'wide', 'section')
- output_bias_grad: float32 [2, 768], P(None, 'section')
- attention_scale_grad: float32 [2, 768], P(None, 'section')
- forward_gain_grad: float32 [2, 768], P(None, 'section')
- forward_shift_grad: float32 [2, 768], P(None, 'section')
- hidden_weight_grad: float32 [2, 768, 3072], P(None, 'wide', 'section')
- hidden_bias_grad: float32 [2, 3072], P(None, 'section')
- return_weight_grad: float32 [2, 3072, 768], P(None, 'section', 'wide')
- return_bias_grad: float32 [2, 768], P(None, 'section')
- forward_scale_grad: float32 [2, 768], P(None, 'section')
The draws below stay inside these ranges and needn't reach their ends.
Inputs may be any that keep to these rules, and one draw needn't show every extreme that they name: `patch_grids`: each row is an image's patch grid (rows, columns): one of (14, 14), (10, 20) and (8, 24); all three occur.
All inputs are finite; a program needn't handle non-finite values.
Results may differ from the reference program's by a relative error of at most 0.018.
Values may be sent and summed in bfloat16 or wider, within the bound.
No kernel may reach another device: no remote copies, remote signals or barrier semaphores. Data moves between devices by JAX's collectives and lax.ppermute only.
A program may use at most 320 MiB of HBM per device.

```python
import jax
import jax.numpy as jnp
from jax import lax

D = 768
HEADS = 12
HEAD = 64
FF = 3072
ROWS = 200
HMAX = 14
WMAX = 24
REL = 1269
LAYERS = 2
IMG_DEV = 8
IMAGES = 64
N_WIDE = 8


def draw_patch_grids(key, part):
    key = jax.random.fold_in(key, 7)
    first_key, later_key = jax.random.split(key)
    leading = jax.random.permutation(first_key, 3)
    others = jax.random.randint(later_key, (IMAGES - 3,), 0, 3)
    grid_kind = jnp.concatenate([leading, others]).astype(jnp.int32)
    heights = jnp.array([14, 10, 8], jnp.int32)
    widths = jnp.array([14, 20, 24], jnp.int32)
    return jnp.stack([heights[grid_kind], widths[grid_kind]], axis=1)


def levels(stream_key, extent, pieces, least, top_value):
    gain = 1.0
    for dim, shards_of in pieces:
        draws = jax.random.uniform(jax.random.fold_in(jax.random.fold_in(stream_key, 6), dim), (shards_of,), jnp.float32, least / len(pieces), top_value / len(pieces))
        gain = gain * jnp.repeat(jnp.exp(draws), extent[dim] // shards_of).reshape((-1,) + (1,) * (len(extent) - 1 - dim))
    return gain


def gaussian(key, shape, deviation, limit, pieces=(), held_as=jnp.bfloat16):
    gain = levels(key, shape, pieces, -0.22, 0.18) if pieces else 1.0
    drawn = jax.random.normal(key, shape, jnp.float32) * deviation * gain
    return jnp.minimum(jnp.maximum(drawn, -limit), limit).astype(held_as)


def setup_inputs(seed: int = 0) -> dict:
    arg_keys = jax.random.split(jax.random.key(seed), 20)
    return {
        "tokens": gaussian(arg_keys[0], (IMAGES, ROWS, D), 1.0, 6.0, ((0, 8),)),
        "cotangent": gaussian(arg_keys[1], (IMAGES, ROWS, D), 1.0, 6.0, ((0, 8),)),
        "patch_grids": draw_patch_grids(jax.random.fold_in(arg_keys[19], 71), 0),
        "attention_gain": jnp.clip(1.0 + 0.18 * jax.random.normal(arg_keys[3], (LAYERS, D), jnp.float32), 0.1, 1.9),
        "attention_shift": gaussian(arg_keys[4], (LAYERS, D), 0.5, 3.0, (), jnp.float32),
        "input_projection": gaussian(arg_keys[5], (LAYERS, D, 3 * D), D ** -0.5, 0.21875),
        "query_bias": gaussian(arg_keys[6], (LAYERS, D), 0.5, 3.0, (), jnp.float32),
        "value_bias": gaussian(arg_keys[7], (LAYERS, D), 0.5, 3.0, (), jnp.float32),
        "relative_table": gaussian(arg_keys[8], (LAYERS, REL, HEADS), 1.0, 4.0, (), jnp.float32),
        "output_projection": gaussian(arg_keys[9], (LAYERS, D, D), (D // 16) ** -0.5, 0.875),
        "output_bias": gaussian(arg_keys[10], (LAYERS, D), 0.3, 2.0, (), jnp.float32),
        "attention_scale": jnp.clip(1.0 + 0.18 * jax.random.normal(arg_keys[11], (LAYERS, D), jnp.float32), 0.1, 1.9),
        "forward_gain": jnp.clip(1.0 + 0.18 * jax.random.normal(arg_keys[12], (LAYERS, D), jnp.float32), 0.1, 1.9),
        "forward_shift": gaussian(arg_keys[13], (LAYERS, D), 0.5, 3.0, (), jnp.float32),
        "hidden_weight": gaussian(arg_keys[14], (LAYERS, D, FF), D ** -0.5, 0.21875),
        "hidden_bias": gaussian(arg_keys[15], (LAYERS, FF), 0.5, 3.0, (), jnp.float32),
        "return_weight": gaussian(arg_keys[16], (LAYERS, FF, D), FF ** -0.5, 0.109375),
        "return_bias": gaussian(arg_keys[17], (LAYERS, D), 0.3, 2.0, (), jnp.float32),
        "forward_scale": jnp.clip(1.0 + 0.18 * jax.random.normal(arg_keys[18], (LAYERS, D), jnp.float32), 0.1, 1.9),
    }


@jax.custom_vjp
def low(v):
    return lax.optimization_barrier(v.astype(jnp.bfloat16)).astype(jnp.float32)

@jax.custom_vjp
def low_back(v):
    return v

def low_keep(v):
    return (low(v), None)

def low_pass(kept, grad):
    return (grad,)

def back_keep(v):
    return (v, None)

def back_low(kept, grad):
    return (low(grad),)
low.defvjp(low_keep, low_pass)
low_back.defvjp(back_keep, back_low)

def grid_tables(patch_grids):
    position = jnp.arange(ROWS, dtype=jnp.int32)
    grid_height = patch_grids[..., 0:1]
    grid_width = patch_grids[..., 1:2]
    row_valid = position < grid_height * grid_width
    grid_row = position // grid_width
    grid_column = position % grid_width
    row_gap = jnp.clip(grid_row[..., :, None] - grid_row[..., None, :] + (HMAX - 1), 0, 2 * HMAX - 2)
    column_gap = jnp.clip(grid_column[..., :, None] - grid_column[..., None, :] + (WMAX - 1), 0, 2 * WMAX - 2)
    return (row_valid, (row_gap * (2 * WMAX - 1) + column_gap).astype(jnp.int32))

def layer_norm(values, norm_gain, norm_shift):
    centered = values - lax.optimization_barrier(jnp.mean(values, axis=-1, keepdims=True))
    spread = lax.optimization_barrier(jnp.mean(centered * centered, axis=-1, keepdims=True))
    return centered * lax.rsqrt(spread + 1e-06) * norm_gain + norm_shift

def product(inputs, matrix):
    return jnp.einsum('nrd,de->nre', inputs, matrix, precision=lax.Precision.HIGHEST)

def attention_branch(stream, params, row_valid, rel_index):
    norm_gain, norm_shift, projection, query_shift, value_shift, bias_table, out_matrix, out_shift, layer_scale = params
    image_count = stream.shape[0]
    heads_shape = (image_count, ROWS, HEADS, HEAD)
    normed = low(layer_norm(stream, norm_gain, norm_shift))
    projected_all = product(normed, projection)
    queries = low(low_back((projected_all[..., :D] + query_shift) * 0.125)).reshape(heads_shape)
    key_heads = low(low_back(projected_all[..., D:2 * D])).reshape(heads_shape)
    value_heads = low(low_back(projected_all[..., 2 * D:] + value_shift)).reshape(heads_shape)
    scores = jnp.einsum('nihe,njhe->nhij', queries, key_heads, precision=lax.Precision.HIGHEST)
    position_bias = jnp.transpose(jnp.take(bias_table, rel_index, axis=0), (0, 3, 1, 2))
    scores = low_back(scores + position_bias)
    scores = jnp.where(row_valid[:, None, None, :], scores, -1000000000.0)
    attention_weights = low(jax.nn.softmax(scores, axis=-1))
    attended = jnp.einsum('nhij,njhe->nihe', attention_weights, value_heads, precision=lax.Precision.HIGHEST)
    attended = low(low_back(attended.reshape(image_count, ROWS, D)))
    branch_out = low_back(product(attended, out_matrix) + out_shift)
    return layer_scale * branch_out * row_valid[..., None].astype(stream.dtype)

def feed_branch(stream, params, row_valid):
    norm_gain, norm_shift, hidden_matrix, hidden_shift, return_matrix, return_shift, layer_scale = params
    normed = low(layer_norm(stream, norm_gain, norm_shift))
    hidden = low_back(product(normed, hidden_matrix) + hidden_shift)
    active = low(jax.nn.gelu(hidden, approximate=False))
    branch_out = low_back(product(active, return_matrix) + return_shift)
    return layer_scale * branch_out * row_valid[..., None].astype(stream.dtype)

def network(stream, params, row_valid, rel_index):
    attention_all = params[:9]
    feed_all = params[9:]
    totals = stream
    current = stream
    for layer_index in range(LAYERS):
        attention_layer = tuple((member[layer_index] for member in attention_all))
        branch = attention_branch(current, attention_layer, row_valid, rel_index)
        totals = totals + branch
        current = low(current + branch)
        feed_layer = tuple((member[layer_index] for member in feed_all))
        branch = feed_branch(current, feed_layer, row_valid)
        totals = totals + branch
        current = low(current + branch)
    return totals

def reference(tokens, cotangent, patch_grids, attention_gain, attention_shift, input_projection, query_bias, value_bias, relative_table, output_projection, output_bias, attention_scale, forward_gain, forward_shift, hidden_weight, hidden_bias, return_weight, return_bias, forward_scale):
    weights = (attention_gain, attention_shift, input_projection, query_bias, value_bias, relative_table, output_projection, output_bias, attention_scale, forward_gain, forward_shift, hidden_weight, hidden_bias, return_weight, return_bias, forward_scale)
    params = tuple((member.astype(jnp.float32) for member in weights))
    token_blocks = tokens.reshape(N_WIDE, IMG_DEV, ROWS, D)
    cot_blocks = cotangent.reshape(N_WIDE, IMG_DEV, ROWS, D)
    grid_blocks = patch_grids.reshape(N_WIDE, IMG_DEV, 2)

    def one_block(totals, block):
        block_tokens, block_cot, block_grids = block
        row_valid, rel_index = grid_tables(block_grids)

        def forward(stream, layer_params):
            return network(stream, layer_params, row_valid, rel_index)
        output, pullback = jax.vjp(forward, block_tokens.astype(jnp.float32), params)
        stream_grad, param_grads = pullback(block_cot.astype(jnp.float32))
        totals = jax.tree.map(jnp.add, totals, param_grads)
        return (totals, (output.astype(jnp.bfloat16), stream_grad.astype(jnp.bfloat16)))
    initial = tuple((jnp.zeros_like(member) for member in params))
    totals, (outputs, grads) = lax.scan(one_block, initial, (token_blocks, cot_blocks, grid_blocks))
    return (outputs.reshape(IMAGES, ROWS, D), grads.reshape(IMAGES, ROWS, D), totals[0], totals[1], totals[2], totals[3], totals[4], totals[5], totals[6], totals[7], totals[8], totals[9], totals[10], totals[11], totals[12], totals[13], totals[14], totals[15])
```

```python
import functools

import jax
import jax.numpy as jnp
from jax import lax
from jax.experimental import pallas as pl
from jax.experimental.pallas import tpu as pltpu
from jax.sharding import PartitionSpec as P

D = 768
HEADS = 12
HEAD = 64
FF = 3072
ROWS = 200
HMAX = 14
WMAX = 24
REL = 1269
LAYERS = 2
QW = 2 * WMAX - 1
PITCH = 64
RP = 208
ROWK = HMAX * WMAX
COLK = HMAX * PITCH
TABW = 2 * HMAX * PITCH
QUAD = 4
F32 = jnp.float32
BF16 = jnp.bfloat16
NN = (((1,), (0,)), ((), ()))
NT = (((1,), (1,)), ((), ()))
TN = (((0,), (0,)), ((), ()))
VMEM = 52 * 1024 * 1024


def dot(left, right, dims=NN):
    return lax.dot_general(left, right, dims, preferred_element_type=F32)


def params(**more):
    return pltpu.CompilerParams(vmem_limit_bytes=VMEM, **more)


def whole(*shape):
    return pl.BlockSpec(shape, lambda *_: (0,) * len(shape))


def norm_stats(u):
    mean = jnp.mean(u, axis=1, keepdims=True)
    centered = u - mean
    inverse = lax.rsqrt(jnp.mean(centered * centered, axis=1, keepdims=True) + 1e-6)
    return centered * inverse, inverse


def norm_back(upstream, whitened, inverse, gain):
    scaled = upstream * gain
    first = jnp.mean(scaled, axis=1, keepdims=True)
    second = jnp.mean(scaled * whitened, axis=1, keepdims=True)
    return (scaled - first - whitened * second) * inverse


def column_sum(v):
    return jnp.sum(v, axis=0, keepdims=True)


def head_masks():
    lane = lax.broadcasted_iota(jnp.int32, (1, 2 * HEAD), 1)
    low = (lane < HEAD).astype(F32)
    return low.astype(BF16), (1.0 - low).astype(BF16)


def skewed(row):
    return pltpu.roll(jnp.broadcast_to(row, (WMAX, TABW)), 0, 1, stride=1, stride_axis=0)


def attention_forward_kernel(
    images, u_ref, total_ref, gain_ref, shift_ref, wq_ref, wk_ref, wv_ref, qb_ref, vb_ref, table_ref,
    wo_ref, ob_ref, scale_ref, live_ref, mask_ref, s_ref, pt_ref,
    next_ref, newtotal_ref, normed_ref, q_ref, k_ref, v_ref, att_ref, w_ref, branch_ref,
    acc_ref, rst_ref,
):
    step = pl.program_id(0)

    @pl.when(step == 0)
    def _():
        whitened, _ = norm_stats(u_ref[...].astype(F32))
        normed_ref[...] = (whitened * gain_ref[...] + shift_ref[...]).astype(BF16)
        acc_ref[...] = jnp.zeros_like(acc_ref)

    normed = normed_ref[...]
    q_ref[...] = ((dot(normed, wq_ref[...]) + qb_ref[...]) * 0.125).astype(BF16)
    k_ref[...] = dot(normed, wk_ref[...]).astype(BF16)
    v_ref[...] = (dot(normed, wv_ref[...]) + vb_ref[...]).astype(BF16)
    masks = head_masks()
    for pair in range(QUAD // 2):
        lanes = slice(128 * pair, 128 * pair + 128)
        for e in range(2):
            base = skewed(table_ref[2 * pair + e])
            odd = pltpu.roll(base, TABW - PITCH, 1)
            for a in range(0, HMAX, 2):
                both = jnp.concatenate(
                    [base[:, PITCH * a : PITCH * a + COLK], odd[:, PITCH * a : PITCH * a + COLK]], axis=0
                )
                at = ROWK * e + WMAX * a
                rst_ref[at : at + 2 * WMAX, :] = both.astype(BF16)
        for n in range(images):
            rows = slice(RP * n, RP * n + RP)
            spread = dot(rst_ref[...], s_ref[n]).astype(BF16)
            qn, kn, vn = q_ref[rows, lanes], k_ref[rows, lanes], v_ref[rows, lanes]
            attended = None
            for e in range(2):
                bias = dot(pt_ref[n], spread[ROWK * e : ROWK * e + ROWK])
                scores = dot(qn * masks[e], kn, NT) + (bias + mask_ref[n])
                peak = jnp.max(scores, axis=1, keepdims=True)
                power = jnp.exp(scores - peak)
                weights = (power * (1.0 / jnp.sum(power, axis=1, keepdims=True))).astype(BF16)
                w_ref[n, 2 * pair + e] = weights
                part = dot(weights, vn * masks[e])
                attended = part if attended is None else attended + part
            att_ref[rows, lanes] = attended.astype(BF16)
    acc_ref[...] += dot(att_ref[...], wo_ref[...])

    @pl.when(step == pl.num_programs(0) - 1)
    def _():
        out = acc_ref[...] + ob_ref[...]
        branch_ref[...] = out.astype(BF16)
        branch = scale_ref[...] * out * live_ref[...]
        next_ref[...] = (u_ref[...].astype(F32) + branch).astype(BF16)
        newtotal_ref[...] = total_ref[...] + branch


def row_of(layer, width=D):
    return pl.BlockSpec((None, 1, width), lambda *_: (layer, 0, 0))


def attention_forward(layer, images, u, total, w, tables):
    m = u.shape[0]
    live, mask, s, pt = tables["live"], tables["mask"], tables["s"], tables["pt"]
    wide = QUAD * HEAD
    steps = HEADS // QUAD
    third = lambda which: pl.BlockSpec((None, D, wide), lambda g: (layer, 0, which * steps + g))
    block = pl.BlockSpec((m, wide), lambda g: (0, g))
    out_type = [
        jax.ShapeDtypeStruct((m, D), BF16),
        jax.ShapeDtypeStruct((m, D), F32),
        jax.ShapeDtypeStruct((m, D), BF16),
        jax.ShapeDtypeStruct((m, D), BF16),
        jax.ShapeDtypeStruct((m, D), BF16),
        jax.ShapeDtypeStruct((m, D), BF16),
        jax.ShapeDtypeStruct((m, D), BF16),
        jax.ShapeDtypeStruct((images, HEADS, RP, RP), BF16),
        jax.ShapeDtypeStruct((m, D), BF16),
    ]
    return pl.pallas_call(
        functools.partial(attention_forward_kernel, images),
        grid=(steps,),
        in_specs=[
            whole(m, D), whole(m, D), row_of(layer), row_of(layer), third(0), third(1), third(2),
            pl.BlockSpec((None, 1, wide), lambda g: (layer, 0, g)),
            pl.BlockSpec((None, 1, wide), lambda g: (layer, 0, g)),
            pl.BlockSpec((None, QUAD, 1, TABW), lambda g: (layer, g, 0, 0)),
            pl.BlockSpec((None, wide, D), lambda g: (layer, g, 0)),
            row_of(layer), row_of(layer), whole(m, 1), whole(images, 1, RP),
            whole(images, COLK, RP), whole(images, RP, ROWK),
        ],
        out_specs=[
            whole(m, D), whole(m, D), whole(m, D), block, block, block, block,
            pl.BlockSpec((images, QUAD, RP, RP), lambda g: (0, g, 0, 0)),
            whole(m, D),
        ],
        out_shape=out_type,
        scratch_shapes=[pltpu.VMEM((m, D), F32), pltpu.VMEM((2 * ROWK, COLK), BF16)],
        compiler_params=params(),
        cost_estimate=pl.CostEstimate(flops=12 * 10**9, bytes_accessed=15 * 10**6, transcendentals=10**6),
        name="attention_forward",
    )(
        u, total, w["attention_gain"], w["attention_shift"], w["input_projection"], w["input_projection"],
        w["input_projection"], w["query_bias"], w["value_bias"], tables["table"], w["output_projection"],
        w["output_bias"], w["attention_scale"], live, mask, s, pt,
    )


def feed_forward_kernel(
    u_ref, total_ref, gain_ref, shift_ref, wh_ref, hb_ref, wr_ref, rb_ref, scale_ref, live_ref,
    next_ref, newtotal_ref, normed_ref, active_ref, slope_ref, branch_ref, acc_ref,
):
    step = pl.program_id(0)

    @pl.when(step == 0)
    def _():
        whitened, _ = norm_stats(u_ref[...].astype(F32))
        normed_ref[...] = (whitened * gain_ref[...] + shift_ref[...]).astype(BF16)
        acc_ref[...] = jnp.zeros_like(acc_ref)

    hidden = dot(normed_ref[...], wh_ref[...]) + hb_ref[...]
    share = 0.5 * (1.0 + lax.erf(hidden * 0.7071067811865476))
    active_ref[...] = (hidden * share).astype(BF16)
    slope_ref[...] = (share + hidden * jnp.exp(-0.5 * hidden * hidden) * 0.3989422804014327).astype(BF16)
    acc_ref[...] += dot(active_ref[...], wr_ref[...])

    @pl.when(step == pl.num_programs(0) - 1)
    def _():
        out = acc_ref[...] + rb_ref[...]
        branch_ref[...] = out.astype(BF16)
        branch = scale_ref[...] * out * live_ref[...]
        next_ref[...] = (u_ref[...].astype(F32) + branch).astype(BF16)
        newtotal_ref[...] = total_ref[...] + branch


def feed_forward(layer, u, total, w, tables, steps):
    m = u.shape[0]
    wide = FF // steps
    block = pl.BlockSpec((m, wide), lambda g: (0, g))
    return pl.pallas_call(
        feed_forward_kernel,
        grid=(steps,),
        in_specs=[
            whole(m, D), whole(m, D), row_of(layer), row_of(layer),
            pl.BlockSpec((None, D, wide), lambda g: (layer, 0, g)),
            pl.BlockSpec((None, 1, wide), lambda g: (layer, 0, g)),
            pl.BlockSpec((None, wide, D), lambda g: (layer, g, 0)),
            row_of(layer), row_of(layer), whole(m, 1),
        ],
        out_specs=[whole(m, D), whole(m, D), whole(m, D), block, block, whole(m, D)],
        out_shape=[
            jax.ShapeDtypeStruct((m, D), BF16),
            jax.ShapeDtypeStruct((m, D), F32),
            jax.ShapeDtypeStruct((m, D), BF16),
            jax.ShapeDtypeStruct((m, FF), BF16),
            jax.ShapeDtypeStruct((m, FF), BF16),
            jax.ShapeDtypeStruct((m, D), BF16),
        ],
        scratch_shapes=[pltpu.VMEM((m, D), F32)],
        compiler_params=params(),
        cost_estimate=pl.CostEstimate(flops=8 * 10**9, bytes_accessed=20 * 10**6, transcendentals=10**6),
        name="feed_forward",
    )(
        u, total, w["forward_gain"], w["forward_shift"], w["hidden_weight"], w["hidden_bias"],
        w["return_weight"], w["return_bias"], w["forward_scale"], tables["live"],
    )


def feed_blocks(order_ref, bg_ref, scale_ref, live_ref, normed_ref, active_ref, slope_ref, wh_ref, wr_ref,
                dh_ref, dr_ref, hb_ref, ng_ref, out_ref, nt_ref, ot_ref):
    @pl.when(pl.program_id(0) == 0)
    def _():
        out = (bg_ref[...].astype(F32) * scale_ref[...] * live_ref[...]).astype(BF16)
        out_ref[...] = out
        ot_ref[...] = out.T
        nt_ref[...] = normed_ref[...].T

    dr_ref[...] = dot(ot_ref[...], active_ref[...]).astype(BF16)
    grad = dot(out_ref[...], wr_ref[...], NT) * slope_ref[...].astype(F32)
    grad = grad.astype(BF16)
    hb_ref[...] = column_sum(grad.astype(F32))
    dh_ref[...] = dot(nt_ref[...], grad).astype(BF16)
    ng_ref[...] += dot(grad, wh_ref[...], NT)


def feed_send_kernel(order_ref, bg_ref, scale_ref, live_ref, normed_ref, active_ref, slope_ref, wh_ref, wr_ref,
                     dh_ref, dr_ref, hb_ref, ng_ref, out_ref, nt_ref, ot_ref):
    @pl.when(pl.program_id(0) == 0)
    def _():
        ng_ref[...] = jnp.zeros_like(ng_ref)

    feed_blocks(order_ref, bg_ref, scale_ref, live_ref, normed_ref, active_ref, slope_ref, wh_ref, wr_ref,
                dh_ref, dr_ref, hb_ref, ng_ref, out_ref, nt_ref, ot_ref)


def feed_keep_kernel(order_ref, bg_ref, scale_ref, live_ref, normed_ref, active_ref, slope_ref, wh_ref, wr_ref,
                     part_ref, u_ref, gain_ref, branch_ref,
                     dh_ref, dr_ref, hb_ref, next_ref, small_ref, ng_ref, out_ref, nt_ref, ot_ref):
    @pl.when(pl.program_id(0) == 0)
    def _():
        ng_ref[...] = part_ref[...]

    feed_blocks(order_ref, bg_ref, scale_ref, live_ref, normed_ref, active_ref, slope_ref, wh_ref, wr_ref,
                dh_ref, dr_ref, hb_ref, ng_ref, out_ref, nt_ref, ot_ref)

    @pl.when(pl.program_id(0) == pl.num_programs(0) - 1)
    def _():
        whitened, inverse = norm_stats(u_ref[...].astype(F32))
        ng = ng_ref[...]
        bg = bg_ref[...].astype(F32)
        next_ref[...] = bg + norm_back(ng, whitened, inverse, gain_ref[...])
        small_ref[...] = jnp.zeros_like(small_ref)
        small_ref[0:1] = column_sum(ng * whitened)
        small_ref[1:2] = column_sum(ng)
        small_ref[2:3] = column_sum(out_ref[...].astype(F32))
        small_ref[3:4] = column_sum(bg * branch_ref[...].astype(F32) * live_ref[...])


def feed_backward(layer, order, sections, bg, saved, w, tables, keep=None):
    m = bg.shape[0]
    wide = FF // sections
    steps = sections // 2
    block = pl.BlockSpec((m, wide), lambda i, order: (0, order[i]))
    in_specs = [
        whole(m, D), row_of(layer), whole(m, 1), whole(m, D), block, block,
        pl.BlockSpec((None, D, wide), lambda i, order: (layer, 0, order[i])),
        pl.BlockSpec((None, wide, D), lambda i, order: (layer, order[i], 0)),
    ]
    operands = [bg, w["forward_scale"], tables["live"], saved["normed"], saved["active"], saved["slope"],
                w["hidden_weight"], w["return_weight"]]
    out_specs = [
        pl.BlockSpec((None, D, wide), lambda i, order: (i, 0, 0)),
        pl.BlockSpec((None, D, wide), lambda i, order: (i, 0, 0)),
        pl.BlockSpec((None, 1, wide), lambda i, order: (i, 0, 0)),
        whole(m, D),
    ]
    out_shape = [
        jax.ShapeDtypeStruct((steps, D, wide), BF16),
        jax.ShapeDtypeStruct((steps, D, wide), BF16),
        jax.ShapeDtypeStruct((steps, 1, wide), F32),
        jax.ShapeDtypeStruct((m, D), F32),
    ]
    scratch = [pltpu.VMEM((m, D), BF16), pltpu.VMEM((D, m), BF16), pltpu.VMEM((D, m), BF16)]
    kernel = feed_send_kernel
    if keep is not None:
        kernel = feed_keep_kernel
        in_specs += [whole(m, D), whole(m, D), row_of(layer), whole(m, D)]
        operands += [keep, saved["u"], w["forward_gain"], saved["branch"]]
        out_specs.append(whole(8, D))
        out_shape.append(jax.ShapeDtypeStruct((8, D), F32))
        scratch = [pltpu.VMEM((m, D), F32)] + scratch
    return pl.pallas_call(
        kernel,
        grid_spec=pltpu.PrefetchScalarGridSpec(
            num_scalar_prefetch=1, grid=(steps,), in_specs=in_specs, out_specs=out_specs, scratch_shapes=scratch
        ),
        out_shape=out_shape,
        compiler_params=params(),
        cost_estimate=pl.CostEstimate(flops=8 * 10**9, bytes_accessed=15 * 10**6, transcendentals=0),
        name="feed_send" if keep is None else "feed_keep",
    )(order, *operands)


def attention_backward_kernel(
    images, u_ref, bg_ref, gain_ref, scale_ref, live_ref, q_ref, k_ref, v_ref, w_ref, branch_ref,
    wq_ref, wk_ref, wv_ref, wo_ref, p_ref, st_ref,
    next_ref, out_ref, gq_ref, gk_ref, gv_ref, table_ref, bias_ref, small_ref,
    ng_ref, even_ref, odd_ref,
):
    step = pl.program_id(0)

    @pl.when(step == 0)
    def _():
        out_ref[...] = (bg_ref[...] * scale_ref[...] * live_ref[...]).astype(BF16)
        ng_ref[...] = jnp.zeros_like(ng_ref)

    att_grad = dot(out_ref[...], wo_ref[...], NT).astype(BF16)
    masks = head_masks()
    for pair in range(QUAD // 2):
        lanes = slice(128 * pair, 128 * pair + 128)
        even_ref[...] = jnp.zeros_like(even_ref)
        odd_ref[...] = jnp.zeros_like(odd_ref)
        for n in range(images):
            rows = slice(RP * n, RP * n + RP)
            qn, kn, vn = q_ref[rows, lanes], k_ref[rows, lanes], v_ref[rows, lanes]
            an = att_grad[rows, lanes]
            dq = dk = dv = None
            for e in range(2):
                weights = w_ref[n, 2 * pair + e]
                chosen = an * masks[e]
                weights_grad = dot(chosen, vn, NT)
                probs = weights.astype(F32)
                product = weights_grad * probs
                score_grad = (product - probs * jnp.sum(product, axis=1, keepdims=True)).astype(BF16)
                parts = (
                    dot(score_grad, kn * masks[e]),
                    dot(score_grad, qn * masks[e], TN),
                    dot(weights, chosen, TN),
                )
                dq, dk, dv = parts if dq is None else (dq + parts[0], dk + parts[1], dv + parts[2])
                moved = dot(p_ref[n], score_grad).astype(BF16)
                spread = dot(moved, st_ref[n])
                for a in range(0, HMAX, 2):
                    at = slice(PITCH * a, PITCH * a + COLK)
                    even_ref[e, :, at] += spread[WMAX * a : WMAX * a + WMAX]
                    odd_ref[e, :, at] += spread[WMAX * a + WMAX : WMAX * a + 2 * WMAX]
            gq_ref[rows, lanes] = (dq.astype(BF16).astype(F32) * 0.125).astype(BF16)
            gk_ref[rows, lanes] = dk.astype(BF16)
            gv_ref[rows, lanes] = dv.astype(BF16)
        for e in range(2):
            both = even_ref[e] + pltpu.roll(odd_ref[e], PITCH, 1)
            table_ref[2 * pair + e] = column_sum(pltpu.roll(both, 0, 1, stride=1, stride_axis=0))
    gq, gk, gv = gq_ref[...], gk_ref[...], gv_ref[...]
    bias_ref[0] = column_sum(gq.astype(F32))
    bias_ref[1] = column_sum(gv.astype(F32))
    ng_ref[...] += dot(gq, wq_ref[...], NT) + dot(gk, wk_ref[...], NT) + dot(gv, wv_ref[...], NT)

    @pl.when(step == pl.num_programs(0) - 1)
    def _():
        whitened, inverse = norm_stats(u_ref[...].astype(F32))
        ng = ng_ref[...]
        bg = bg_ref[...]
        next_ref[...] = bg + norm_back(ng, whitened, inverse, gain_ref[...])
        small_ref[...] = jnp.zeros_like(small_ref)
        small_ref[0:1] = column_sum(ng * whitened)
        small_ref[1:2] = column_sum(ng)
        small_ref[2:3] = column_sum(out_ref[...].astype(F32))
        small_ref[3:4] = column_sum(bg * branch_ref[...].astype(F32) * live_ref[...])


def attention_backward(layer, images, bg, saved, w, tables):
    m = bg.shape[0]
    wide = QUAD * HEAD
    steps = HEADS // QUAD
    block = pl.BlockSpec((m, wide), lambda g: (0, g))
    third = lambda which: pl.BlockSpec((None, D, wide), lambda g: (layer, 0, which * steps + g))
    return pl.pallas_call(
        functools.partial(attention_backward_kernel, images),
        grid=(steps,),
        in_specs=[
            whole(m, D), whole(m, D), row_of(layer), row_of(layer), whole(m, 1), block, block, block,
            pl.BlockSpec((images, QUAD, RP, RP), lambda g: (0, g, 0, 0)),
            whole(m, D), third(0), third(1), third(2),
            pl.BlockSpec((None, wide, D), lambda g: (layer, g, 0)),
            whole(images, ROWK, RP), whole(images, RP, COLK),
        ],
        out_specs=[
            whole(m, D), whole(m, D), block, block, block,
            pl.BlockSpec((QUAD, 1, TABW), lambda g: (g, 0, 0)),
            pl.BlockSpec((2, 1, wide), lambda g: (0, 0, g)),
            whole(8, D),
        ],
        out_shape=[
            jax.ShapeDtypeStruct((m, D), F32),
            jax.ShapeDtypeStruct((m, D), BF16),
            jax.ShapeDtypeStruct((m, D), BF16),
            jax.ShapeDtypeStruct((m, D), BF16),
            jax.ShapeDtypeStruct((m, D), BF16),
            jax.ShapeDtypeStruct((HEADS, 1, TABW), F32),
            jax.ShapeDtypeStruct((2, 1, D), F32),
            jax.ShapeDtypeStruct((8, D), F32),
        ],
        scratch_shapes=[
            pltpu.VMEM((m, D), F32), pltpu.VMEM((2, WMAX, TABW), F32), pltpu.VMEM((2, WMAX, TABW), F32),
        ],
        compiler_params=params(),
        cost_estimate=pl.CostEstimate(flops=16 * 10**9, bytes_accessed=15 * 10**6, transcendentals=0),
        name="attention_backward",
    )(
        saved["u"], bg, w["attention_gain"], w["attention_scale"], tables["live"], saved["q"], saved["k"], saved["v"],
        saved["w"], saved["branch"], w["input_projection"], w["input_projection"], w["input_projection"],
        w["output_projection"], tables["p"], tables["st"],
    )


def attention_weights_kernel(order_ref, normed_ref, att_ref, grads_ref, out_ref, nt_ref, at_ref):
    @pl.when(pl.program_id(0) == 0)
    def _():
        nt_ref[...] = normed_ref[...].T
        at_ref[...] = att_ref[...].T

    first = 3 * D // (4 * 128) * 128
    low = lax.broadcasted_iota(jnp.int32, (1, 128), 1) < HEAD
    left = dot(nt_ref[...], grads_ref[:, : first + 128])
    right = dot(at_ref[...], grads_ref[:, first:])
    out_ref[:, :first] = left[:, :first].astype(BF16)
    out_ref[:, first : first + 128] = jnp.where(low, left[:, first:], right[:, :128]).astype(BF16)
    out_ref[:, first + 128 :] = right[:, 128:].astype(BF16)


def attention_weights(order, sections, saved, grads):
    m = grads.shape[1]
    steps = sections // 2
    return pl.pallas_call(
        attention_weights_kernel,
        grid_spec=pltpu.PrefetchScalarGridSpec(
            num_scalar_prefetch=1,
            grid=(steps,),
            in_specs=[
                whole(m, D), whole(m, D), pl.BlockSpec((None, m, D), lambda i, order: (order[i], 0, 0)),
            ],
            out_specs=pl.BlockSpec((None, D, D), lambda i, order: (i, 0, 0)),
            scratch_shapes=[pltpu.VMEM((D, m), BF16), pltpu.VMEM((D, m), BF16)],
        ),
        out_shape=jax.ShapeDtypeStruct((steps, D, D), BF16),
        compiler_params=params(),
        cost_estimate=pl.CostEstimate(flops=2 * 10**9, bytes_accessed=5 * 10**6, transcendentals=0),
        name="attention_weights",
    )(order, saved["normed"], saved["attended"], grads)


def flip(value, axis, bit):
    count = lax.axis_size(axis)
    return lax.ppermute(value, axis, [(i, i ^ bit) for i in range(count)])


def bits_of(axis):
    return [1 << i for i in range(lax.axis_size(axis).bit_length() - 1)]


def own_bit(axis, bit):
    return (lax.axis_index(axis) // bit) % 2


def sum_up(terms):
    total = terms[0].astype(F32)
    for term in terms[1:]:
        total = total + term.astype(F32)
    return total


def halvings(keep, received, order):
    section_bits = [("section", bit) for bit in reversed(bits_of("section")[1:])]
    wide_bits = [("wide", bit) for bit in reversed(bits_of("wide"))]
    names = section_bits + wide_bits
    shape = (2,) * len(names) + (D // lax.axis_size("wide"),) + keep.shape[2:]
    terms = [keep.reshape(shape), received.reshape(shape)]
    for name in order:
        at = names.index(name)
        names = names[:at] + names[at + 1 :]
        mine = own_bit(*name)
        take = lambda term, which: lax.dynamic_index_in_dim(term, which, at, keepdims=False)
        going = sum_up([take(term, 1 - mine) for term in terms]).astype(BF16)
        terms = [take(term, mine) for term in terms] + [flip(going, *name)]
    return sum_up(terms)


def orders():
    section_bits = [("section", bit) for bit in bits_of("section")[1:]]
    wide_bits = [("wide", bit) for bit in bits_of("wide")]
    return section_bits + wide_bits, wide_bits[:1] + section_bits + wide_bits[1:]


def small_total(parts):
    value = parts
    for bit in reversed(bits_of("section")):
        value = value.reshape((2, -1) + value.shape[1:])
        mine = own_bit("section", bit)
        other = flip(lax.dynamic_index_in_dim(value, 1 - mine, 0, keepdims=False), "section", bit)
        value = lax.dynamic_index_in_dim(value, mine, 0, keepdims=False) + other
    for bit in bits_of("wide"):
        value = value + flip(value, "wide", bit)
    return value[0]


def redistribute(rows, sections):
    me = lax.axis_index("section")
    images = rows.shape[0]
    width = D // sections
    cut = lambda s: lax.dynamic_slice_in_dim(rows, s * width, width, 2)
    result = jnp.zeros((sections * images, ROWS, width), rows.dtype)
    for distance in range(sections):
        piece = cut(me ^ distance)
        if distance:
            piece = flip(piece, "section", distance)
        result = lax.dynamic_update_slice_in_dim(result, piece, (me ^ distance) * images, 0)
    return result


def on_device(
    tokens, cotangent, patch_grids, attention_gain, attention_shift, input_projection, query_bias, value_bias,
    relative_table, output_projection, output_bias, attention_scale, forward_gain, forward_shift, hidden_weight,
    hidden_bias, return_weight, return_bias, forward_scale,
):
    sections = lax.axis_size("section")
    me = lax.axis_index("section")
    images = tokens.shape[0] // sections
    m = images * RP
    row = lambda v: v.reshape(LAYERS, 1, -1)
    w = {
        "attention_gain": row(attention_gain), "attention_shift": row(attention_shift),
        "input_projection": input_projection, "query_bias": row(query_bias), "value_bias": row(value_bias),
        "output_projection": output_projection, "output_bias": row(output_bias),
        "attention_scale": row(attention_scale), "forward_gain": row(forward_gain),
        "forward_shift": row(forward_shift), "hidden_weight": hidden_weight, "hidden_bias": row(hidden_bias),
        "return_weight": return_weight, "return_bias": row(return_bias), "forward_scale": row(forward_scale),
    }

    def mine(v):
        part = lax.dynamic_slice_in_dim(v, me * images, images, 0)
        return jnp.pad(part, ((0, 0), (0, RP - ROWS), (0, 0))).reshape(m, D)

    u = mine(tokens)
    cot = mine(cotangent)
    grids = lax.dynamic_slice_in_dim(patch_grids, me * images, images, 0)

    place = lax.broadcasted_iota(jnp.int32, (images, RP), 1)
    height, width = grids[:, 0:1], grids[:, 1:2]
    a, b = place // width, place % width
    live = place < height * width
    row_forward = jnp.where(live, a * WMAX + (WMAX - 1) - b, -1)
    row_backward = jnp.where(live, a * WMAX + b, -1)
    column = jnp.where(live, (HMAX - 1 - a) * PITCH + (WMAX - 1) - b, -1)
    pick = lambda index, count: (index[:, :, None] == lax.broadcasted_iota(jnp.int32, (1, 1, count), 2)).astype(BF16)
    pick_t = lambda index, count: (index[:, None, :] == lax.broadcasted_iota(jnp.int32, (1, count, 1), 1)).astype(BF16)
    table = jnp.transpose(relative_table.reshape(LAYERS, 2 * HMAX - 1, QW, HEADS), (0, 3, 1, 2))
    table = jnp.pad(table, ((0, 0), (0, 0), (0, 1), (0, PITCH - QW))).reshape(LAYERS, HEADS, 1, TABW)
    table = jnp.roll(table, -(WMAX - 1), axis=3)
    tables = {
        "live": live.reshape(m, 1).astype(F32),
        "mask": jnp.where(live, 0.0, -1e9).astype(F32).reshape(images, 1, RP),
        "s": pick_t(column, COLK),
        "st": pick(column, COLK),
        "pt": pick(row_forward, ROWK),
        "p": pick_t(row_backward, ROWK),
        "table": table,
    }

    total = u.astype(F32)
    kept_attention, kept_feed = [], []
    for layer in range(LAYERS):
        later, total, normed, q, k, v, attended, weights, branch = attention_forward(layer, images, u, total, w, tables)
        kept_attention.append(dict(u=u, normed=normed, q=q, k=k, v=v, attended=attended, w=weights, branch=branch))
        u = later
        later, total, normed, active, slope, branch = feed_forward(layer, u, total, w, tables, sections)
        kept_feed.append(dict(u=u, normed=normed, active=active, slope=slope, branch=branch))
        u = later
    layer_output = redistribute(total.reshape(images, RP, D)[:, :ROWS].astype(BF16), sections)

    core = me % 2
    sent = jnp.arange(sections // 2, dtype=jnp.int32) * 2 + (1 - core)
    kept = jnp.arange(sections // 2, dtype=jnp.int32) * 2 + core
    first, second = orders()
    bg = cot.astype(F32)
    hidden_grads, return_grads, projection_grads, out_grads, smalls = ([None] * LAYERS for _ in range(5))
    for layer in reversed(range(LAYERS)):
        saved = kept_feed[layer]
        dh_send, dr_send, hb_send, part = feed_backward(layer, sent, sections, bg, saved, w, tables)
        dh_got, dr_got = flip(dh_send, "section", 1), flip(dr_send, "section", 1)
        dh_keep, dr_keep, hb_keep, bg, feed_small = feed_backward(
            layer, kept, sections, bg, saved, w, tables, keep=part
        )
        hidden_grads[layer] = halvings(dh_keep, dh_got, first)
        return_grads[layer] = halvings(dr_keep, dr_got, second)
        hidden_shift = jnp.zeros((sections // 2, 2, FF // sections), F32)
        hidden_shift = lax.dynamic_update_slice_in_dim(hidden_shift, hb_send, 1 - core, 1)
        hidden_shift = lax.dynamic_update_slice_in_dim(hidden_shift, hb_keep, core, 1)

        saved = kept_attention[layer]
        bg, out_rows, gq, gk, gv, table_grad, biases, attention_small = attention_backward(
            layer, images, bg, saved, w, tables
        )
        projected = jnp.concatenate([gq, gk, gv], axis=1)
        part = 3 * D // sections
        grads = jnp.stack([
            jnp.concatenate(
                [projected[:, part * s : part * s + part], out_rows[:, D // sections * s : D // sections * (s + 1)]],
                axis=1,
            )
            for s in range(sections)
        ])
        da_send = attention_weights(sent, sections, saved, grads)
        da_got = flip(da_send, "section", 1)
        da_keep = attention_weights(kept, sections, saved, grads)
        half = D // 2
        da = jnp.concatenate([
            halvings(da_keep[:, :, :half], da_got[:, :, :half], first),
            halvings(da_keep[:, :, half:], da_got[:, :, half:], second),
        ], axis=1)
        projection_grads[layer], out_grads[layer] = da[:, :part], da[:, part:]
        vectors = jnp.concatenate([attention_small[:4], feed_small[:4], biases[:, 0]], axis=0)
        vectors = jnp.transpose(vectors.reshape(10, sections, D // sections), (1, 0, 2)).reshape(sections, -1)
        packed = jnp.concatenate(
            [vectors, hidden_shift.reshape(sections, -1), table_grad.reshape(sections, -1)], axis=1
        )
        smalls[layer] = small_total(packed)
    input_grad = redistribute(bg.reshape(images, RP, D)[:, :ROWS].astype(BF16), sections)

    small = jnp.stack(smalls)
    each = D // sections
    vector = lambda i: small[:, i * each : (i + 1) * each]
    hidden_shift = small[:, 10 * each : 10 * each + FF // sections]
    table_grad = small[:, 10 * each + FF // sections :].reshape(LAYERS, HEADS // sections, 2 * HMAX, PITCH)
    table_grad = table_grad[:, :, : 2 * HMAX - 1, :QW].reshape(LAYERS, HEADS // sections, REL)
    return (
        layer_output, input_grad,
        vector(0), vector(1), jnp.stack(projection_grads), vector(8), vector(9),
        jnp.transpose(table_grad, (0, 2, 1)), jnp.stack(out_grads), vector(2), vector(3),
        vector(4), vector(5), jnp.stack(hidden_grads), hidden_shift,
        jnp.transpose(jnp.stack(return_grads), (0, 2, 1)), vector(6), vector(7),
    )


def solution(mesh):
    three, two = P("wide", None, "section"), P(None, "section")
    weight = P(None, "wide", "section")
    return jax.shard_map(
        on_device,
        mesh=mesh,
        in_specs=(P("wide", None, None), P("wide", None, None), P("wide", None)) + (P(),) * 16,
        out_specs=(
            three, three, two, two, weight, two, two, P(None, None, "section"), weight, two, two, two, two,
            weight, two, P(None, "section", "wide"), two, two,
        ),
        check_vma=False,
    )
```

```python
import functools
from typing import NamedTuple

import jax
import jax.numpy as jnp
from jax import lax
from jax.experimental import pallas as pl
from jax.experimental.pallas import tpu as pltpu
from jax.sharding import PartitionSpec as P

SECTION = "section"
WIDE = "wide"
D = 768
HEADS = 12
HEAD = 64
FF = 3072
IN_ATT, IN_FEED, ATTENDED, OUT_FEED, ACTIVE = range(5)
ROWS = 200
HMAX = 14
WMAX = 24
REL = 1269
LAYERS = 2
QW = 2 * WMAX - 1
RP = 208
CP = 256
SPAN = 512
TABLE = 1280
SMALL = 28
QUAD = 4
F32 = jnp.float32
BF16 = jnp.bfloat16
NN = (((1,), (0,)), ((), ()))
NT = (((1,), (1,)), ((), ()))
TN = (((0,), (0,)), ((), ()))
VMEM = 48 * 1024 * 1024


def dot(left, right, dims=NN):
    return lax.dot_general(left, right, dims, preferred_element_type=F32)


def whole(*shape):
    return pl.BlockSpec(shape, lambda *_: (0,) * len(shape))


class Kept(NamedTuple):
    active: jax.Array
    q: jax.Array
    k: jax.Array
    v: jax.Array
    w: jax.Array
    branch_att: jax.Array
    slope: jax.Array
    branch_feed: jax.Array


class Weights(NamedTuple):
    attention_gain: jax.Array
    attention_shift: jax.Array
    input_projection: jax.Array
    query_bias: jax.Array
    value_bias: jax.Array
    output_projection: jax.Array
    output_bias: jax.Array
    attention_scale: jax.Array
    forward_gain: jax.Array
    forward_shift: jax.Array
    hidden_weight: jax.Array
    hidden_bias: jax.Array
    return_weight: jax.Array
    return_bias: jax.Array
    forward_scale: jax.Array


class Tables(NamedTuple):
    live: jax.Array
    mask: jax.Array
    upper: jax.Array
    rows: jax.Array


def run(kernel, *, grid, in_specs, out_specs, out_shape, operands, scratch=(), prefetch=(), after=(), held=(), name):
    first = len(prefetch) + len(in_specs)
    count = len(after) + len(held)
    outs = len(out_shape)

    def body(*refs):
        kept = refs[:first] + refs[first + count : first + count + outs]
        kernel(*kept, *refs[first + count + outs + len(held) :])

    anywhere = pl.BlockSpec(memory_space=pl.ANY)
    return pl.pallas_call(
        body,
        grid_spec=pltpu.PrefetchScalarGridSpec(
            num_scalar_prefetch=len(prefetch),
            grid=grid,
            in_specs=list(in_specs) + [anywhere] * count,
            out_specs=list(out_specs) + [anywhere] * len(held),
            scratch_shapes=list(scratch),
        ),
        out_shape=list(out_shape) + [jax.ShapeDtypeStruct(v.shape, v.dtype) for v in held],
        input_output_aliases={first + len(after) + i: outs + i for i in range(len(held))},
        compiler_params=pltpu.CompilerParams(vmem_limit_bytes=VMEM),
        cost_estimate=pl.CostEstimate(flops=10**6, bytes_accessed=10**5, transcendentals=0),
        name=name,
    )(*prefetch, *operands, *after, *held)


def hold(held, after):
    def kernel(out_ref):
        out_ref[...] = jnp.zeros_like(out_ref)

    tiny = [jax.ShapeDtypeStruct((8, 128), F32)]
    _, *held = run(
        kernel, grid=(1,), in_specs=[], out_specs=[whole(8, 128)], out_shape=tiny, operands=[], after=after, held=held,
        name="hold",
    )
    return held


def norm_stats(u):
    mean = jnp.mean(u, axis=1, keepdims=True)
    centered = u - mean
    inverse = lax.rsqrt(jnp.mean(centered * centered, axis=1, keepdims=True) + 1e-6)
    return centered * inverse, inverse


def norm_back(upstream, whitened, inverse, gain):
    scaled = upstream * gain
    first = jnp.mean(scaled, axis=1, keepdims=True)
    second = jnp.mean(scaled * whitened, axis=1, keepdims=True)
    return (scaled - first - whitened * second) * inverse


def column_sum(v):
    return jnp.sum(v, axis=0, keepdims=True)


def head_masks():
    lane = lax.broadcasted_iota(jnp.int32, (1, 2 * HEAD), 1)
    low = (lane < HEAD).astype(F32)
    return low.astype(BF16), (1.0 - low).astype(BF16)


def bias_rows_kernel(table_ref, index_ref, out_ref):
    table = table_ref[...]
    high = table.astype(BF16)
    rest = table - high.astype(F32)
    middle = rest.astype(BF16)
    low = (rest - middle.astype(F32)).astype(BF16)
    chosen = (lax.broadcasted_iota(jnp.int32, (table.shape[1], SPAN), 0) == index_ref[...]).astype(F32).astype(BF16)
    out_ref[...] = dot(high, chosen) + dot(middle, chosen) + dot(low, chosen)


def bias_rows(table, index):
    places = index.shape[0]
    return run(
        bias_rows_kernel,
        grid=(places,),
        in_specs=[whole(*table.shape), pl.BlockSpec((None, 1, SPAN), lambda i: (i, 0, 0))],
        out_specs=[pl.BlockSpec((None, table.shape[0], SPAN), lambda i: (i, 0, 0))],
        out_shape=[jax.ShapeDtypeStruct((places, table.shape[0], SPAN), F32)],
        operands=[table, index],
        name="bias_rows",
    )[0]


def diagonal_base(row):
    return pltpu.roll(jnp.broadcast_to(row, (8, SPAN)), 0, 1, stride=1, stride_axis=0)


def row_blocks():
    return [(16 * c, [(128 * t + 16 * c, t) for t in range(2) if 128 * t + 16 * c < RP]) for c in range(8)]


def turned_pair(base, turn):
    return [pltpu.roll(base, turn + 8 * i, 1) if turn + 8 * i else base for i in range(2)]


def diagonal_block(pair, tiles):
    pick = lambda v, k: v[:, 128 * ((k - tiles) % 4) : 128 * ((k - tiles) % 4) + 128]
    return jnp.concatenate([jnp.concatenate([pick(v, k) for k in range(CP // 128)], axis=1) for v in pair], axis=0)


def straighten(sums):
    row = lax.broadcasted_iota(jnp.int32, (8, 1), 0)
    for bit in (1, 2, 4):
        sums = jnp.where((row // bit) % 2 == 1, pltpu.roll(sums, SPAN - bit, 1), sums)
    return column_sum(sums)


def forward_kernel(
    images, steps, sections,
    me_ref, order_ref, tokens_ref, cot_ref, gain_ref, shift_ref, wq_ref, wk_ref, wv_ref, qb_ref, vb_ref, rows_ref,
    wo_ref, ob_ref, scale_ref, fgain_ref, fshift_ref, wh_ref, hb_ref, wr_ref, rb_ref, fscale_ref, live_ref, mask_ref,
    upper_ref, *refs,
):
    cross_ref, active_ref, q_ref, k_ref, v_ref, w_ref, branch_att_ref, slope_ref, branch_feed_ref, *refs = refs
    piece_refs, (now_ref, total_ref, acc_ref, scores_ref, normed_ref, att_ref) = refs[:sections], refs[sections:]
    t = pl.program_id(0)
    per = steps + sections
    phase = lax.rem(t, per)
    m = images * RP
    layer = t // per
    own = pl.ds(layer, 1)
    lanes_of = lambda at, width: pl.ds(pl.multiple_of(at * width, width), width)

    @pl.when(t == 0)
    def _():
        now_ref[...] = jnp.zeros_like(now_ref)
        for n in range(images):
            now_ref[RP * n : RP * n + ROWS] = tokens_ref[n]
        total_ref[...] = now_ref[...].astype(F32)

    def norm(gain, shift):
        whitened, _ = norm_stats(now_ref[...].astype(F32))
        acc_ref[...] = jnp.zeros_like(acc_ref)
        normed_ref[...] = (whitened * gain + shift).astype(BF16)

    def add_branch(out, scale):
        branch = scale * out * live_ref[...]
        now_ref[...] = (now_ref[...].astype(F32) + branch).astype(BF16)
        total_ref[...] += branch

    @pl.when(phase == 0)
    def _():
        cross_ref[IN_ATT] = now_ref[...]
        norm(gain_ref[own], shift_ref[own])
        cross_ref[OUT_FEED] = jnp.zeros((m, D), BF16)
        for n in range(images):
            rows = slice(RP * n, RP * n + ROWS)
            out = cot_ref[n].astype(F32) * fscale_ref[LAYERS - 1 : LAYERS] * live_ref[rows]
            cross_ref[OUT_FEED, rows] = out.astype(BF16)

    @pl.when(phase < steps)
    def _():
        normed = normed_ref[...]
        here = lanes_of(phase, QUAD * HEAD)
        q_ref[...] = ((dot(normed, wq_ref[...]) + qb_ref[own, here]) * 0.125).astype(BF16)
        k_ref[0:m] = dot(normed, wk_ref[...]).astype(BF16)
        v_ref[0:m] = (dot(normed, wv_ref[...]) + vb_ref[own, here]).astype(BF16)
        k_ref[m:] = jnp.zeros_like(k_ref[m:])
        v_ref[m:] = jnp.zeros_like(v_ref[m:])
        masks = head_masks()
        head = layer * HEADS + phase * QUAD
        cells = [(n, h) for n in range(images) for h in range(QUAD)]
        for at, (n, h) in enumerate(cells):
            lanes = slice(128 * (h // 2), 128 * (h // 2) + 128)
            qn = q_ref[RP * n : RP * n + RP, lanes] * masks[h % 2]
            scores_ref[at] = dot(qn, k_ref[RP * n : RP * n + CP, lanes], NT)
        for n in range(images):
            bases = [[diagonal_base(rows_ref[2 * n + i, pl.ds(head + h, 1), :]) for i in range(2)] for h in range(QUAD)]
            for turn, blocks in row_blocks():
                pairs = [[turned_pair(base, turn) for base in each] for each in bases]
                for row, tiles in blocks:
                    above = (upper_ref[n, row : row + 16] > 0.0)[None]
                    first, second = (
                        jnp.stack([diagonal_block(each[i], tiles) for each in pairs]) for i in range(2)
                    )
                    bias = jnp.where(above, first, second) + mask_ref[n]
                    scores_ref[QUAD * n : QUAD * n + QUAD, row : row + 16] += bias
        for n in range(images):
            for row in range(0, RP, 16):
                scores = scores_ref[QUAD * n : QUAD * n + QUAD, row : row + 16]
                power = jnp.exp(scores - jnp.max(scores, axis=2, keepdims=True))
                weights = power * (1.0 / jnp.sum(power, axis=2, keepdims=True))
                w_ref[n, :, row : row + 16] = weights.astype(BF16)
        for n in range(images):
            for pair in range(QUAD // 2):
                lanes = slice(128 * pair, 128 * pair + 128)
                vn = v_ref[RP * n : RP * n + CP, lanes]
                attended = dot(w_ref[n, 2 * pair], vn * masks[0]) + dot(w_ref[n, 2 * pair + 1], vn * masks[1])
                att_ref[RP * n : RP * n + RP, lanes] = attended.astype(BF16)
        acc_ref[...] += dot(att_ref[...], wo_ref[...])
        cross_ref[ATTENDED, :, here] = att_ref[...]

    @pl.when(phase == steps - 1)
    def _():
        out = acc_ref[...] + ob_ref[own]
        branch_att_ref[...] = out.astype(BF16)
        add_branch(out, scale_ref[own])
        cross_ref[IN_FEED] = now_ref[...]

    @pl.when(phase == steps)
    def _():
        norm(fgain_ref[own], fshift_ref[own])

    @pl.when(phase >= steps)
    def _():
        at = phase - steps
        hidden = dot(normed_ref[...], wh_ref[...]) + hb_ref[own, lanes_of(order_ref[at], FF // sections)]
        share = 0.5 * (1.0 + lax.erf(hidden * 0.7071067811865476))
        active = (hidden * share).astype(BF16)
        slope_ref[...] = (share + hidden * jnp.exp(-0.5 * hidden * hidden) * 0.3989422804014327).astype(BF16)
        acc_ref[...] += dot(active, wr_ref[...])

        @pl.when(at < sections // 2)
        def _():
            cross_ref[ACTIVE + at] = active

        @pl.when(at >= sections // 2)
        def _():
            active_ref[...] = active

    @pl.when(phase == per - 1)
    def _():
        out = acc_ref[...] + rb_ref[own]
        branch_feed_ref[...] = out.astype(BF16)
        add_branch(out, fscale_ref[own])

    @pl.when(t == pl.num_programs(0) - 1)
    def _():
        send_pieces(me_ref[0], images, total_ref, piece_refs)


def send_pieces(me, images, rows_ref, piece_refs):
    sections = len(piece_refs)
    width = D // sections
    turned = [rows_ref[RP * n : RP * n + RP].T for n in range(images)]
    for own in range(sections):

        @pl.when(me == own)
        def _():
            for distance, piece in enumerate(piece_refs):
                at = width * (own ^ distance)
                for n in range(images):
                    piece[n] = turned[n][at : at + width, :ROWS].astype(BF16)


def pieces_shape(images, sections):
    return [jax.ShapeDtypeStruct((images, D // sections, ROWS), BF16)] * sections


def forward(images, sections, me, order, tokens, cotangent, w, tables):
    m = images * RP
    mc = (images - 1) * RP + CP
    wide = QUAD * HEAD
    steps = HEADS // QUAD
    per = steps + sections
    deep = FF // sections
    half = sections // 2
    layer = lambda t: t // per
    phase = lambda t: lax.rem(t, per)

    def att_at(t):
        inside = phase(t) < steps
        more = layer(t) + 1 < LAYERS
        l = jnp.where(inside, layer(t), jnp.minimum(layer(t) + 1, LAYERS - 1))
        return l, jnp.where(inside, phase(t), jnp.where(more, 0, steps - 1))

    def feed_at(t):
        return layer(t), jnp.maximum(phase(t) - steps, 0)

    def third(which):
        def index(t, *_):
            l, g = att_at(t)
            return l, 0, which * steps + g

        return pl.BlockSpec((None, D, wide), index)

    def att_in(block, place):
        return pl.BlockSpec(block, lambda t, *_: place(*att_at(t)))

    def feed_in(block, place):
        return pl.BlockSpec(block, lambda t, me, order: place(layer(t), order[feed_at(t)[1]]))

    def att_out(block, place):
        return pl.BlockSpec(block, lambda t, *_: place(layer(t), jnp.minimum(phase(t), steps - 1)))

    per_layer = lambda *block: pl.BlockSpec((None,) + block, lambda t, *_: (layer(t),) + (0,) * len(block))
    row = whole(LAYERS, D)
    mine = pl.BlockSpec((images, ROWS, D), lambda t, me, order: (me[0], 0, 0))
    shape = lambda *s, dtype=BF16: jax.ShapeDtypeStruct(s, dtype)
    results = run(
        functools.partial(forward_kernel, images, steps, sections),
        grid=(LAYERS * per,),
        prefetch=[me, order],
        in_specs=[
            mine, mine, row, row, third(0), third(1), third(2), row, row,
            whole(2 * images, LAYERS * HEADS, SPAN),
            att_in((None, wide, D), lambda l, g: (l, g, 0)),
            row, row, row, row,
            feed_in((None, D, deep), lambda l, f: (l, 0, f)),
            whole(LAYERS, FF),
            feed_in((None, deep, D), lambda l, f: (l, f, 0)),
            row, row, whole(m, 1), whole(images, 1, CP), whole(images, RP, CP),
        ],
        out_specs=[
            per_layer(ACTIVE + half, m, D),
            pl.BlockSpec((None, None, m, deep), lambda t, *_: (layer(t), jnp.maximum(feed_at(t)[1] - half, 0), 0, 0)),
            att_out((None, m, wide), lambda l, g: (l, 0, g)),
            att_out((None, mc, wide), lambda l, g: (l, 0, g)),
            att_out((None, mc, wide), lambda l, g: (l, 0, g)),
            att_out((None, images, QUAD, RP, CP), lambda l, g: (l, 0, g, 0, 0)),
            per_layer(m, D),
            pl.BlockSpec((None, None, m, deep), lambda t, *_: feed_at(t) + (0, 0)),
            per_layer(m, D),
        ]
        + [whole(images, D // sections, ROWS)] * sections,
        out_shape=[
            shape(LAYERS, ACTIVE + half, m, D), shape(LAYERS, half, m, deep),
            shape(LAYERS, m, D), shape(LAYERS, mc, D), shape(LAYERS, mc, D), shape(LAYERS, images, HEADS, RP, CP),
            shape(LAYERS, m, D), shape(LAYERS, sections, m, deep), shape(LAYERS, m, D),
        ]
        + pieces_shape(images, sections),
        scratch=[
            pltpu.VMEM((m, D), BF16), pltpu.VMEM((m, D), F32), pltpu.VMEM((m, D), F32),
            pltpu.VMEM((images * QUAD, RP, CP), F32), pltpu.VMEM((m, D), BF16), pltpu.VMEM((m, wide), BF16),
        ],
        name="forward",
        operands=[
            tokens, cotangent, w.attention_gain, w.attention_shift, w.input_projection, w.input_projection,
            w.input_projection, w.query_bias, w.value_bias, tables.rows, w.output_projection,
            w.output_bias, w.attention_scale, w.forward_gain, w.forward_shift, w.hidden_weight,
            w.hidden_bias, w.return_weight, w.return_bias, w.forward_scale, tables.live,
            tables.mask, tables.upper,
        ],
    )
    return results[0], Kept(*results[1:-sections]), results[-sections:]


def layer_block(layer, *block):
    return pl.BlockSpec((None,) + block, lambda *_: (layer,) + (0,) * len(block))


def feed_steps(step, steps, gain, bg_rows, out_ref, u_ref, live_ref, branch_ref, slope_ref, wh_ref, wr_ref,
               next_ref, small_ref, hb_ref, send_ref, keep_ref, ng_ref):
    @pl.when(step == 0)
    def _():
        ng_ref[...] = jnp.zeros_like(ng_ref)

    grad = dot(out_ref[...], wr_ref[...], NT) * slope_ref[...].astype(F32)
    grad = grad.astype(BF16)
    hb_ref[...] = column_sum(grad.astype(F32))
    ng_ref[...] += dot(grad, wh_ref[...], NT)

    @pl.when(step < steps // 2)
    def _():
        send_ref[jnp.minimum(step, steps // 2 - 1)] = grad

    @pl.when(step >= steps // 2)
    def _():
        keep_ref[...] = grad

    @pl.when(step == steps - 1)
    def _():
        bg_rows()
        bg = next_ref[...]
        whitened, inverse = norm_stats(u_ref[...].astype(F32))
        ng = ng_ref[...]
        small_ref[...] = jnp.zeros_like(small_ref)
        small_ref[0:1] = column_sum(ng * whitened)
        small_ref[1:2] = column_sum(ng)
        small_ref[2:3] = column_sum(out_ref[...].astype(F32))
        small_ref[3:4] = column_sum(bg * branch_ref[...].astype(F32) * live_ref[...])
        next_ref[...] = bg + norm_back(ng, whitened, inverse, gain)


def first_chain_kernel(images, me_ref, order_ref, cot_ref, out_ref, u_ref, gain_ref, live_ref, branch_ref, slope_ref,
                       wh_ref, wr_ref, next_ref, small_ref, hb_ref, keep_ref, send_ref, ng_ref):
    def bg_rows():
        next_ref[...] = jnp.zeros_like(next_ref)
        for n in range(images):
            next_ref[RP * n : RP * n + ROWS] = cot_ref[n].astype(F32)

    feed_steps(
        pl.program_id(0), pl.num_programs(0), gain_ref[LAYERS - 1 : LAYERS], bg_rows, out_ref, u_ref, live_ref,
        branch_ref, slope_ref, wh_ref, wr_ref, next_ref, small_ref, hb_ref, send_ref, keep_ref, ng_ref,
    )


def slot(layer, index, m):
    return pl.BlockSpec((None, None, m, D), lambda *_: (layer, index, 0, 0))


def first_chain(images, sections, me, order, cotangent, cross, kept, w, tables):
    layer = LAYERS - 1
    m = images * RP
    wide = FF // sections
    sends = sections // 2
    shape = jax.ShapeDtypeStruct
    return run(
        functools.partial(first_chain_kernel, images),
        grid=(sections,),
        in_specs=[
            pl.BlockSpec((images, ROWS, D), lambda i, me, order: (me[0], 0, 0)),
            slot(layer, OUT_FEED, m), slot(layer, IN_FEED, m), whole(LAYERS, D), whole(m, 1), layer_block(layer, m, D),
            pl.BlockSpec((None, None, m, wide), lambda i, me, order: (layer, i, 0, 0)),
            pl.BlockSpec((None, D, wide), lambda i, me, order: (layer, 0, order[i])),
            pl.BlockSpec((None, wide, D), lambda i, me, order: (layer, order[i], 0)),
        ],
        out_specs=[
            whole(m, D), whole(8, D),
            pl.BlockSpec((None, 1, wide), lambda i, *_: (i, 0, 0)),
            pl.BlockSpec((None, m, wide), lambda i, *_: (jnp.maximum(i - sends, 0), 0, 0)),
            whole(sends, m, wide),
        ],
        out_shape=[
            shape((m, D), F32), shape((8, D), F32), shape((sections, 1, wide), F32), shape((sends, m, wide), BF16),
            shape((sends, m, wide), BF16),
        ],
        scratch=[pltpu.VMEM((m, D), F32)],
        prefetch=[me, order],
        operands=[
            cotangent, cross, cross, w.forward_gain, tables.live, kept.branch_feed, kept.slope, w.hidden_weight,
            w.return_weight,
        ],
        name="first_chain",
    )


def by_first_bit(total, own, send_ref, keep_ref):
    pairs, rows, width = keep_ref.shape
    blocks = total.astype(BF16).reshape(pairs, 2, rows, width)
    even, odd = blocks[:, 0], blocks[:, 1]

    @pl.when(own == 0)
    def _():
        keep_ref[...] = even
        send_ref[...] = odd

    @pl.when(own == 1)
    def _():
        keep_ref[...] = odd
        send_ref[...] = even


def store_halves(totals, own, a_send_ref, a_keep_ref, b_send_ref, b_keep_ref):
    last = pl.program_id(0) == pl.num_programs(0) - 1
    for j, total in enumerate(totals):
        half = total.shape[1] // 2
        left = total[:, :half].astype(BF16)

        @pl.when(last)
        def _():
            a_keep_ref[j] = left

        @pl.when(jnp.logical_not(last))
        def _():
            a_send_ref[j] = left

        by_first_bit(total[:, half:], own, b_send_ref.at[j], b_keep_ref.at[j])


def halves_out(count, sends, rows):
    half = D // 2
    pairs = D // (2 * rows)
    piece = pl.BlockSpec((count, None, pairs, rows, half), lambda i, *_: (0, i, 0, 0, 0))
    specs = [whole(count, D, half), whole(count, D, half), piece, piece]
    shapes = [jax.ShapeDtypeStruct((count, D, half), BF16)] * 2
    return specs, shapes + [jax.ShapeDtypeStruct((count, sends, pairs, rows, half), BF16)] * 2


def turned_norm(u_ref, gain, shift):
    whitened, _ = norm_stats(u_ref[...].astype(F32))
    return (whitened * gain + shift).astype(BF16).T


def feed_keep_kernel(layer, own_ref, out_ref, out_got_ref, u_ref, u_got_ref, gain_ref, shift_ref,
                     active_ref, active_got_ref, hg_ref, *refs):
    hg_got_ref, out_refs, (ot_ref, nt_ref) = refs[0], refs[1:5], refs[5:]

    @pl.when(pl.program_id(0) == 0)
    def _():
        gain, shift = gain_ref[layer : layer + 1], shift_ref[layer : layer + 1]
        for i, (out, u) in enumerate(((out_ref, u_ref), (out_got_ref, u_got_ref))):
            ot_ref[i] = out[...].T
            nt_ref[i] = turned_norm(u, gain, shift)

    returned = dot(ot_ref[0], active_ref[...]) + dot(ot_ref[1], active_got_ref[...])
    hidden = dot(nt_ref[0], hg_ref[...]) + dot(nt_ref[1], hg_got_ref[...])
    store_halves([returned, hidden], own_ref[0], *out_refs)


def feed_keep(layer, own, rows, out, out_got, out_specs, cross, cross_got, active, hg, hg_got, w, after):
    sends, m, wide = hg.shape
    halves, out_shape = halves_out(2, sends, rows)
    block = pl.BlockSpec((None, m, wide), lambda i, own: (i, 0, 0))
    return run(
        functools.partial(feed_keep_kernel, layer),
        grid=(sends,),
        in_specs=[
            *out_specs, slot(layer, IN_FEED, m), slot(layer, IN_FEED, m), whole(LAYERS, D), whole(LAYERS, D),
            pl.BlockSpec((None, None, m, wide), lambda i, own: (layer, i, 0, 0)),
            pl.BlockSpec((None, None, m, wide), lambda i, own: (layer, ACTIVE + i, 0, 0)), block, block,
        ],
        out_specs=halves,
        out_shape=out_shape,
        scratch=[pltpu.VMEM((2, D, m), BF16), pltpu.VMEM((2, D, m), BF16)],
        prefetch=[own],
        operands=[out, out_got, cross, cross_got, w.forward_gain, w.forward_shift, active, cross_got, hg, hg_got],
        after=after,
        name="feed_keep",
    )


def attention_steps(
    step, images, sections, me, gain, scale, finish, u_ref, bg_ref, live_ref, q_ref, k_ref, v_ref, w_ref, branch_ref,
    wq_ref, wk_ref, wv_ref, wo_ref, upper_ref, next_ref, send_ref, keep_ref, rows_ref, bias_ref, small_ref,
    ng_ref, out_ref, wg_ref, sg_ref, parts_ref,
):
    steps = HEADS // QUAD
    sends = sections // 2

    @pl.when(step == 0)
    def _():
        out_ref[...] = (bg_ref[...] * scale * live_ref[...]).astype(BF16)
        ng_ref[...] = jnp.zeros_like(ng_ref)

    att_grad = dot(out_ref[...], wo_ref[...], NT).astype(BF16)
    masks = head_masks()
    lanes_of = lambda pair: slice(128 * pair, 128 * pair + 128)
    for n in range(images):
        for h in range(QUAD):
            lanes = lanes_of(h // 2)
            chosen = att_grad[RP * n : RP * n + RP, lanes] * masks[h % 2]
            wg_ref[QUAD * n + h] = dot(chosen, v_ref[RP * n : RP * n + CP, lanes], NT)
    for n in range(images):
        for row in range(0, RP, 16):
            probs = w_ref[n, :, row : row + 16].astype(F32)
            product = wg_ref[QUAD * n : QUAD * n + QUAD, row : row + 16] * probs
            grad = product - probs * jnp.sum(product, axis=2, keepdims=True)
            sg_ref[QUAD * n : QUAD * n + QUAD, row : row + 16] = grad.astype(BF16)
    grads = [[], [], []]
    for n in range(images):
        here = [[], [], []]
        for pair in range(QUAD // 2):
            lanes = lanes_of(pair)
            rows = slice(RP * n, RP * n + RP)
            kn, qn, an = k_ref[RP * n : RP * n + CP, lanes], q_ref[rows, lanes], att_grad[rows, lanes]
            one, two = QUAD * n + 2 * pair, QUAD * n + 2 * pair + 1
            dq = dot(sg_ref[one], kn * masks[0]) + dot(sg_ref[two], kn * masks[1])
            dk = dot(sg_ref[one], qn * masks[0], TN) + dot(sg_ref[two], qn * masks[1], TN)
            dv = dot(w_ref[n, 2 * pair], an * masks[0], TN) + dot(w_ref[n, 2 * pair + 1], an * masks[1], TN)
            here[0].append((dq.astype(BF16).astype(F32) * 0.125).astype(BF16))
            here[1].append(dk[:RP].astype(BF16))
            here[2].append(dv[:RP].astype(BF16))
        for i in range(3):
            grads[i].append(jnp.concatenate(here[i], axis=1))
    gq, gk, gv = (jnp.concatenate(each, axis=0) for each in grads)
    wide = QUAD * HEAD
    for i, each in enumerate((gq, gk, gv)):
        for g in range(steps):

            @pl.when(step == g)
            def _():
                parts_ref[:, i * D + g * wide : i * D + g * wide + wide] = each
    for n in range(images):
        for h in range(QUAD):
            sums = [None, None]
            for g in range(0, 16, 2):
                blocks = [(g, 0)] + ([(g + 16, 1)] if 8 * (g + 16) < RP else [])
                loaded = {}
                for start, _ in blocks:
                    both = sg_ref[QUAD * n + h, 8 * start : 8 * start + 16].astype(F32)
                    above = jnp.where(upper_ref[n, 8 * start : 8 * start + 16] > 0.0, both, 0.0)
                    loaded[start] = (above, both - above)
                for u in range(2):
                    for i in range(2):
                        cut = lambda s, k: loaded[s][u][8 * i : 8 * i + 8, 128 * k : 128 * k + 128]
                        zero = jnp.zeros((8, 128), F32)
                        tiles = [cut(g, 0), cut(g, 1), zero, zero]
                        if len(blocks) > 1:
                            tiles = [tiles[0] + cut(g + 16, 1), tiles[1], zero, cut(g + 16, 0)]
                        block = jnp.concatenate(tiles, axis=1)
                        if g + i:
                            block = pltpu.roll(block, SPAN - 8 * (g + i), 1)
                        sums[u] = block if sums[u] is None else sums[u] + block
            for u in range(2):
                rows_ref[2 * n + u, pl.ds(step * QUAD + h, 1)] = straighten(sums[u])
    bias_ref[0] = column_sum(gq.astype(F32))
    bias_ref[1] = column_sum(gv.astype(F32))
    ng_ref[...] += dot(gq, wq_ref[...], NT) + dot(gk, wk_ref[...], NT) + dot(gv, wv_ref[...], NT)

    @pl.when(step == steps - 1)
    def _():
        whitened, inverse = norm_stats(u_ref[...].astype(F32))
        ng = ng_ref[...]
        bg = bg_ref[...]
        next_ref[...] = bg + norm_back(ng, whitened, inverse, gain)
        small_ref[...] = jnp.zeros_like(small_ref)
        small_ref[0:1] = column_sum(ng * whitened)
        small_ref[1:2] = column_sum(ng)
        small_ref[2:3] = column_sum(out_ref[...].astype(F32))
        small_ref[3:4] = column_sum(bg * branch_ref[...].astype(F32) * live_ref[...])
        part, each = 3 * D // sections, D // sections
        for own in range(sections):

            @pl.when(me == own)
            def _():
                for s in range(sections):
                    place = sends - 1 - ((s // 2) ^ (own // 2))
                    target = (keep_ref if s % 2 == own % 2 else send_ref).at[place]
                    target[:, :part] = parts_ref[:, part * s : part * s + part]
                    target[:, part:] = out_ref[:, each * s : each * s + each]
        finish()


def middle_chain_kernel(
    images, sections, me_ref, order_ref, u_ref, bg_ref, gain_ref, scale_ref, fgain_ref, fscale_ref, live_ref, q_ref,
    k_ref, v_ref, w_ref, branch_ref, wq_ref, wk_ref, wv_ref, wo_ref, upper_ref, u_feed_ref, branch_feed_ref, slope_ref,
    wh_ref, wr_ref,
    next_ref, send_ref, keep_ref, rows_ref, bias_ref, small_ref, feed_small_ref, hb_ref, hg_keep_ref, hg_send_ref,
    ng_ref, out_ref, wg_ref, sg_ref, parts_ref,
):
    t = pl.program_id(0)
    steps = HEADS // QUAD
    att, feed = slice(LAYERS - 1, LAYERS), slice(LAYERS - 2, LAYERS - 1)
    out_rows_ref = hg_send_ref.at[sections // 2]

    def finish():
        out_rows_ref[...] = (next_ref[...] * fscale_ref[feed] * live_ref[...]).astype(BF16)

    @pl.when(t < steps)
    def _():
        attention_steps(
            t, images, sections, me_ref[0], gain_ref[att], scale_ref[att], finish, u_ref, bg_ref, live_ref, q_ref, k_ref,
            v_ref, w_ref, branch_ref, wq_ref, wk_ref, wv_ref, wo_ref, upper_ref, next_ref, send_ref, keep_ref, rows_ref,
            bias_ref, small_ref, ng_ref, out_ref, wg_ref, sg_ref, parts_ref,
        )

    @pl.when(t >= steps)
    def _():
        feed_steps(
            t - steps, sections, fgain_ref[feed], lambda: None, out_rows_ref, u_feed_ref, live_ref, branch_feed_ref,
            slope_ref, wh_ref, wr_ref, next_ref, feed_small_ref, hb_ref, hg_send_ref, hg_keep_ref, ng_ref,
        )


def attention_specs(layer, images, at):
    m = images * RP
    mc = (images - 1) * RP + CP
    wide = QUAD * HEAD
    steps = HEADS // QUAD
    block = lambda count: pl.BlockSpec((None, count, wide), lambda t, *_: (layer, 0, at(t)))
    third = lambda which: pl.BlockSpec((None, D, wide), lambda t, *_: (layer, 0, which * steps + at(t)))
    return [
        block(m), block(mc), block(mc),
        pl.BlockSpec((None, images, QUAD, RP, CP), lambda t, *_: (layer, 0, at(t), 0, 0)),
        layer_block(layer, m, D), third(0), third(1), third(2),
        pl.BlockSpec((None, wide, D), lambda t, *_: (layer, at(t), 0)), whole(images, RP, CP),
    ]


def attention_out(images, sections, at):
    m = images * RP
    sends = sections // 2
    shape = jax.ShapeDtypeStruct
    specs = [
        whole(m, D), whole(sends, m, D), whole(sends, m, D), whole(2 * images, HEADS, SPAN),
        pl.BlockSpec((2, 1, QUAD * HEAD), lambda t, *_: (0, 0, at(t))), whole(8, D),
    ]
    shapes = [
        shape((m, D), F32), shape((sends, m, D), BF16), shape((sends, m, D), BF16),
        shape((2 * images, HEADS, SPAN), F32), shape((2, 1, D), F32), shape((8, D), F32),
    ]
    return specs, shapes


def attention_scratch(images):
    m = images * RP
    return [
        pltpu.VMEM((m, D), F32), pltpu.VMEM((m, D), BF16), pltpu.VMEM((images * QUAD, RP, CP), F32),
        pltpu.VMEM((images * QUAD, RP, CP), BF16), pltpu.VMEM((m, 3 * D), BF16),
    ]


def attention_operands(kept, w, tables):
    return [
        kept.q, kept.k, kept.v, kept.w, kept.branch_att, w.input_projection, w.input_projection, w.input_projection,
        w.output_projection, tables.upper,
    ]


def middle_chain(images, sections, me, order, bg, cross, kept, w, tables, after):
    m = images * RP
    wide = FF // sections
    sends = sections // 2
    steps = HEADS // QUAD
    late = lambda t: jnp.maximum(t - steps, 0)
    early = lambda t: jnp.minimum(t, steps - 1)
    shape = jax.ShapeDtypeStruct
    out_specs, out_shape = attention_out(images, sections, early)
    return run(
        functools.partial(middle_chain_kernel, images, sections),
        grid=(steps + sections,),
        prefetch=[me, order],
        in_specs=[slot(LAYERS - 1, IN_ATT, m), whole(m, D)] + [whole(LAYERS, D)] * 4 + [whole(m, 1)]
        + attention_specs(LAYERS - 1, images, early)
        + [
            slot(LAYERS - 2, IN_FEED, m), layer_block(LAYERS - 2, m, D),
            pl.BlockSpec((None, None, m, wide), lambda t, me, order: (LAYERS - 2, late(t), 0, 0)),
            pl.BlockSpec((None, D, wide), lambda t, me, order: (LAYERS - 2, 0, order[late(t)])),
            pl.BlockSpec((None, wide, D), lambda t, me, order: (LAYERS - 2, order[late(t)], 0)),
        ],
        out_specs=out_specs + [
            whole(8, D), pl.BlockSpec((None, 1, wide), lambda t, *_: (late(t), 0, 0)),
            pl.BlockSpec((None, m, wide), lambda t, *_: (jnp.maximum(late(t) - sends, 0), 0, 0)),
            whole(sends + 1, m, wide),
        ],
        out_shape=out_shape + [
            shape((8, D), F32), shape((sections, 1, wide), F32), shape((sends, m, wide), BF16),
            shape((sends + 1, m, wide), BF16),
        ],
        scratch=attention_scratch(images),
        operands=[cross, bg, w.attention_gain, w.attention_scale, w.forward_gain, w.forward_scale, tables.live]
        + attention_operands(kept, w, tables)
        + [cross, kept.branch_feed, kept.slope, w.hidden_weight, w.return_weight],
        after=after,
        name="middle_chain",
    )


def last_chain_kernel(images, sections, me_ref, u_ref, bg_ref, gain_ref, scale_ref, live_ref, *refs):
    first = 10 + sections
    ins, early_refs, outs, piece_refs, scratch = (
        refs[:10], refs[10:first], refs[first : first + 6], refs[first + 6 : first + 6 + sections], refs[-5:]
    )
    next_ref = outs[0]

    def finish():
        for early_ref, piece_ref in zip(early_refs, piece_refs):
            piece_ref[0] = early_ref[...]
        send_pieces(me_ref[0], images, next_ref, [piece.at[1] for piece in piece_refs])

    attention_steps(
        pl.program_id(0), images, sections, me_ref[0], gain_ref[0:1], scale_ref[0:1], finish, u_ref, bg_ref, live_ref,
        *ins, *outs, *scratch,
    )


def last_chain(images, sections, me, bg, cross, kept, w, tables, after, early):
    m = images * RP
    at = lambda t: t
    out_specs, out_shape = attention_out(images, sections, at)
    return run(
        functools.partial(last_chain_kernel, images, sections),
        grid=(HEADS // QUAD,),
        prefetch=[me],
        in_specs=[slot(0, IN_ATT, m), whole(m, D)] + [whole(LAYERS, D)] * 2 + [whole(m, 1)]
        + attention_specs(0, images, at) + [whole(*piece.shape) for piece in early],
        out_specs=out_specs + [whole(2, *piece.shape) for piece in early],
        out_shape=out_shape + [jax.ShapeDtypeStruct((2,) + piece.shape, BF16) for piece in early],
        scratch=attention_scratch(images),
        operands=[cross, bg, w.attention_gain, w.attention_scale, tables.live, *attention_operands(kept, w, tables), *early],
        after=after,
        name="last_chain",
    )


def attention_product(nt, at, grads):
    first = 3 * D // (4 * 128) * 128
    low = lax.broadcasted_iota(jnp.int32, (1, 128), 1) < HEAD
    left = dot(nt, grads[:, : first + 128])
    right = dot(at, grads[:, first:])
    middle = jnp.where(low, left[:, first:], right[:, :128])
    return jnp.concatenate([left[:, :first], middle, right[:, 128:]], axis=1)


def attention_keep_kernel(layer, own_ref, u_ref, u_got_ref, att_ref, att_got_ref, gain_ref, shift_ref, grads_ref, *refs):
    got_ref, out_refs, (nt_ref, at_ref) = refs[0], refs[1:5], refs[5:]

    @pl.when(pl.program_id(0) == 0)
    def _():
        gain, shift = gain_ref[layer : layer + 1], shift_ref[layer : layer + 1]
        for i, (u, att) in enumerate(((u_ref, att_ref), (u_got_ref, att_got_ref))):
            nt_ref[i] = turned_norm(u, gain, shift)
            at_ref[i] = att[...].T

    total = attention_product(nt_ref[0], at_ref[0], grads_ref[...])
    total += attention_product(nt_ref[1], at_ref[1], got_ref[...])
    store_halves([total], own_ref[0], *out_refs)


def attention_keep(layer, own, rows, cross, cross_got, grads, got, w, after):
    sends, m, _ = grads.shape
    out_specs, out_shape = halves_out(1, sends, rows)
    return run(
        functools.partial(attention_keep_kernel, layer),
        grid=(sends,),
        in_specs=[
            slot(layer, IN_ATT, m), slot(layer, IN_ATT, m), slot(layer, ATTENDED, m), slot(layer, ATTENDED, m),
            whole(LAYERS, D), whole(LAYERS, D),
        ] + [pl.BlockSpec((None, m, D), lambda i, own: (i, 0, 0))] * 2,
        out_specs=out_specs,
        out_shape=out_shape,
        scratch=[pltpu.VMEM((2, D, m), BF16), pltpu.VMEM((2, D, m), BF16)],
        prefetch=[own],
        operands=[cross, cross_got, cross, cross_got, w.attention_gain, w.attention_shift, grads, got],
        after=after,
        name="attention_keep",
    )


def flip(value, axis, bit):
    count = lax.axis_size(axis)
    return lax.ppermute(value, axis, [(i, i ^ bit) for i in range(count)])


def wide_names():
    return [(WIDE, 1 << i) for i in reversed(range(lax.axis_size(WIDE).bit_length() - 1))]


def own_bit(axis, bit):
    return (lax.axis_index(axis) // bit) % 2


ACROSS = (SECTION, 2)


class Chunk:
    def __init__(self, keep, received, lead, names, order, rows):
        self.width = keep.shape[-1]
        self.rows = rows
        shape = keep.shape[:1] + (2,) * len(names) + (rows, self.width)
        self.terms = [(array.reshape(shape), lead, tuple(names)) for array in (keep, received)]
        self.left = tuple(names)
        self.done = ()
        self.order = list(order)

    def arrived(self):
        return [self.terms[-1][0]]


class Small:
    def __init__(self, keep, received):
        self.terms = [keep, received]
        self.order = [ACROSS] + list(reversed(wide_names()))


def combine(groups, mine, after, name, writer=None, out_shape=None, small=None, held=()):
    all_names = wide_names()
    specs, operands, counts, out_specs, shapes = [], [], [], [], []
    rows = groups[0][0].rows if groups else 0
    split = 2 if rows % 32 == 0 and writer is None else 1
    rows = rows // split
    for group in groups:
        for chunk in group:
            stage = None if writer else chunk.order[0]
            for array, lead, names in chunk.terms:
                fixed = [n in chunk.done or n == stage for n in names]
                block = (None,) + tuple(None if f else 2 for f in fixed) + (rows, chunk.width)

                def index(i, mine_ref, lead=lead, names=names, fixed=fixed, stage=stage):
                    at = []
                    for n, f in zip(names, fixed):
                        own = 1 if n == ACROSS else mine_ref[all_names.index(n)]
                        at.append((1 - own if n == stage else own) if f else 0)
                    return (lead, *at, i, 0)

                specs.append(pl.BlockSpec(block, index))
                operands.append(array)
            counts.append(len(chunk.terms))
        if writer is None:
            chunk = group[0]
            dims = (len(group),) + (2,) * (len(chunk.left) - 1)
            shapes.append(jax.ShapeDtypeStruct(dims + (chunk.rows, chunk.width), BF16))
            out_specs.append(
                pl.BlockSpec(dims + (rows, chunk.width), lambda i, mine_ref, n=len(dims): (0,) * n + (i, 0))
            )
    if writer:
        shapes = out_shape
        out_specs = [whole(*s.shape) for s in shapes]

    if small:
        specs += [whole(*term.shape) for term in small.terms]
        operands += small.terms
        shape = small.terms[0].shape[-2:]
        shapes += [jax.ShapeDtypeStruct(shape, F32)] * (1 + (small.order[0] == ACROSS))
        out_specs += [whole(*shape)] * (len(shapes) - len(out_specs))

    def kernel(mine_ref, *refs):
        ins, outs = refs[: len(operands)], refs[len(operands) :]
        if small:
            value = ins[-2][...] + ins[-1][...]
            if small.order[0] == ACROSS:
                outs[-2][...], outs[-1][...] = value[0], value[1]
            else:
                outs[-1][...] = value
        totals, at = [], 0
        for count in counts:
            total = ins[at][...].astype(F32)
            for ref in ins[at + 1 : at + count]:
                total = total + ref[...].astype(F32)
            totals.append(total)
            at += count
        if writer:
            writer(outs, totals)
            return
        for group, out in zip(groups, outs):
            for j in range(len(group)):
                out[j] = totals.pop(0).astype(BF16)

    results = run(
        kernel, grid=(split,), in_specs=specs, out_specs=out_specs, out_shape=shapes,
        prefetch=[mine], operands=operands, after=list(after), held=held, name=name,
    )
    if writer:
        return results
    held_count = len(held)
    results, held = results[: len(results) - held_count], results[len(results) - held_count :]
    if small:
        stage = small.order[0]
        small.order = small.order[1:]
        small.terms = [results[-1], flip(results[-2] if stage == ACROSS else results[-1], *stage)]
    for group, sent in zip(groups, results):
        stage = group[0].order[0]
        got = flip(sent, *stage)
        for j, chunk in enumerate(group):
            chunk.order = chunk.order[1:]
            chunk.done = chunk.done + (stage,)
            chunk.left = tuple(n for n in chunk.left if n != stage)
            chunk.terms = chunk.terms + [(got, j, chunk.left)]
    return (results, held) if held else results


def pack_kernel(sections, me_ref, index_ref, rows0_ref, rows1_ref, a0_ref, a1_ref, f0_ref, f1_ref, b0_ref, b1_ref,
                h0_ref, h1_ref, send_ref, keep_ref, sum_ref):
    step = pl.program_id(0)

    @pl.when(step == 0)
    def _():
        sum_ref[...] = jnp.zeros_like(sum_ref)

    chosen = (lax.broadcasted_iota(jnp.int32, (TABLE, SPAN), 0) == index_ref[...]).astype(F32).astype(BF16)
    rows = jnp.concatenate([rows0_ref[...], rows1_ref[...]], axis=0)
    high = rows.astype(BF16)
    low = (rows - high.astype(F32)).astype(BF16)
    sum_ref[...] += dot(high, chosen, NT) + dot(low, chosen, NT)
    each = D // sections
    heads = HEADS // sections
    sends = sections // 2
    tiles = TABLE // 256
    layers = ((a0_ref, f0_ref, b0_ref, h0_ref), (a1_ref, f1_ref, b1_ref, h1_ref))

    def fill(own):
        for s in range(sections):
            place = sends - 1 - ((s // 2) ^ (own // 2))
            ref = (keep_ref if s % 2 == own % 2 else send_ref).at[place]
            lanes = slice(each * s, each * s + each)
            for layer, (a_ref, f_ref, b_ref, h_ref) in enumerate(layers):
                at = layer * SMALL
                ref[at : at + 4, 0:each] = a_ref[0:4, lanes]
                ref[at + 4 : at + 8, 0:each] = f_ref[0:4, lanes]
                for i in range(2):
                    ref[at + 8 + i : at + 9 + i, 0:each] = b_ref[i, :, lanes]
                where = place + (sends if s % 2 == own % 2 else 0)
                for j in range(FF // sections // 256):
                    ref[at + 10 + j : at + 11 + j] = h_ref[where, :, 256 * j : 256 * j + 256]
                for k in range(heads):
                    row = layer * HEADS + s * heads + k
                    for j in range(tiles):
                        to = at + 13 + k * tiles + j
                        ref[to : to + 1] = sum_ref[row : row + 1, 256 * j : 256 * j + 256]

    @pl.when(step == pl.num_programs(0) - 1)
    def _():
        send_ref[...] = jnp.zeros_like(send_ref)
        keep_ref[...] = jnp.zeros_like(keep_ref)
        for own in range(sections):
            pl.when(me_ref[0] == own)(functools.partial(fill, own))


def pack(me, sections, index, rows, att, feed, bias, hidden, after):
    places = index.shape[0]
    row = pl.BlockSpec((None, HEADS, SPAN), lambda i, me: (i, 0, 0))
    hidden_wide = FF // sections
    shape = (sections // 2, LAYERS * SMALL, 256)
    return run(
        functools.partial(pack_kernel, sections),
        grid=(places,),
        prefetch=[me],
        in_specs=[pl.BlockSpec((None, 1, SPAN), lambda i, me: (i, 0, 0)), row, row]
        + [whole(8, D)] * 4 + [whole(2, 1, D)] * 2 + [whole(sections, 1, hidden_wide)] * 2,
        out_specs=[whole(*shape)] * 2,
        out_shape=[jax.ShapeDtypeStruct(shape, F32)] * 2,
        scratch=[pltpu.VMEM((LAYERS * HEADS, TABLE), F32)],
        operands=[index, *rows, *att, *feed, *bias, *hidden],
        after=after,
        name="pack",
    )


def unpack_kernel(keep_ref, got_ref, *out_refs):
    *vector_refs, hidden_ref, table_ref, small_ref = out_refs
    small_ref[...] = keep_ref[...] + got_ref[...]
    each = vector_refs[0].shape[1]
    heads = table_ref.shape[0]
    tiles = TABLE // 256
    for layer in range(LAYERS):
        at = layer * SMALL
        for i, ref in enumerate(vector_refs):
            ref[layer : layer + 1] = small_ref[at + i : at + i + 1, 0:each]
        for j in range(hidden_ref.shape[1] // 256):
            hidden_ref[layer : layer + 1, 256 * j : 256 * j + 256] = small_ref[at + 10 + j : at + 11 + j]
        for k in range(heads):
            row = at + 13 + k * tiles
            line = jnp.concatenate([small_ref[r : r + 1] for r in range(row, row + tiles)], axis=1)
            table_ref[k, layer : layer + 1] = line[:, :REL]


def unpack(small, sections, after):
    shape = jax.ShapeDtypeStruct
    out_shape = [shape((LAYERS, D // sections), F32)] * 10
    out_shape += [shape((LAYERS, FF // sections), F32), shape((HEADS // sections, LAYERS, REL), F32)]
    return run(
        unpack_kernel, grid=(1,), in_specs=[whole(LAYERS * SMALL, 256)] * 2, out_specs=[whole(*s.shape) for s in out_shape],
        out_shape=out_shape, operands=small.terms, scratch=[pltpu.VMEM((LAYERS * SMALL, 256), F32)], after=after,
        name="unpack",
    )


def assemble_kernel(me_ref, *refs):
    *piece_refs, output_ref, grad_ref = refs
    images = piece_refs[0].shape[1]
    for distance, piece in enumerate(piece_refs):
        rows = pl.ds((me_ref[0] ^ distance) * images, images)
        output_ref[rows] = piece[0]
        grad_ref[rows] = piece[1]


def assemble(me, pieces, after):
    sections = len(pieces)
    _, images, width, rows = pieces[0].shape
    shape = (sections * images, width, rows)
    return run(
        assemble_kernel, grid=(1,), prefetch=[me], in_specs=[whole(*pieces[0].shape)] * sections,
        out_specs=[whole(*shape)] * 2, out_shape=[jax.ShapeDtypeStruct(shape, BF16)] * 2,
        operands=pieces, after=after, name="assemble",
    )


def on_device(
    tokens, cotangent, patch_grids, attention_gain, attention_shift, input_projection, query_bias, value_bias,
    relative_table, output_projection, output_bias, attention_scale, forward_gain, forward_shift, hidden_weight,
    hidden_bias, return_weight, return_bias, forward_scale,
):
    sections = lax.axis_size(SECTION)
    me = lax.axis_index(SECTION).astype(jnp.int32)
    me_row = me.reshape(1)
    images = tokens.shape[0] // sections
    m = images * RP
    rows = D // lax.axis_size(WIDE)
    w = Weights(
        attention_gain, attention_shift, input_projection, query_bias, value_bias, output_projection, output_bias,
        attention_scale, forward_gain, forward_shift, hidden_weight, hidden_bias, return_weight, return_bias,
        forward_scale,
    )
    grids = lax.dynamic_slice_in_dim(patch_grids, me * images, images, 0)
    height, width = grids[:, 0:1], grids[:, 1:2]
    place = lax.broadcasted_iota(jnp.int32, (images, CP), 1)
    live = place < height * width
    column = place % width
    turn = lax.broadcasted_iota(jnp.int32, (images, SPAN), 1)
    gap = jnp.where(turn < CP, -turn, SPAN - turn)
    b = jnp.mod(gap, width)
    a = (gap - b) // width
    entry = lambda p, q: jnp.clip(p + HMAX - 1, 0, 2 * HMAX - 2) * QW + jnp.clip(q + WMAX - 1, 0, QW - 1)
    index = jnp.stack([entry(a, b), entry(a + 1, b - width)], axis=1).reshape(2 * images, 1, SPAN)
    table = jnp.transpose(relative_table, (0, 2, 1)).reshape(LAYERS * HEADS, REL)
    table = jnp.pad(table, ((0, 0), (0, TABLE - REL)))
    tables = Tables(
        live[:, :RP].reshape(m, 1).astype(F32),
        jnp.where(live, 0.0, -1e9).astype(F32).reshape(images, 1, CP),
        (column[:, :RP, None] >= column[:, None, :]).astype(F32),
        bias_rows(table, index),
    )
    high, core = me // 2, me % 2
    order = jnp.stack([2 * (1 - high) + 1 - core, 2 * high + 1 - core, 2 * (1 - high) + core, 2 * high + core])
    cross, kept, pieces = forward(images, sections, me_row, order, tokens, cotangent, w, tables)

    names = wide_names()
    mine_bits = jnp.stack([own_bit(*name) for name in names]).astype(jnp.int32)
    own = own_bit(WIDE, 1).astype(jnp.int32).reshape(1)
    first = names[-1]
    core_flip = lambda sent: flip(sent, SECTION, 1)

    def launch(a_send, a_keep, b_send, b_keep):
        a_got, b_got = flip(a_send, *ACROSS), flip(b_send, *first)
        across = [ACROSS] + names[:-1]
        chunks = []
        for j in range(a_keep.shape[0]):
            chunks.append((
                Chunk(a_keep, a_got, j, names, list(reversed(names)), rows),
                Chunk(b_keep, b_got, j, across, [ACROSS] + list(reversed(names[:-1])), rows),
            ))
        left, right = zip(*chunks)
        return list(left), list(right), [a_got, b_got]

    def step(groups, after, name, small=None, held=()):
        return combine(groups, mine_bits, after, name, small=small, held=held)

    def finish(groups, after, name, writer, out_shape):
        while any(group[0].order for group in groups):
            after = step([group for group in groups if group[0].order], after, name)
        return combine(groups, mine_bits, after, name, writer, out_shape)

    cross_got = core_flip(cross)
    spec = slot(1, OUT_FEED, m)
    bg, feed_small1, hidden1, hg, sent = first_chain(images, sections, me_row, order, cotangent, cross, kept, w, tables)
    out = feed_keep(
        1, own, rows, cross, cross_got, [spec, spec], cross, cross_got, kept.active, hg, core_flip(sent), w, [bg]
    )
    a1, b1, launched = launch(*out)
    bg, grads_sent, grads, *small1, feed_small0, hidden0, hg, sent = middle_chain(
        images, sections, me_row, order, bg, cross, kept, w, tables, out[1:2]
    )
    grads_sent, sent = hold([grads_sent, sent], [bg, *launched])
    grads_got = core_flip(grads_sent)
    sent_got = core_flip(sent)
    last = step([a1, b1], [grads_sent], "second")
    spec = pl.BlockSpec((None, m, D), lambda *_: (sections // 2, 0, 0))
    out = feed_keep(
        0, own, rows, sent, sent_got, [spec, spec], cross, cross_got, kept.active, hg, sent_got, w, last
    )
    a0, b0, _ = launch(*out)
    last = step([a1 + b1], [*out[1:2], grads_got], "third")
    a_send, a_keep, b_send, b_keep = attention_keep(1, own, rows, cross, cross_got, grads, grads_got, w, last)
    pa1, pb1, launched = launch(a_send, a_keep, b_send, b_keep)
    last = [b_keep]
    bg, grads0_sent, grads0, *rest = last_chain(images, sections, me_row, bg, cross, kept, w, tables, last, pieces)
    small0, pieces = rest[:3], rest[3:]
    pieces = pieces[:1] + [flip(pieces[d], SECTION, d) for d in range(1, sections)]
    last, (grads0_sent,) = step([a0, b0, a1 + b1], [bg], "second", held=[grads0_sent])
    grads0_got = core_flip(grads0_sent)
    (a_keep,) = hold([a_keep], [grads0_got])
    a_send, a_keep, b_send, b_keep = attention_keep(0, own, rows, cross, cross_got, grads0, grads0_got, w, [a_keep])
    last, (a_send, b_send) = step([a0 + b0], [a_keep, *a1[0].arrived(), *b1[0].arrived()], "third", held=[a_send, b_send])
    pa0, pb0, _ = launch(a_send, a_keep, b_send, b_keep)
    core_sent, core_kept = pack(
        me_row, sections, index, (small0[0], small1[0]), (small0[2], small1[2]), (feed_small0, feed_small1),
        (small0[1], small1[1]), (hidden0, hidden1), last,
    )
    (core_sent,) = hold([core_sent], launched)
    small = Small(core_kept, core_flip(core_sent))
    last = step([a0 + b0], [core_sent], "fourth", small)
    last = step([pa0 + pa1, pb0 + pb1], last, "second", small)
    last = step([pa0 + pb0 + pa1 + pb1], last, "third", small)

    def write_feed(outs, totals):
        for layer in range(LAYERS):
            ra, ha, rb, hb = totals[4 * layer : 4 * layer + 4]
            half = D // 2
            outs[0][layer, :, :half] = ha
            outs[0][layer, :, half:] = hb
            outs[1][layer, :, :half] = ra
            outs[1][layer, :, half:] = rb

    def write_attention(outs, totals):
        part = 3 * D // sections
        for layer in range(LAYERS):
            left, right = totals[2 * layer], totals[2 * layer + 1]
            outs[0][layer, :, : D // 2] = left
            outs[0][layer, :, D // 2 :] = right[:, : part - D // 2]
            outs[1][layer] = right[:, part - D // 2 :]

    shape = lambda *s: jax.ShapeDtypeStruct(s, F32)
    wide = FF // sections
    hidden_grad, return_grad = finish(
        [a0 + b0, a1 + b1], last, "last", write_feed, [shape(LAYERS, rows, wide)] * 2
    )
    last = step([pa0 + pb0 + pa1 + pb1], [hidden_grad], "fourth", small)
    layer_output, input_grad = assemble(me_row, pieces, last)
    projection_grad, out_grad = finish(
        [pa0 + pb0, pa1 + pb1], [layer_output], "last", write_attention,
        [shape(LAYERS, rows, 3 * D // sections), shape(LAYERS, rows, D // sections)],
    )
    while small.order:
        last = combine([], mine_bits, [], "more", small=small)
    vectors = unpack(small, sections, [out_grad])
    gain, shift, out_shift, scale, fgain, fshift, return_shift, fscale, query, value, hidden_shift, table_grad = vectors
    return (
        jnp.swapaxes(layer_output, 1, 2), jnp.swapaxes(input_grad, 1, 2), gain, shift, projection_grad, query, value, jnp.transpose(table_grad, (1, 2, 0)), out_grad, out_shift, scale,
        fgain, fshift, hidden_grad, hidden_shift, jnp.swapaxes(return_grad, 1, 2), return_shift, fscale,
    )


def solution(mesh):
    three, two = P(WIDE, None, SECTION), P(None, SECTION)
    weight = P(None, WIDE, SECTION)
    return jax.shard_map(
        on_device,
        mesh=mesh,
        in_specs=(P(WIDE, None, None), P(WIDE, None, None), P(WIDE, None)) + (P(),) * 16,
        out_specs=(
            three, three, two, two, weight, two, two, P(None, None, SECTION), weight, two, two, two, two,
            weight, two, P(None, SECTION, WIDE), two, two,
        ),
        check_vma=False,
    )
```

```python
import functools
from typing import NamedTuple

import jax
import jax.numpy as jnp
from jax import lax
from jax.experimental import pallas as pl
from jax.experimental.pallas import tpu as pltpu
from jax.sharding import PartitionSpec as P

SECTION = "section"
WIDE = "wide"
D = 768
HEADS = 12
HEAD = 64
FF = 3072
IN_ATT, IN_FEED, ATTENDED, OUT_FEED, ACTIVE = range(5)
ROWS = 200
HMAX = 14
WMAX = 24
REL = 1269
LAYERS = 2
QW = 2 * WMAX - 1
RP = 208
CP = 256
SPAN = 512
TABLE = 1280
SMALL = 28
QUAD = 4
F32 = jnp.float32
BF16 = jnp.bfloat16
NN = (((1,), (0,)), ((), ()))
NT = (((1,), (1,)), ((), ()))
TN = (((0,), (0,)), ((), ()))
VMEM = 48 * 1024 * 1024


def dot(left, right, dims=NN):
    return lax.dot_general(left, right, dims, preferred_element_type=F32)


def whole(*shape):
    return pl.BlockSpec(shape, lambda *_: (0,) * len(shape))


class Kept(NamedTuple):
    active: jax.Array
    q: jax.Array
    k: jax.Array
    v: jax.Array
    w: jax.Array
    branch_att: jax.Array
    slope: jax.Array
    branch_feed: jax.Array


class Weights(NamedTuple):
    attention_gain: jax.Array
    attention_shift: jax.Array
    input_projection: jax.Array
    query_bias: jax.Array
    value_bias: jax.Array
    output_projection: jax.Array
    output_bias: jax.Array
    attention_scale: jax.Array
    forward_gain: jax.Array
    forward_shift: jax.Array
    hidden_weight: jax.Array
    hidden_bias: jax.Array
    return_weight: jax.Array
    return_bias: jax.Array
    forward_scale: jax.Array


class Tables(NamedTuple):
    live: jax.Array
    mask: jax.Array
    upper: jax.Array
    rows: jax.Array


def run(kernel, *, grid, in_specs, out_specs, out_shape, operands, scratch=(), prefetch=(), after=(), held=(), name):
    first = len(prefetch) + len(in_specs)
    count = len(after) + len(held)
    outs = len(out_shape)

    def body(*refs):
        kept = refs[:first] + refs[first + count : first + count + outs]
        kernel(*kept, *refs[first + count + outs + len(held) :])

    anywhere = pl.BlockSpec(memory_space=pl.ANY)
    return pl.pallas_call(
        body,
        grid_spec=pltpu.PrefetchScalarGridSpec(
            num_scalar_prefetch=len(prefetch),
            grid=grid,
            in_specs=list(in_specs) + [anywhere] * count,
            out_specs=list(out_specs) + [anywhere] * len(held),
            scratch_shapes=list(scratch),
        ),
        out_shape=list(out_shape) + [jax.ShapeDtypeStruct(v.shape, v.dtype) for v in held],
        input_output_aliases={first + len(after) + i: outs + i for i in range(len(held))},
        compiler_params=pltpu.CompilerParams(vmem_limit_bytes=VMEM),
        cost_estimate=pl.CostEstimate(flops=10**6, bytes_accessed=10**5, transcendentals=0),
        name=name,
    )(*prefetch, *operands, *after, *held)


def hold(held, after):
    def kernel(out_ref):
        out_ref[...] = jnp.zeros_like(out_ref)

    tiny = [jax.ShapeDtypeStruct((8, 128), F32)]
    _, *held = run(
        kernel, grid=(1,), in_specs=[], out_specs=[whole(8, 128)], out_shape=tiny, operands=[], after=after, held=held,
        name="hold",
    )
    return held


def norm_stats(u):
    mean = jnp.mean(u, axis=1, keepdims=True)
    centered = u - mean
    inverse = lax.rsqrt(jnp.mean(centered * centered, axis=1, keepdims=True) + 1e-6)
    return centered * inverse, inverse


def norm_back(upstream, whitened, inverse, gain):
    scaled = upstream * gain
    first = jnp.mean(scaled, axis=1, keepdims=True)
    second = jnp.mean(scaled * whitened, axis=1, keepdims=True)
    return (scaled - first - whitened * second) * inverse


def column_sum(v):
    return jnp.sum(v, axis=0, keepdims=True)


def head_masks():
    lane = lax.broadcasted_iota(jnp.int32, (1, 2 * HEAD), 1)
    low = (lane < HEAD).astype(F32)
    return low.astype(BF16), (1.0 - low).astype(BF16)


def bias_rows_kernel(table_ref, index_ref, out_ref):
    table = table_ref[...]
    high = table.astype(BF16)
    rest = table - high.astype(F32)
    middle = rest.astype(BF16)
    low = (rest - middle.astype(F32)).astype(BF16)
    chosen = (lax.broadcasted_iota(jnp.int32, (table.shape[1], SPAN), 0) == index_ref[...]).astype(F32).astype(BF16)
    out_ref[...] = dot(high, chosen) + dot(middle, chosen) + dot(low, chosen)


def bias_rows(table, index):
    places = index.shape[0]
    return run(
        bias_rows_kernel,
        grid=(places,),
        in_specs=[whole(*table.shape), pl.BlockSpec((None, 1, SPAN), lambda i: (i, 0, 0))],
        out_specs=[pl.BlockSpec((None, table.shape[0], SPAN), lambda i: (i, 0, 0))],
        out_shape=[jax.ShapeDtypeStruct((places, table.shape[0], SPAN), F32)],
        operands=[table, index],
        name="bias_rows",
    )[0]


def diagonal_base(row):
    return pltpu.roll(jnp.broadcast_to(row, (8, SPAN)), 0, 1, stride=1, stride_axis=0)


def row_blocks():
    return [(16 * c, [(128 * t + 16 * c, t) for t in range(2) if 128 * t + 16 * c < RP]) for c in range(8)]


def turned_pair(base, turn):
    return [pltpu.roll(base, turn + 8 * i, 1) if turn + 8 * i else base for i in range(2)]


def diagonal_block(pair, tiles):
    pick = lambda v, k: v[:, 128 * ((k - tiles) % 4) : 128 * ((k - tiles) % 4) + 128]
    return jnp.concatenate([jnp.concatenate([pick(v, k) for k in range(CP // 128)], axis=1) for v in pair], axis=0)


def straighten(sums):
    row = lax.broadcasted_iota(jnp.int32, (8, 1), 0)
    for bit in (1, 2, 4):
        sums = jnp.where((row // bit) % 2 == 1, pltpu.roll(sums, SPAN - bit, 1), sums)
    return column_sum(sums)


def forward_kernel(
    images, steps, sections,
    me_ref, order_ref, tokens_ref, cot_ref, gain_ref, shift_ref, wq_ref, wk_ref, wv_ref, qb_ref, vb_ref, rows_ref,
    wo_ref, ob_ref, scale_ref, fgain_ref, fshift_ref, wh_ref, hb_ref, wr_ref, rb_ref, fscale_ref, live_ref, mask_ref,
    upper_ref, *refs,
):
    cross_ref, active_ref, q_ref, k_ref, v_ref, w_ref, branch_att_ref, slope_ref, branch_feed_ref, *refs = refs
    piece_refs, (now_ref, total_ref, acc_ref, scores_ref, normed_ref, att_ref) = refs[:sections], refs[sections:]
    t = pl.program_id(0)
    per = steps + sections
    phase = lax.rem(t, per)
    m = images * RP
    layer = t // per
    own = pl.ds(layer, 1)
    lanes_of = lambda at, width: pl.ds(pl.multiple_of(at * width, width), width)

    @pl.when(t == 0)
    def _():
        now_ref[...] = jnp.zeros_like(now_ref)
        for n in range(images):
            now_ref[RP * n : RP * n + ROWS] = tokens_ref[n]
        total_ref[...] = now_ref[...].astype(F32)

    def norm(gain, shift):
        whitened, _ = norm_stats(now_ref[...].astype(F32))
        acc_ref[...] = jnp.zeros_like(acc_ref)
        normed_ref[...] = (whitened * gain + shift).astype(BF16)

    def add_branch(out, scale):
        branch = scale * out * live_ref[...]
        now_ref[...] = (now_ref[...].astype(F32) + branch).astype(BF16)
        total_ref[...] += branch

    @pl.when(phase == 0)
    def _():
        cross_ref[IN_ATT] = now_ref[...]
        norm(gain_ref[own], shift_ref[own])
        cross_ref[OUT_FEED] = jnp.zeros((m, D), BF16)
        for n in range(images):
            rows = slice(RP * n, RP * n + ROWS)
            out = cot_ref[n].astype(F32) * fscale_ref[LAYERS - 1 : LAYERS] * live_ref[rows]
            cross_ref[OUT_FEED, rows] = out.astype(BF16)

    @pl.when(phase < steps)
    def _():
        normed = normed_ref[...]
        here = lanes_of(phase, QUAD * HEAD)
        q_ref[...] = ((dot(normed, wq_ref[...]) + qb_ref[own, here]) * 0.125).astype(BF16)
        k_ref[0:m] = dot(normed, wk_ref[...]).astype(BF16)
        v_ref[0:m] = (dot(normed, wv_ref[...]) + vb_ref[own, here]).astype(BF16)
        k_ref[m:] = jnp.zeros_like(k_ref[m:])
        v_ref[m:] = jnp.zeros_like(v_ref[m:])
        masks = head_masks()
        head = layer * HEADS + phase * QUAD
        cells = [(n, h) for n in range(images) for h in range(QUAD)]
        for at, (n, h) in enumerate(cells):
            lanes = slice(128 * (h // 2), 128 * (h // 2) + 128)
            qn = q_ref[RP * n : RP * n + RP, lanes] * masks[h % 2]
            scores_ref[at] = dot(qn, k_ref[RP * n : RP * n + CP, lanes], NT)
        for n in range(images):
            bases = [[diagonal_base(rows_ref[2 * n + i, pl.ds(head + h, 1), :]) for i in range(2)] for h in range(QUAD)]
            for turn, blocks in row_blocks():
                pairs = [[turned_pair(base, turn) for base in each] for each in bases]
                for row, tiles in blocks:
                    above = (upper_ref[n, row : row + 16] > 0.0)[None]
                    first, second = (
                        jnp.stack([diagonal_block(each[i], tiles) for each in pairs]) for i in range(2)
                    )
                    bias = jnp.where(above, first, second) + mask_ref[n]
                    scores_ref[QUAD * n : QUAD * n + QUAD, row : row + 16] += bias
        for n in range(images):
            for row in range(0, RP, 16):
                scores = scores_ref[QUAD * n : QUAD * n + QUAD, row : row + 16]
                power = jnp.exp(scores - jnp.max(scores, axis=2, keepdims=True))
                weights = power * (1.0 / jnp.sum(power, axis=2, keepdims=True))
                w_ref[n, :, row : row + 16] = weights.astype(BF16)
        for n in range(images):
            for pair in range(QUAD // 2):
                lanes = slice(128 * pair, 128 * pair + 128)
                vn = v_ref[RP * n : RP * n + CP, lanes]
                attended = dot(w_ref[n, 2 * pair], vn * masks[0]) + dot(w_ref[n, 2 * pair + 1], vn * masks[1])
                att_ref[RP * n : RP * n + RP, lanes] = attended.astype(BF16)
        acc_ref[...] += dot(att_ref[...], wo_ref[...])
        cross_ref[ATTENDED, :, here] = att_ref[...]

    @pl.when(phase == steps - 1)
    def _():
        out = acc_ref[...] + ob_ref[own]
        branch_att_ref[...] = out.astype(BF16)
        add_branch(out, scale_ref[own])
        cross_ref[IN_FEED] = now_ref[...]

    @pl.when(phase == steps)
    def _():
        norm(fgain_ref[own], fshift_ref[own])

    @pl.when(phase >= steps)
    def _():
        at = phase - steps
        bias = hb_ref[own, lanes_of(order_ref[at], FF // sections)]
        spans = [slice(RP * n, RP * n + RP) for n in range(images)]
        hiddens = [dot(normed_ref[rows], wh_ref[...]) + bias for rows in spans]
        actives = []
        for rows, hidden in zip(spans, hiddens):
            share = 0.5 * (1.0 + lax.erf(hidden * 0.7071067811865476))
            actives.append((hidden * share).astype(BF16))
            bell = jnp.exp(-0.5 * hidden * hidden) * 0.3989422804014327
            slope_ref[rows] = (share + hidden * bell).astype(BF16)
        for rows, active in zip(spans, actives):
            acc_ref[rows] += dot(active, wr_ref[...])

        @pl.when(at < sections // 2)
        def _():
            for rows, active in zip(spans, actives):
                cross_ref[ACTIVE + at, rows] = active

        @pl.when(at >= sections // 2)
        def _():
            for rows, active in zip(spans, actives):
                active_ref[rows] = active

    @pl.when(phase == per - 1)
    def _():
        out = acc_ref[...] + rb_ref[own]
        branch_feed_ref[...] = out.astype(BF16)
        add_branch(out, fscale_ref[own])

    @pl.when(t == pl.num_programs(0) - 1)
    def _():
        send_pieces(me_ref[0], images, total_ref, piece_refs)


def send_pieces(me, images, rows_ref, piece_refs):
    sections = len(piece_refs)
    width = D // sections
    turned = [rows_ref[RP * n : RP * n + RP].T for n in range(images)]
    for own in range(sections):

        @pl.when(me == own)
        def _():
            for distance, piece in enumerate(piece_refs):
                at = width * (own ^ distance)
                for n in range(images):
                    piece[n] = turned[n][at : at + width, :ROWS].astype(BF16)


def pieces_shape(images, sections):
    return [jax.ShapeDtypeStruct((images, D // sections, ROWS), BF16)] * sections


def forward(images, sections, me, order, tokens, cotangent, w, tables):
    m = images * RP
    mc = (images - 1) * RP + CP
    wide = QUAD * HEAD
    steps = HEADS // QUAD
    per = steps + sections
    deep = FF // sections
    half = sections // 2
    layer = lambda t: t // per
    phase = lambda t: lax.rem(t, per)

    def att_at(t):
        inside = phase(t) < steps
        more = layer(t) + 1 < LAYERS
        l = jnp.where(inside, layer(t), jnp.minimum(layer(t) + 1, LAYERS - 1))
        return l, jnp.where(inside, phase(t), jnp.where(more, 0, steps - 1))

    def feed_at(t):
        return layer(t), jnp.maximum(phase(t) - steps, 0)

    def third(which):
        def index(t, *_):
            l, g = att_at(t)
            return l, 0, which * steps + g

        return pl.BlockSpec((None, D, wide), index)

    def att_in(block, place):
        return pl.BlockSpec(block, lambda t, *_: place(*att_at(t)))

    def feed_in(block, place):
        return pl.BlockSpec(block, lambda t, me, order: place(layer(t), order[feed_at(t)[1]]))

    def att_out(block, place):
        return pl.BlockSpec(block, lambda t, *_: place(layer(t), jnp.minimum(phase(t), steps - 1)))

    per_layer = lambda *block: pl.BlockSpec((None,) + block, lambda t, *_: (layer(t),) + (0,) * len(block))
    row = whole(LAYERS, D)
    mine = pl.BlockSpec((images, ROWS, D), lambda t, me, order: (me[0], 0, 0))
    shape = lambda *s, dtype=BF16: jax.ShapeDtypeStruct(s, dtype)
    results = run(
        functools.partial(forward_kernel, images, steps, sections),
        grid=(LAYERS * per,),
        prefetch=[me, order],
        in_specs=[
            mine, mine, row, row, third(0), third(1), third(2), row, row,
            whole(2 * images, LAYERS * HEADS, SPAN),
            att_in((None, wide, D), lambda l, g: (l, g, 0)),
            row, row, row, row,
            feed_in((None, D, deep), lambda l, f: (l, 0, f)),
            whole(LAYERS, FF),
            feed_in((None, deep, D), lambda l, f: (l, f, 0)),
            row, row, whole(m, 1), whole(images, 1, CP), whole(images, RP, CP),
        ],
        out_specs=[
            per_layer(ACTIVE + half, m, D),
            pl.BlockSpec((None, None, m, deep), lambda t, *_: (layer(t), jnp.maximum(feed_at(t)[1] - half, 0), 0, 0)),
            att_out((None, m, wide), lambda l, g: (l, 0, g)),
            att_out((None, mc, wide), lambda l, g: (l, 0, g)),
            att_out((None, mc, wide), lambda l, g: (l, 0, g)),
            att_out((None, images, QUAD, RP, CP), lambda l, g: (l, 0, g, 0, 0)),
            per_layer(m, D),
            pl.BlockSpec((None, None, m, deep), lambda t, *_: feed_at(t) + (0, 0)),
            per_layer(m, D),
        ]
        + [whole(images, D // sections, ROWS)] * sections,
        out_shape=[
            shape(LAYERS, ACTIVE + half, m, D), shape(LAYERS, half, m, deep),
            shape(LAYERS, m, D), shape(LAYERS, mc, D), shape(LAYERS, mc, D), shape(LAYERS, images, HEADS, RP, CP),
            shape(LAYERS, m, D), shape(LAYERS, sections, m, deep), shape(LAYERS, m, D),
        ]
        + pieces_shape(images, sections),
        scratch=[
            pltpu.VMEM((m, D), BF16), pltpu.VMEM((m, D), F32), pltpu.VMEM((m, D), F32),
            pltpu.VMEM((images * QUAD, RP, CP), F32), pltpu.VMEM((m, D), BF16), pltpu.VMEM((m, wide), BF16),
        ],
        name="forward",
        operands=[
            tokens, cotangent, w.attention_gain, w.attention_shift, w.input_projection, w.input_projection,
            w.input_projection, w.query_bias, w.value_bias, tables.rows, w.output_projection,
            w.output_bias, w.attention_scale, w.forward_gain, w.forward_shift, w.hidden_weight,
            w.hidden_bias, w.return_weight, w.return_bias, w.forward_scale, tables.live,
            tables.mask, tables.upper,
        ],
    )
    return results[0], Kept(*results[1:-sections]), results[-sections:]


def layer_block(layer, *block):
    return pl.BlockSpec((None,) + block, lambda *_: (layer,) + (0,) * len(block))


def feed_steps(step, steps, gain, bg_rows, out_ref, u_ref, live_ref, branch_ref, slope_ref, wh_ref, wr_ref,
               next_ref, small_ref, hb_ref, send_ref, keep_ref, ng_ref):
    @pl.when(step == 0)
    def _():
        ng_ref[...] = jnp.zeros_like(ng_ref)

    grad = dot(out_ref[...], wr_ref[...], NT) * slope_ref[...].astype(F32)
    grad = grad.astype(BF16)
    hb_ref[...] = column_sum(grad.astype(F32))
    ng_ref[...] += dot(grad, wh_ref[...], NT)

    @pl.when(step < steps // 2)
    def _():
        send_ref[jnp.minimum(step, steps // 2 - 1)] = grad

    @pl.when(step >= steps // 2)
    def _():
        keep_ref[...] = grad

    @pl.when(step == steps - 1)
    def _():
        bg_rows()
        bg = next_ref[...]
        whitened, inverse = norm_stats(u_ref[...].astype(F32))
        ng = ng_ref[...]
        small_ref[...] = jnp.zeros_like(small_ref)
        small_ref[0:1] = column_sum(ng * whitened)
        small_ref[1:2] = column_sum(ng)
        small_ref[2:3] = column_sum(out_ref[...].astype(F32))
        small_ref[3:4] = column_sum(bg * branch_ref[...].astype(F32) * live_ref[...])
        next_ref[...] = bg + norm_back(ng, whitened, inverse, gain)


def first_chain_kernel(images, me_ref, order_ref, cot_ref, out_ref, u_ref, gain_ref, live_ref, branch_ref, slope_ref,
                       wh_ref, wr_ref, next_ref, small_ref, hb_ref, keep_ref, send_ref, ng_ref):
    def bg_rows():
        next_ref[...] = jnp.zeros_like(next_ref)
        for n in range(images):
            next_ref[RP * n : RP * n + ROWS] = cot_ref[n].astype(F32)

    feed_steps(
        pl.program_id(0), pl.num_programs(0), gain_ref[LAYERS - 1 : LAYERS], bg_rows, out_ref, u_ref, live_ref,
        branch_ref, slope_ref, wh_ref, wr_ref, next_ref, small_ref, hb_ref, send_ref, keep_ref, ng_ref,
    )


def slot(layer, index, m):
    return pl.BlockSpec((None, None, m, D), lambda *_: (layer, index, 0, 0))


def first_chain(images, sections, me, order, cotangent, cross, kept, w, tables):
    layer = LAYERS - 1
    m = images * RP
    wide = FF // sections
    sends = sections // 2
    shape = jax.ShapeDtypeStruct
    return run(
        functools.partial(first_chain_kernel, images),
        grid=(sections,),
        in_specs=[
            pl.BlockSpec((images, ROWS, D), lambda i, me, order: (me[0], 0, 0)),
            slot(layer, OUT_FEED, m), slot(layer, IN_FEED, m), whole(LAYERS, D), whole(m, 1), layer_block(layer, m, D),
            pl.BlockSpec((None, None, m, wide), lambda i, me, order: (layer, i, 0, 0)),
            pl.BlockSpec((None, D, wide), lambda i, me, order: (layer, 0, order[i])),
            pl.BlockSpec((None, wide, D), lambda i, me, order: (layer, order[i], 0)),
        ],
        out_specs=[
            whole(m, D), whole(8, D),
            pl.BlockSpec((None, 1, wide), lambda i, *_: (i, 0, 0)),
            pl.BlockSpec((None, m, wide), lambda i, *_: (jnp.maximum(i - sends, 0), 0, 0)),
            whole(sends, m, wide),
        ],
        out_shape=[
            shape((m, D), F32), shape((8, D), F32), shape((sections, 1, wide), F32), shape((sends, m, wide), BF16),
            shape((sends, m, wide), BF16),
        ],
        scratch=[pltpu.VMEM((m, D), F32)],
        prefetch=[me, order],
        operands=[
            cotangent, cross, cross, w.forward_gain, tables.live, kept.branch_feed, kept.slope, w.hidden_weight,
            w.return_weight,
        ],
        name="first_chain",
    )


def by_first_bit(total, own, send_ref, keep_ref):
    pairs, rows, width = keep_ref.shape
    blocks = total.astype(BF16).reshape(pairs, 2, rows, width)
    even, odd = blocks[:, 0], blocks[:, 1]

    @pl.when(own == 0)
    def _():
        keep_ref[...] = even
        send_ref[...] = odd

    @pl.when(own == 1)
    def _():
        keep_ref[...] = odd
        send_ref[...] = even


def store_halves(totals, own, a_send_ref, a_keep_ref, b_send_ref, b_keep_ref):
    last = pl.program_id(0) == pl.num_programs(0) - 1
    for j, total in enumerate(totals):
        half = total.shape[1] // 2
        left = total[:, :half].astype(BF16)

        @pl.when(last)
        def _():
            a_keep_ref[j] = left

        @pl.when(jnp.logical_not(last))
        def _():
            a_send_ref[j] = left

        by_first_bit(total[:, half:], own, b_send_ref.at[j], b_keep_ref.at[j])


def halves_out(count, sends, rows):
    half = D // 2
    pairs = D // (2 * rows)
    piece = pl.BlockSpec((count, None, pairs, rows, half), lambda i, *_: (0, i, 0, 0, 0))
    specs = [whole(count, D, half), whole(count, D, half), piece, piece]
    shapes = [jax.ShapeDtypeStruct((count, D, half), BF16)] * 2
    return specs, shapes + [jax.ShapeDtypeStruct((count, sends, pairs, rows, half), BF16)] * 2


def turned_norm(u_ref, gain, shift):
    whitened, _ = norm_stats(u_ref[...].astype(F32))
    return (whitened * gain + shift).astype(BF16).T


def feed_keep_kernel(layer, returned, hidden, own_ref, *refs):
    ins, out_refs, turned_ref = refs[:-5], refs[-5:-1], refs[-1]
    first = pl.program_id(0) == 0
    totals = []
    if returned:
        out_ref, out_got_ref, active_ref, active_got_ref, *ins = ins

        @pl.when(first)
        def _():
            turned_ref[0] = out_ref[...].T
            turned_ref[1] = out_got_ref[...].T

        totals.append(dot(turned_ref[0], active_ref[...]) + dot(turned_ref[1], active_got_ref[...]))
    if hidden:
        u_ref, u_got_ref, gain_ref, shift_ref, hg_ref, hg_got_ref = ins
        at = 2 * returned

        @pl.when(first)
        def _():
            gain, shift = gain_ref[layer : layer + 1], shift_ref[layer : layer + 1]
            turned_ref[at] = turned_norm(u_ref, gain, shift)
            turned_ref[at + 1] = turned_norm(u_got_ref, gain, shift)

        totals.append(dot(turned_ref[at], hg_ref[...]) + dot(turned_ref[at + 1], hg_got_ref[...]))
    store_halves(totals, own_ref[0], *out_refs)


def feed_keep(layer, own, rows, cross, cross_got, kept, w, after, returned=None, hidden=None):
    wide = FF // lax.axis_size(SECTION)
    sends, m = kept.active.shape[1:3]
    count = (returned is not None) + (hidden is not None)
    halves, out_shape = halves_out(count, sends, rows)
    specs, operands = [], []
    if returned:
        specs += [
            *returned[2:],
            pl.BlockSpec((None, None, m, wide), lambda i, own: (layer, i, 0, 0)),
            pl.BlockSpec((None, None, m, wide), lambda i, own: (layer, ACTIVE + i, 0, 0)),
        ]
        operands += [*returned[:2], kept.active, cross_got]
    if hidden:
        block = pl.BlockSpec((None, m, wide), lambda i, own: (i, 0, 0))
        specs += [slot(layer, IN_FEED, m)] * 2 + [whole(LAYERS, D)] * 2 + [block] * 2
        operands += [cross, cross_got, w.forward_gain, w.forward_shift, *hidden]
    return run(
        functools.partial(feed_keep_kernel, layer, returned is not None, hidden is not None),
        grid=(sends,),
        in_specs=specs,
        out_specs=halves,
        out_shape=out_shape,
        scratch=[pltpu.VMEM((2 * count, D, m), BF16)],
        prefetch=[own],
        operands=operands,
        after=after,
        name="feed_keep",
    )


def attention_steps(
    step, images, sections, me, gain, scale, finish, u_ref, bg_ref, live_ref, q_ref, k_ref, v_ref, w_ref, branch_ref,
    wq_ref, wk_ref, wv_ref, wo_ref, next_ref, send_ref, keep_ref, sg_ref, bias_ref, small_ref,
    ng_ref, out_ref, wg_ref, parts_ref,
):
    steps = HEADS // QUAD
    sends = sections // 2

    @pl.when(step == 0)
    def _():
        out_ref[...] = (bg_ref[...] * scale * live_ref[...]).astype(BF16)
        ng_ref[...] = jnp.zeros_like(ng_ref)

    att_grad = dot(out_ref[...], wo_ref[...], NT).astype(BF16)
    masks = head_masks()
    lanes_of = lambda pair: slice(128 * pair, 128 * pair + 128)
    for n in range(images):
        for h in range(QUAD):
            lanes = lanes_of(h // 2)
            chosen = att_grad[RP * n : RP * n + RP, lanes] * masks[h % 2]
            wg_ref[QUAD * n + h] = dot(chosen, v_ref[RP * n : RP * n + CP, lanes], NT)
    for n in range(images):
        for row in range(0, RP, 16):
            probs = w_ref[n, :, row : row + 16].astype(F32)
            product = wg_ref[QUAD * n : QUAD * n + QUAD, row : row + 16] * probs
            grad = product - probs * jnp.sum(product, axis=2, keepdims=True)
            sg_ref[n, :, row : row + 16] = grad.astype(BF16)
    grads = [[], [], []]
    for n in range(images):
        here = [[], [], []]
        for pair in range(QUAD // 2):
            lanes = lanes_of(pair)
            rows = slice(RP * n, RP * n + RP)
            kn, qn, an = k_ref[RP * n : RP * n + CP, lanes], q_ref[rows, lanes], att_grad[rows, lanes]
            one, two = (n, 2 * pair), (n, 2 * pair + 1)
            dq = dot(sg_ref[one], kn * masks[0]) + dot(sg_ref[two], kn * masks[1])
            dk = dot(sg_ref[one], qn * masks[0], TN) + dot(sg_ref[two], qn * masks[1], TN)
            dv = dot(w_ref[n, 2 * pair], an * masks[0], TN) + dot(w_ref[n, 2 * pair + 1], an * masks[1], TN)
            here[0].append((dq.astype(BF16).astype(F32) * 0.125).astype(BF16))
            here[1].append(dk[:RP].astype(BF16))
            here[2].append(dv[:RP].astype(BF16))
        for i in range(3):
            grads[i].append(jnp.concatenate(here[i], axis=1))
    gq, gk, gv = (jnp.concatenate(each, axis=0) for each in grads)
    wide = QUAD * HEAD
    for i, each in enumerate((gq, gk, gv)):
        for g in range(steps):

            @pl.when(step == g)
            def _():
                parts_ref[:, i * D + g * wide : i * D + g * wide + wide] = each
    bias_ref[0] = column_sum(gq.astype(F32))
    bias_ref[1] = column_sum(gv.astype(F32))
    ng_ref[...] += dot(gq, wq_ref[...], NT) + dot(gk, wk_ref[...], NT) + dot(gv, wv_ref[...], NT)

    @pl.when(step == steps - 1)
    def _():
        whitened, inverse = norm_stats(u_ref[...].astype(F32))
        ng = ng_ref[...]
        bg = bg_ref[...]
        next_ref[...] = bg + norm_back(ng, whitened, inverse, gain)
        small_ref[...] = jnp.zeros_like(small_ref)
        small_ref[0:1] = column_sum(ng * whitened)
        small_ref[1:2] = column_sum(ng)
        small_ref[2:3] = column_sum(out_ref[...].astype(F32))
        small_ref[3:4] = column_sum(bg * branch_ref[...].astype(F32) * live_ref[...])
        part, each = 3 * D // sections, D // sections
        for own in range(sections):

            @pl.when(me == own)
            def _():
                for s in range(sections):
                    place = sends - 1 - ((s // 2) ^ (own // 2))
                    target = (keep_ref if s % 2 == own % 2 else send_ref).at[place]
                    target[:, :part] = parts_ref[:, part * s : part * s + part]
                    target[:, part:] = out_ref[:, each * s : each * s + each]
        finish()


def middle_chain_kernel(
    images, sections, me_ref, order_ref, u_ref, bg_ref, gain_ref, scale_ref, fgain_ref, fscale_ref, live_ref, q_ref,
    k_ref, v_ref, w_ref, branch_ref, wq_ref, wk_ref, wv_ref, wo_ref, u_feed_ref, branch_feed_ref, slope_ref,
    wh_ref, wr_ref,
    next_ref, send_ref, keep_ref, sg_ref, bias_ref, small_ref, feed_small_ref, hb_ref, hg_keep_ref, hg_send_ref,
    ng_ref, out_ref, wg_ref, parts_ref,
):
    t = pl.program_id(0)
    steps = HEADS // QUAD
    att, feed = slice(LAYERS - 1, LAYERS), slice(LAYERS - 2, LAYERS - 1)
    out_rows_ref = hg_send_ref.at[sections // 2]

    def finish():
        out_rows_ref[...] = (next_ref[...] * fscale_ref[feed] * live_ref[...]).astype(BF16)

    @pl.when(t < steps)
    def _():
        attention_steps(
            t, images, sections, me_ref[0], gain_ref[att], scale_ref[att], finish, u_ref, bg_ref, live_ref, q_ref, k_ref,
            v_ref, w_ref, branch_ref, wq_ref, wk_ref, wv_ref, wo_ref, next_ref, send_ref, keep_ref, sg_ref,
            bias_ref, small_ref, ng_ref, out_ref, wg_ref, parts_ref,
        )

    @pl.when(t >= steps)
    def _():
        feed_steps(
            t - steps, sections, fgain_ref[feed], lambda: None, out_rows_ref, u_feed_ref, live_ref, branch_feed_ref,
            slope_ref, wh_ref, wr_ref, next_ref, feed_small_ref, hb_ref, hg_send_ref, hg_keep_ref, ng_ref,
        )


def attention_specs(layer, images, at):
    m = images * RP
    mc = (images - 1) * RP + CP
    wide = QUAD * HEAD
    steps = HEADS // QUAD
    block = lambda count: pl.BlockSpec((None, count, wide), lambda t, *_: (layer, 0, at(t)))
    third = lambda which: pl.BlockSpec((None, D, wide), lambda t, *_: (layer, 0, which * steps + at(t)))
    return [
        block(m), block(mc), block(mc),
        pl.BlockSpec((None, images, QUAD, RP, CP), lambda t, *_: (layer, 0, at(t), 0, 0)),
        layer_block(layer, m, D), third(0), third(1), third(2),
        pl.BlockSpec((None, wide, D), lambda t, *_: (layer, at(t), 0)),
    ]


def attention_out(images, sections, at):
    m = images * RP
    sends = sections // 2
    shape = jax.ShapeDtypeStruct
    specs = [
        whole(m, D), whole(sends, m, D), whole(sends, m, D),
        pl.BlockSpec((images, QUAD, RP, CP), lambda t, *_: (0, at(t), 0, 0)),
        pl.BlockSpec((2, 1, QUAD * HEAD), lambda t, *_: (0, 0, at(t))), whole(8, D),
    ]
    shapes = [
        shape((m, D), F32), shape((sends, m, D), BF16), shape((sends, m, D), BF16),
        shape((images, HEADS, RP, CP), BF16), shape((2, 1, D), F32), shape((8, D), F32),
    ]
    return specs, shapes


def attention_scratch(images):
    m = images * RP
    return [
        pltpu.VMEM((m, D), F32), pltpu.VMEM((m, D), BF16), pltpu.VMEM((images * QUAD, RP, CP), F32),
        pltpu.VMEM((m, 3 * D), BF16),
    ]


def attention_operands(kept, w, tables):
    return [
        kept.q, kept.k, kept.v, kept.w, kept.branch_att, w.input_projection, w.input_projection, w.input_projection,
        w.output_projection,
    ]


def middle_chain(images, sections, me, order, bg, cross, kept, w, tables, after):
    m = images * RP
    wide = FF // sections
    sends = sections // 2
    steps = HEADS // QUAD
    late = lambda t: jnp.maximum(t - steps, 0)
    early = lambda t: jnp.minimum(t, steps - 1)
    shape = jax.ShapeDtypeStruct
    out_specs, out_shape = attention_out(images, sections, early)
    return run(
        functools.partial(middle_chain_kernel, images, sections),
        grid=(steps + sections,),
        prefetch=[me, order],
        in_specs=[slot(LAYERS - 1, IN_ATT, m), whole(m, D)] + [whole(LAYERS, D)] * 4 + [whole(m, 1)]
        + attention_specs(LAYERS - 1, images, early)
        + [
            slot(LAYERS - 2, IN_FEED, m), layer_block(LAYERS - 2, m, D),
            pl.BlockSpec((None, None, m, wide), lambda t, me, order: (LAYERS - 2, late(t), 0, 0)),
            pl.BlockSpec((None, D, wide), lambda t, me, order: (LAYERS - 2, 0, order[late(t)])),
            pl.BlockSpec((None, wide, D), lambda t, me, order: (LAYERS - 2, order[late(t)], 0)),
        ],
        out_specs=out_specs + [
            whole(8, D), pl.BlockSpec((None, 1, wide), lambda t, *_: (late(t), 0, 0)),
            pl.BlockSpec((None, m, wide), lambda t, *_: (jnp.maximum(late(t) - sends, 0), 0, 0)),
            whole(sends + 1, m, wide),
        ],
        out_shape=out_shape + [
            shape((8, D), F32), shape((sections, 1, wide), F32), shape((sends, m, wide), BF16),
            shape((sends + 1, m, wide), BF16),
        ],
        scratch=attention_scratch(images),
        operands=[cross, bg, w.attention_gain, w.attention_scale, w.forward_gain, w.forward_scale, tables.live]
        + attention_operands(kept, w, tables)
        + [cross, kept.branch_feed, kept.slope, w.hidden_weight, w.return_weight],
        after=after,
        name="middle_chain",
    )


def last_chain_kernel(images, sections, me_ref, u_ref, bg_ref, gain_ref, scale_ref, live_ref, *refs):
    first = 9 + sections
    ins, early_refs, outs, piece_refs, scratch = (
        refs[:9], refs[9:first], refs[first : first + 6], refs[first + 6 : first + 6 + sections], refs[-4:]
    )
    next_ref = outs[0]

    def finish():
        for early_ref, piece_ref in zip(early_refs, piece_refs):
            piece_ref[0] = early_ref[...]
        send_pieces(me_ref[0], images, next_ref, [piece.at[1] for piece in piece_refs])

    attention_steps(
        pl.program_id(0), images, sections, me_ref[0], gain_ref[0:1], scale_ref[0:1], finish, u_ref, bg_ref, live_ref,
        *ins, *outs, *scratch,
    )


def last_chain(images, sections, me, bg, cross, kept, w, tables, after, early):
    m = images * RP
    at = lambda t: t
    out_specs, out_shape = attention_out(images, sections, at)
    return run(
        functools.partial(last_chain_kernel, images, sections),
        grid=(HEADS // QUAD,),
        prefetch=[me],
        in_specs=[slot(0, IN_ATT, m), whole(m, D)] + [whole(LAYERS, D)] * 2 + [whole(m, 1)]
        + attention_specs(0, images, at) + [whole(*piece.shape) for piece in early],
        out_specs=out_specs + [whole(2, *piece.shape) for piece in early],
        out_shape=out_shape + [jax.ShapeDtypeStruct((2,) + piece.shape, BF16) for piece in early],
        scratch=attention_scratch(images),
        operands=[cross, bg, w.attention_gain, w.attention_scale, tables.live, *attention_operands(kept, w, tables), *early],
        after=after,
        name="last_chain",
    )


def table_rows_kernel(images, sg_ref, upper_ref, rows_ref):
    for n in range(images):
        for h in range(QUAD):
            sums = [None, None]
            for g in range(0, 16, 2):
                blocks = [(g, 0)] + ([(g + 16, 1)] if 8 * (g + 16) < RP else [])
                loaded = {}
                for start, _ in blocks:
                    both = sg_ref[n, h, 8 * start : 8 * start + 16].astype(F32)
                    above = jnp.where(upper_ref[n, 8 * start : 8 * start + 16] > 0.0, both, 0.0)
                    loaded[start] = (above, both - above)
                for u in range(2):
                    for i in range(2):
                        cut = lambda s, k: loaded[s][u][8 * i : 8 * i + 8, 128 * k : 128 * k + 128]
                        zero = jnp.zeros((8, 128), F32)
                        tiles = [cut(g, 0), cut(g, 1), zero, zero]
                        if len(blocks) > 1:
                            tiles = [tiles[0] + cut(g + 16, 1), tiles[1], zero, cut(g + 16, 0)]
                        block = jnp.concatenate(tiles, axis=1)
                        if g + i:
                            block = pltpu.roll(block, SPAN - 8 * (g + i), 1)
                        sums[u] = block if sums[u] is None else sums[u] + block
            for u in range(2):
                rows_ref[2 * n + u, pl.ds(pl.program_id(0) * QUAD + h, 1)] = straighten(sums[u])


def table_rows(images, sg, tables, after):
    shape = (2 * images, HEADS, SPAN)
    return run(
        functools.partial(table_rows_kernel, images),
        grid=(HEADS // QUAD,),
        in_specs=[pl.BlockSpec((images, QUAD, RP, CP), lambda g: (0, g, 0, 0)), whole(images, RP, CP)],
        out_specs=[whole(*shape)],
        out_shape=[jax.ShapeDtypeStruct(shape, F32)],
        operands=[sg, tables.upper],
        after=after,
        name="table_rows",
    )[0]


def attention_product(nt, at, grads):
    first = 3 * D // (4 * 128) * 128
    low = lax.broadcasted_iota(jnp.int32, (1, 128), 1) < HEAD
    left = dot(nt, grads[:, : first + 128])
    right = dot(at, grads[:, first:])
    middle = jnp.where(low, left[:, first:], right[:, :128])
    return jnp.concatenate([left[:, :first], middle, right[:, 128:]], axis=1)


def attention_keep_kernel(layer, own_ref, u_ref, u_got_ref, att_ref, att_got_ref, gain_ref, shift_ref, grads_ref, *refs):
    got_ref, out_refs, (nt_ref, at_ref) = refs[0], refs[1:5], refs[5:]

    @pl.when(pl.program_id(0) == 0)
    def _():
        gain, shift = gain_ref[layer : layer + 1], shift_ref[layer : layer + 1]
        for i, (u, att) in enumerate(((u_ref, att_ref), (u_got_ref, att_got_ref))):
            nt_ref[i] = turned_norm(u, gain, shift)
            at_ref[i] = att[...].T

    total = attention_product(nt_ref[0], at_ref[0], grads_ref[...])
    total += attention_product(nt_ref[1], at_ref[1], got_ref[...])
    store_halves([total], own_ref[0], *out_refs)


def attention_keep(layer, own, rows, cross, cross_got, grads, got, w, after):
    sends, m, _ = grads.shape
    out_specs, out_shape = halves_out(1, sends, rows)
    return run(
        functools.partial(attention_keep_kernel, layer),
        grid=(sends,),
        in_specs=[
            slot(layer, IN_ATT, m), slot(layer, IN_ATT, m), slot(layer, ATTENDED, m), slot(layer, ATTENDED, m),
            whole(LAYERS, D), whole(LAYERS, D),
        ] + [pl.BlockSpec((None, m, D), lambda i, own: (i, 0, 0))] * 2,
        out_specs=out_specs,
        out_shape=out_shape,
        scratch=[pltpu.VMEM((2, D, m), BF16), pltpu.VMEM((2, D, m), BF16)],
        prefetch=[own],
        operands=[cross, cross_got, cross, cross_got, w.attention_gain, w.attention_shift, grads, got],
        after=after,
        name="attention_keep",
    )


def flip(value, axis, bit):
    count = lax.axis_size(axis)
    return lax.ppermute(value, axis, [(i, i ^ bit) for i in range(count)])


def wide_names():
    return [(WIDE, 1 << i) for i in reversed(range(lax.axis_size(WIDE).bit_length() - 1))]


def own_bit(axis, bit):
    return (lax.axis_index(axis) // bit) % 2


ACROSS = (SECTION, 2)


class Chunk:
    def __init__(self, keep, received, lead, names, order, rows):
        self.width = keep.shape[-1]
        self.rows = rows
        shape = keep.shape[:1] + (2,) * len(names) + (rows, self.width)
        self.terms = [(array.reshape(shape), lead, tuple(names)) for array in (keep, received)]
        self.left = tuple(names)
        self.done = ()
        self.order = list(order)

    def arrived(self):
        return [self.terms[-1][0]]


class Small:
    def __init__(self, keep, received):
        self.terms = [keep, received]
        self.order = [ACROSS] + list(reversed(wide_names()))


def combine(groups, mine, after, name, writer=None, out_shape=None, small=None, held=()):
    all_names = wide_names()
    specs, operands, counts, out_specs, shapes = [], [], [], [], []
    rows = groups[0][0].rows if groups else 0
    split = 2 if rows % 32 == 0 and writer is None else 1
    rows = rows // split
    for group in groups:
        for chunk in group:
            stage = None if writer else chunk.order[0]
            for array, lead, names in chunk.terms:
                fixed = [n in chunk.done or n == stage for n in names]
                block = (None,) + tuple(None if f else 2 for f in fixed) + (rows, chunk.width)

                def index(i, mine_ref, lead=lead, names=names, fixed=fixed, stage=stage):
                    at = []
                    for n, f in zip(names, fixed):
                        own = 1 if n == ACROSS else mine_ref[all_names.index(n)]
                        at.append((1 - own if n == stage else own) if f else 0)
                    return (lead, *at, i, 0)

                specs.append(pl.BlockSpec(block, index))
                operands.append(array)
            counts.append(len(chunk.terms))
        if writer is None:
            chunk = group[0]
            dims = (len(group),) + (2,) * (len(chunk.left) - 1)
            shapes.append(jax.ShapeDtypeStruct(dims + (chunk.rows, chunk.width), BF16))
            out_specs.append(
                pl.BlockSpec(dims + (rows, chunk.width), lambda i, mine_ref, n=len(dims): (0,) * n + (i, 0))
            )
    if writer:
        shapes = out_shape
        out_specs = [whole(*s.shape) for s in shapes]

    if small:
        specs += [whole(*term.shape) for term in small.terms]
        operands += small.terms
        shape = small.terms[0].shape[-2:]
        shapes += [jax.ShapeDtypeStruct(shape, F32)] * (1 + (small.order[0] == ACROSS))
        out_specs += [whole(*shape)] * (len(shapes) - len(out_specs))

    def kernel(mine_ref, *refs):
        ins, outs = refs[: len(operands)], refs[len(operands) :]
        if small:
            value = ins[-2][...] + ins[-1][...]
            if small.order[0] == ACROSS:
                outs[-2][...], outs[-1][...] = value[0], value[1]
            else:
                outs[-1][...] = value
        totals, at = [], 0
        for count in counts:
            total = ins[at][...].astype(F32)
            for ref in ins[at + 1 : at + count]:
                total = total + ref[...].astype(F32)
            totals.append(total)
            at += count
        if writer:
            writer(outs, totals)
            return
        for group, out in zip(groups, outs):
            for j in range(len(group)):
                out[j] = totals.pop(0).astype(BF16)

    results = run(
        kernel, grid=(split,), in_specs=specs, out_specs=out_specs, out_shape=shapes,
        prefetch=[mine], operands=operands, after=list(after), held=held, name=name,
    )
    if writer:
        return results
    held_count = len(held)
    results, held = results[: len(results) - held_count], results[len(results) - held_count :]
    if small:
        stage = small.order[0]
        small.order = small.order[1:]
        small.terms = [results[-1], flip(results[-2] if stage == ACROSS else results[-1], *stage)]
    for group, sent in zip(groups, results):
        stage = group[0].order[0]
        got = flip(sent, *stage)
        for j, chunk in enumerate(group):
            chunk.order = chunk.order[1:]
            chunk.done = chunk.done + (stage,)
            chunk.left = tuple(n for n in chunk.left if n != stage)
            chunk.terms = chunk.terms + [(got, j, chunk.left)]
    return (results, held) if held else results


def pack_kernel(sections, me_ref, index_ref, rows0_ref, rows1_ref, a0_ref, a1_ref, f0_ref, f1_ref, b0_ref, b1_ref,
                h0_ref, h1_ref, send_ref, keep_ref, sum_ref):
    step = pl.program_id(0)

    @pl.when(step == 0)
    def _():
        sum_ref[...] = jnp.zeros_like(sum_ref)

    chosen = (lax.broadcasted_iota(jnp.int32, (TABLE, SPAN), 0) == index_ref[...]).astype(F32).astype(BF16)
    rows = jnp.concatenate([rows0_ref[...], rows1_ref[...]], axis=0)
    high = rows.astype(BF16)
    low = (rows - high.astype(F32)).astype(BF16)
    sum_ref[...] += dot(high, chosen, NT) + dot(low, chosen, NT)
    each = D // sections
    heads = HEADS // sections
    sends = sections // 2
    tiles = TABLE // 256
    layers = ((a0_ref, f0_ref, b0_ref, h0_ref), (a1_ref, f1_ref, b1_ref, h1_ref))

    def fill(own):
        for s in range(sections):
            place = sends - 1 - ((s // 2) ^ (own // 2))
            ref = (keep_ref if s % 2 == own % 2 else send_ref).at[place]
            lanes = slice(each * s, each * s + each)
            for layer, (a_ref, f_ref, b_ref, h_ref) in enumerate(layers):
                at = layer * SMALL
                ref[at : at + 4, 0:each] = a_ref[0:4, lanes]
                ref[at + 4 : at + 8, 0:each] = f_ref[0:4, lanes]
                for i in range(2):
                    ref[at + 8 + i : at + 9 + i, 0:each] = b_ref[i, :, lanes]
                where = place + (sends if s % 2 == own % 2 else 0)
                for j in range(FF // sections // 256):
                    ref[at + 10 + j : at + 11 + j] = h_ref[where, :, 256 * j : 256 * j + 256]
                for k in range(heads):
                    row = layer * HEADS + s * heads + k
                    for j in range(tiles):
                        to = at + 13 + k * tiles + j
                        ref[to : to + 1] = sum_ref[row : row + 1, 256 * j : 256 * j + 256]

    @pl.when(step == pl.num_programs(0) - 1)
    def _():
        send_ref[...] = jnp.zeros_like(send_ref)
        keep_ref[...] = jnp.zeros_like(keep_ref)
        for own in range(sections):
            pl.when(me_ref[0] == own)(functools.partial(fill, own))


def pack(me, sections, index, rows, att, feed, bias, hidden, after):
    places = index.shape[0]
    row = pl.BlockSpec((None, HEADS, SPAN), lambda i, me: (i, 0, 0))
    hidden_wide = FF // sections
    shape = (sections // 2, LAYERS * SMALL, 256)
    return run(
        functools.partial(pack_kernel, sections),
        grid=(places,),
        prefetch=[me],
        in_specs=[pl.BlockSpec((None, 1, SPAN), lambda i, me: (i, 0, 0)), row, row]
        + [whole(8, D)] * 4 + [whole(2, 1, D)] * 2 + [whole(sections, 1, hidden_wide)] * 2,
        out_specs=[whole(*shape)] * 2,
        out_shape=[jax.ShapeDtypeStruct(shape, F32)] * 2,
        scratch=[pltpu.VMEM((LAYERS * HEADS, TABLE), F32)],
        operands=[index, *rows, *att, *feed, *bias, *hidden],
        after=after,
        name="pack",
    )


def unpack_kernel(keep_ref, got_ref, *out_refs):
    *vector_refs, hidden_ref, table_ref, small_ref = out_refs
    small_ref[...] = keep_ref[...] + got_ref[...]
    each = vector_refs[0].shape[1]
    heads = table_ref.shape[0]
    tiles = TABLE // 256
    for layer in range(LAYERS):
        at = layer * SMALL
        for i, ref in enumerate(vector_refs):
            ref[layer : layer + 1] = small_ref[at + i : at + i + 1, 0:each]
        for j in range(hidden_ref.shape[1] // 256):
            hidden_ref[layer : layer + 1, 256 * j : 256 * j + 256] = small_ref[at + 10 + j : at + 11 + j]
        for k in range(heads):
            row = at + 13 + k * tiles
            line = jnp.concatenate([small_ref[r : r + 1] for r in range(row, row + tiles)], axis=1)
            table_ref[k, layer : layer + 1] = line[:, :REL]


def unpack(small, sections, after):
    shape = jax.ShapeDtypeStruct
    out_shape = [shape((LAYERS, D // sections), F32)] * 10
    out_shape += [shape((LAYERS, FF // sections), F32), shape((HEADS // sections, LAYERS, REL), F32)]
    return run(
        unpack_kernel, grid=(1,), in_specs=[whole(LAYERS * SMALL, 256)] * 2, out_specs=[whole(*s.shape) for s in out_shape],
        out_shape=out_shape, operands=small.terms, scratch=[pltpu.VMEM((LAYERS * SMALL, 256), F32)], after=after,
        name="unpack",
    )


def assemble_kernel(me_ref, *refs):
    *piece_refs, output_ref, grad_ref = refs
    images = piece_refs[0].shape[1]
    for distance, piece in enumerate(piece_refs):
        rows = pl.ds((me_ref[0] ^ distance) * images, images)
        output_ref[rows] = piece[0]
        grad_ref[rows] = piece[1]


def assemble(me, pieces, after):
    sections = len(pieces)
    _, images, width, rows = pieces[0].shape
    shape = (sections * images, width, rows)
    return run(
        assemble_kernel, grid=(1,), prefetch=[me], in_specs=[whole(*pieces[0].shape)] * sections,
        out_specs=[whole(*shape)] * 2, out_shape=[jax.ShapeDtypeStruct(shape, BF16)] * 2,
        operands=pieces, after=after, name="assemble",
    )


def on_device(
    tokens, cotangent, patch_grids, attention_gain, attention_shift, input_projection, query_bias, value_bias,
    relative_table, output_projection, output_bias, attention_scale, forward_gain, forward_shift, hidden_weight,
    hidden_bias, return_weight, return_bias, forward_scale,
):
    sections = lax.axis_size(SECTION)
    me = lax.axis_index(SECTION).astype(jnp.int32)
    me_row = me.reshape(1)
    images = tokens.shape[0] // sections
    m = images * RP
    rows = D // lax.axis_size(WIDE)
    w = Weights(
        attention_gain, attention_shift, input_projection, query_bias, value_bias, output_projection, output_bias,
        attention_scale, forward_gain, forward_shift, hidden_weight, hidden_bias, return_weight, return_bias,
        forward_scale,
    )
    grids = lax.dynamic_slice_in_dim(patch_grids, me * images, images, 0)
    height, width = grids[:, 0:1], grids[:, 1:2]
    place = lax.broadcasted_iota(jnp.int32, (images, CP), 1)
    live = place < height * width
    column = place % width
    turn = lax.broadcasted_iota(jnp.int32, (images, SPAN), 1)
    gap = jnp.where(turn < CP, -turn, SPAN - turn)
    b = jnp.mod(gap, width)
    a = (gap - b) // width
    entry = lambda p, q: jnp.clip(p + HMAX - 1, 0, 2 * HMAX - 2) * QW + jnp.clip(q + WMAX - 1, 0, QW - 1)
    index = jnp.stack([entry(a, b), entry(a + 1, b - width)], axis=1).reshape(2 * images, 1, SPAN)
    table = jnp.transpose(relative_table, (0, 2, 1)).reshape(LAYERS * HEADS, REL)
    table = jnp.pad(table, ((0, 0), (0, TABLE - REL)))
    tables = Tables(
        live[:, :RP].reshape(m, 1).astype(F32),
        jnp.where(live, 0.0, -1e9).astype(F32).reshape(images, 1, CP),
        (column[:, :RP, None] >= column[:, None, :]).astype(F32),
        bias_rows(table, index),
    )
    high, core = me // 2, me % 2
    order = jnp.stack([2 * (1 - high) + 1 - core, 2 * high + 1 - core, 2 * (1 - high) + core, 2 * high + core])
    cross, kept, pieces = forward(images, sections, me_row, order, tokens, cotangent, w, tables)

    names = wide_names()
    mine_bits = jnp.stack([own_bit(*name) for name in names]).astype(jnp.int32)
    own = own_bit(WIDE, 1).astype(jnp.int32).reshape(1)
    first = names[-1]
    core_flip = lambda sent: flip(sent, SECTION, 1)

    def launch(a_send, a_keep, b_send, b_keep):
        a_got, b_got = flip(a_send, *ACROSS), flip(b_send, *first)
        across = [ACROSS] + names[:-1]
        chunks = []
        for j in range(a_keep.shape[0]):
            chunks.append((
                Chunk(a_keep, a_got, j, names, list(reversed(names)), rows),
                Chunk(b_keep, b_got, j, across, [ACROSS] + list(reversed(names[:-1])), rows),
            ))
        left, right = zip(*chunks)
        return list(left), list(right), [a_got, b_got]

    def step(groups, after, name, small=None, held=()):
        return combine(groups, mine_bits, after, name, small=small, held=held)

    def finish(groups, after, name, writer, out_shape):
        while any(group[0].order for group in groups):
            after = step([group for group in groups if group[0].order], after, name)
        return combine(groups, mine_bits, after, name, writer, out_shape)

    cross_got = core_flip(cross)
    spec = slot(1, OUT_FEED, m)
    bg, feed_small1, hidden1, hg, sent = first_chain(images, sections, me_row, order, cotangent, cross, kept, w, tables)
    out = feed_keep(
        1, own, rows, cross, cross_got, kept, w, [bg], returned=(cross, cross_got, spec, spec),
        hidden=(hg, core_flip(sent)),
    )
    a1, b1, launched = launch(*out)
    bg, grads_sent, grads, sg1, *small1, feed_small0, hidden0, hg, sent = middle_chain(
        images, sections, me_row, order, bg, cross, kept, w, tables, out[1:2]
    )
    grads_sent, sent = hold([grads_sent, sent], [bg, *launched])
    grads_got = core_flip(grads_sent)
    sent_got = core_flip(sent)
    last = step([a1, b1], [grads_sent], "second")
    spec = pl.BlockSpec((None, m, D), lambda *_: (sections // 2, 0, 0))
    out = feed_keep(
        0, own, rows, cross, cross_got, kept, w, last, returned=(sent, sent_got, spec, spec), hidden=(hg, sent_got)
    )
    a0, b0, _ = launch(*out)
    last = step([a1 + b1], [*out[1:2], grads_got], "third")
    a_send, a_keep, b_send, b_keep = attention_keep(1, own, rows, cross, cross_got, grads, grads_got, w, last)
    pa1, pb1, launched = launch(a_send, a_keep, b_send, b_keep)
    last = [b_keep]
    bg, grads0_sent, grads0, sg0, biases, small0, *pieces = last_chain(
        images, sections, me_row, bg, cross, kept, w, tables, last, pieces
    )
    pieces = [pieces[0]] + [flip(pieces[d], SECTION, d) for d in range(1, sections)]
    rows1 = table_rows(images, sg1, tables, [bg])
    last, (grads0_sent,) = step([a0 + pa1, b0 + pb1, a1 + b1], [rows1], "second", held=[grads0_sent])
    grads0_got = core_flip(grads0_sent)
    (a_keep,) = hold([a_keep], [grads0_got])
    a_send, a_keep, b_send, b_keep = attention_keep(0, own, rows, cross, cross_got, grads0, grads0_got, w, [a_keep])
    rows0 = table_rows(images, sg0, tables, [a_keep])
    last, (a_send, b_send) = step([a0 + b0], [rows0, *a1[0].arrived(), *b1[0].arrived()], "third", held=[a_send, b_send])
    pa0, pb0, _ = launch(a_send, a_keep, b_send, b_keep)
    core_sent, core_kept = pack(
        me_row, sections, index, (rows0, rows1), (small0, small1[1]), (feed_small0, feed_small1),
        (biases, small1[0]), (hidden0, hidden1), last,
    )
    small = Small(core_kept, core_flip(core_sent))
    last = step([a0 + b0, pa1 + pb1], [core_kept], "fourth", small)
    last = step([pa0, pb0], last, "second", small)
    last = step([pa0 + pb0, pa1 + pb1], [*last, *a0[0].arrived()], "third", small)

    def write_feed(outs, totals):
        for layer in range(LAYERS):
            ra, ha, rb, hb = totals[4 * layer : 4 * layer + 4]
            half = D // 2
            outs[0][layer, :, :half] = ha
            outs[0][layer, :, half:] = hb
            outs[1][layer, :, :half] = ra
            outs[1][layer, :, half:] = rb

    def write_attention(outs, totals):
        part = 3 * D // sections
        for layer in range(LAYERS):
            left, right = totals[2 * layer], totals[2 * layer + 1]
            outs[0][layer, :, : D // 2] = left
            outs[0][layer, :, D // 2 :] = right[:, : part - D // 2]
            outs[1][layer] = right[:, part - D // 2 :]

    shape = lambda *s: jax.ShapeDtypeStruct(s, F32)
    wide = FF // sections
    hidden_grad, return_grad = finish(
        [a0 + b0, a1 + b1], last, "last", write_feed, [shape(LAYERS, rows, wide)] * 2
    )
    last = step([pa0 + pb0], [hidden_grad], "fourth", small)
    layer_output, input_grad = assemble(me_row, pieces, last)
    projection_grad, out_grad = finish(
        [pa0 + pb0, pa1 + pb1], [layer_output], "last", write_attention,
        [shape(LAYERS, rows, 3 * D // sections), shape(LAYERS, rows, D // sections)],
    )
    while small.order:
        last = combine([], mine_bits, [], "more", small=small)
    vectors = unpack(small, sections, [out_grad])
    gain, shift, out_shift, scale, fgain, fshift, return_shift, fscale, query, value, hidden_shift, table_grad = vectors
    return (
        jnp.swapaxes(layer_output, 1, 2), jnp.swapaxes(input_grad, 1, 2), gain, shift, projection_grad, query, value, jnp.transpose(table_grad, (1, 2, 0)), out_grad, out_shift, scale,
        fgain, fshift, hidden_grad, hidden_shift, jnp.swapaxes(return_grad, 1, 2), return_shift, fscale,
    )


def solution(mesh):
    three, two = P(WIDE, None, SECTION), P(None, SECTION)
    weight = P(None, WIDE, SECTION)
    return jax.shard_map(
        on_device,
        mesh=mesh,
        in_specs=(P(WIDE, None, None), P(WIDE, None, None), P(WIDE, None)) + (P(),) * 16,
        out_specs=(
            three, three, two, two, weight, two, two, P(None, None, SECTION), weight, two, two, two, two,
            weight, two, P(None, SECTION, WIDE), two, two,
        ),
        check_vma=False,
    )
```

```python
import functools
from typing import NamedTuple

import jax
import jax.numpy as jnp
from jax import lax
from jax.experimental import pallas as pl
from jax.experimental.pallas import tpu as pltpu
from jax.sharding import PartitionSpec as P

SECTION = "section"
WIDE = "wide"
D = 768
HEADS = 12
HEAD = 64
FF = 3072
IN_ATT, IN_FEED, ATTENDED, OUT_FEED, ACTIVE = range(5)
ROWS = 200
HMAX = 14
WMAX = 24
REL = 1269
LAYERS = 2
QW = 2 * WMAX - 1
RP = 208
CP = 256
SPAN = 512
TABLE = 1280
SMALL = 28
QUAD = 4
F32 = jnp.float32
BF16 = jnp.bfloat16
NN = (((1,), (0,)), ((), ()))
NT = (((1,), (1,)), ((), ()))
TN = (((0,), (0,)), ((), ()))
VMEM = 48 * 1024 * 1024


def dot(left, right, dims=NN):
    return lax.dot_general(left, right, dims, preferred_element_type=F32)


def whole(*shape):
    return pl.BlockSpec(shape, lambda *_: (0,) * len(shape))


class Kept(NamedTuple):
    active: jax.Array
    q: jax.Array
    k: jax.Array
    v: jax.Array
    w: jax.Array
    branch_att: jax.Array
    slope: jax.Array
    branch_feed: jax.Array


class Weights(NamedTuple):
    attention_gain: jax.Array
    attention_shift: jax.Array
    input_projection: jax.Array
    query_bias: jax.Array
    value_bias: jax.Array
    output_projection: jax.Array
    output_bias: jax.Array
    attention_scale: jax.Array
    forward_gain: jax.Array
    forward_shift: jax.Array
    hidden_weight: jax.Array
    hidden_bias: jax.Array
    return_weight: jax.Array
    return_bias: jax.Array
    forward_scale: jax.Array


class Tables(NamedTuple):
    live: jax.Array
    mask: jax.Array
    upper: jax.Array
    rows: jax.Array


def run(kernel, *, grid, in_specs, out_specs, out_shape, operands, scratch=(), prefetch=(), after=(), held=(), name):
    first = len(prefetch) + len(in_specs)
    count = len(after) + len(held)
    outs = len(out_shape)

    def body(*refs):
        kept = refs[:first] + refs[first + count : first + count + outs]
        kernel(*kept, *refs[first + count + outs + len(held) :])

    anywhere = pl.BlockSpec(memory_space=pl.ANY)
    return pl.pallas_call(
        body,
        grid_spec=pltpu.PrefetchScalarGridSpec(
            num_scalar_prefetch=len(prefetch),
            grid=grid,
            in_specs=list(in_specs) + [anywhere] * count,
            out_specs=list(out_specs) + [anywhere] * len(held),
            scratch_shapes=list(scratch),
        ),
        out_shape=list(out_shape) + [jax.ShapeDtypeStruct(v.shape, v.dtype) for v in held],
        input_output_aliases={first + len(after) + i: outs + i for i in range(len(held))},
        compiler_params=pltpu.CompilerParams(vmem_limit_bytes=VMEM),
        cost_estimate=pl.CostEstimate(flops=10**6, bytes_accessed=10**5, transcendentals=0),
        name=name,
    )(*prefetch, *operands, *after, *held)


def hold(held, after):
    def kernel(out_ref):
        out_ref[...] = jnp.zeros_like(out_ref)

    tiny = [jax.ShapeDtypeStruct((8, 128), F32)]
    _, *held = run(
        kernel, grid=(1,), in_specs=[], out_specs=[whole(8, 128)], out_shape=tiny, operands=[], after=after, held=held,
        name="hold",
    )
    return held


def norm_stats(u):
    mean = jnp.mean(u, axis=1, keepdims=True)
    centered = u - mean
    inverse = lax.rsqrt(jnp.mean(centered * centered, axis=1, keepdims=True) + 1e-6)
    return centered * inverse, inverse


def norm_back(upstream, whitened, inverse, gain):
    scaled = upstream * gain
    first = jnp.mean(scaled, axis=1, keepdims=True)
    second = jnp.mean(scaled * whitened, axis=1, keepdims=True)
    return (scaled - first - whitened * second) * inverse


def column_sum(v):
    return jnp.sum(v, axis=0, keepdims=True)


def head_masks():
    lane = lax.broadcasted_iota(jnp.int32, (1, 2 * HEAD), 1)
    low = (lane < HEAD).astype(F32)
    return low.astype(BF16), (1.0 - low).astype(BF16)


def bias_rows_kernel(table_ref, index_ref, out_ref):
    table = table_ref[...]
    high = table.astype(BF16)
    rest = table - high.astype(F32)
    middle = rest.astype(BF16)
    low = (rest - middle.astype(F32)).astype(BF16)
    chosen = (lax.broadcasted_iota(jnp.int32, (table.shape[1], SPAN), 0) == index_ref[...]).astype(F32).astype(BF16)
    out_ref[...] = dot(high, chosen) + dot(middle, chosen) + dot(low, chosen)


def bias_rows(table, index):
    places = index.shape[0]
    return run(
        bias_rows_kernel,
        grid=(places,),
        in_specs=[whole(*table.shape), pl.BlockSpec((None, 1, SPAN), lambda i: (i, 0, 0))],
        out_specs=[pl.BlockSpec((None, table.shape[0], SPAN), lambda i: (i, 0, 0))],
        out_shape=[jax.ShapeDtypeStruct((places, table.shape[0], SPAN), F32)],
        operands=[table, index],
        name="bias_rows",
    )[0]


def diagonal_base(row):
    return pltpu.roll(jnp.broadcast_to(row, (8, SPAN)), 0, 1, stride=1, stride_axis=0)


def row_blocks():
    return [(16 * c, [(128 * t + 16 * c, t) for t in range(2) if 128 * t + 16 * c < RP]) for c in range(8)]


def turned_pair(base, turn):
    return [pltpu.roll(base, turn + 8 * i, 1) if turn + 8 * i else base for i in range(2)]


def diagonal_block(pair, tiles):
    pick = lambda v, k: v[:, 128 * ((k - tiles) % 4) : 128 * ((k - tiles) % 4) + 128]
    return jnp.concatenate([jnp.concatenate([pick(v, k) for k in range(CP // 128)], axis=1) for v in pair], axis=0)


def straighten(sums):
    row = lax.broadcasted_iota(jnp.int32, (8, 1), 0)
    for bit in (1, 2, 4):
        sums = jnp.where((row // bit) % 2 == 1, pltpu.roll(sums, SPAN - bit, 1), sums)
    return column_sum(sums)


def forward_kernel(
    images, steps, sections,
    me_ref, order_ref, tokens_ref, cot_ref, gain_ref, shift_ref, wq_ref, wk_ref, wv_ref, qb_ref, vb_ref, rows_ref,
    wo_ref, ob_ref, scale_ref, fgain_ref, fshift_ref, hb_ref, rb_ref, fscale_ref, live_ref, mask_ref,
    upper_ref, *refs,
):
    half = sections // 2
    wh_refs, wr_refs, refs = refs[:half], refs[half:sections], refs[sections:]
    cross_ref, active_ref, q_ref, k_ref, v_ref, w_ref, branch_att_ref, slope_ref, branch_feed_ref, *refs = refs
    piece_refs, (now_ref, total_ref, acc_ref, scores_ref, normed_ref, att_ref) = refs[:sections], refs[sections:]
    t = pl.program_id(0)
    per = steps + 2
    phase = lax.rem(t, per)
    m = images * RP
    layer = t // per
    own = pl.ds(layer, 1)
    lanes_of = lambda at, width: pl.ds(pl.multiple_of(at * width, width), width)

    @pl.when(t == 0)
    def _():
        now_ref[...] = jnp.zeros_like(now_ref)
        for n in range(images):
            now_ref[RP * n : RP * n + ROWS] = tokens_ref[n]
        total_ref[...] = now_ref[...].astype(F32)

    def norm(gain, shift):
        whitened, _ = norm_stats(now_ref[...].astype(F32))
        acc_ref[...] = jnp.zeros_like(acc_ref)
        normed_ref[...] = (whitened * gain + shift).astype(BF16)

    def add_branch(out, scale):
        branch = scale * out * live_ref[...]
        now_ref[...] = (now_ref[...].astype(F32) + branch).astype(BF16)
        total_ref[...] += branch

    @pl.when(phase == 0)
    def _():
        cross_ref[IN_ATT] = now_ref[...]
        norm(gain_ref[own], shift_ref[own])
        cross_ref[OUT_FEED] = jnp.zeros((m, D), BF16)
        for n in range(images):
            rows = slice(RP * n, RP * n + ROWS)
            out = cot_ref[n].astype(F32) * fscale_ref[LAYERS - 1 : LAYERS] * live_ref[rows]
            cross_ref[OUT_FEED, rows] = out.astype(BF16)

    @pl.when(phase < steps)
    def _():
        normed = normed_ref[...]
        here = lanes_of(phase, QUAD * HEAD)
        q_ref[...] = ((dot(normed, wq_ref[...]) + qb_ref[own, here]) * 0.125).astype(BF16)
        k_ref[0:m] = dot(normed, wk_ref[...]).astype(BF16)
        v_ref[0:m] = (dot(normed, wv_ref[...]) + vb_ref[own, here]).astype(BF16)
        k_ref[m:] = jnp.zeros_like(k_ref[m:])
        v_ref[m:] = jnp.zeros_like(v_ref[m:])
        masks = head_masks()
        head = layer * HEADS + phase * QUAD
        cells = [(n, h) for n in range(images) for h in range(QUAD)]
        for at, (n, h) in enumerate(cells):
            lanes = slice(128 * (h // 2), 128 * (h // 2) + 128)
            qn = q_ref[RP * n : RP * n + RP, lanes] * masks[h % 2]
            scores_ref[at] = dot(qn, k_ref[RP * n : RP * n + CP, lanes], NT)
        for n in range(images):
            bases = [[diagonal_base(rows_ref[2 * n + i, pl.ds(head + h, 1), :]) for i in range(2)] for h in range(QUAD)]
            for turn, blocks in row_blocks():
                pairs = [[turned_pair(base, turn) for base in each] for each in bases]
                for row, tiles in blocks:
                    above = (upper_ref[n, row : row + 16] > 0.0)[None]
                    first, second = (
                        jnp.stack([diagonal_block(each[i], tiles) for each in pairs]) for i in range(2)
                    )
                    bias = jnp.where(above, first, second) + mask_ref[n]
                    scores_ref[QUAD * n : QUAD * n + QUAD, row : row + 16] += bias
        for n in range(images):
            for row in range(0, RP, 16):
                scores = scores_ref[QUAD * n : QUAD * n + QUAD, row : row + 16]
                power = jnp.exp(scores - jnp.max(scores, axis=2, keepdims=True))
                weights = power * (1.0 / jnp.sum(power, axis=2, keepdims=True))
                w_ref[n, :, row : row + 16] = weights.astype(BF16)
        for n in range(images):
            for pair in range(QUAD // 2):
                lanes = slice(128 * pair, 128 * pair + 128)
                vn = v_ref[RP * n : RP * n + CP, lanes]
                attended = dot(w_ref[n, 2 * pair], vn * masks[0]) + dot(w_ref[n, 2 * pair + 1], vn * masks[1])
                att_ref[RP * n : RP * n + RP, lanes] = attended.astype(BF16)
        acc_ref[...] += dot(att_ref[...], wo_ref[...])
        cross_ref[ATTENDED, :, here] = att_ref[...]

    @pl.when(phase == steps - 1)
    def _():
        out = acc_ref[...] + ob_ref[own]
        branch_att_ref[...] = out.astype(BF16)
        add_branch(out, scale_ref[own])
        cross_ref[IN_FEED] = now_ref[...]

    @pl.when(phase == steps)
    def _():
        norm(fgain_ref[own], fshift_ref[own])

    @pl.when(phase >= steps)
    def _():
        at = phase - steps
        spans = [slice(RP * n, RP * n + RP) for n in range(images)]
        actives = []
        for j in range(half):
            bias = hb_ref[own, lanes_of(order_ref[at * half + j], FF // sections)]
            hiddens = [dot(normed_ref[rows], wh_refs[j][...]) + bias for rows in spans]
            for rows, hidden in zip(spans, hiddens):
                share = 0.5 * (1.0 + lax.erf(hidden * 0.7071067811865476))
                actives.append((j, rows, (hidden * share).astype(BF16)))
                bell = jnp.exp(-0.5 * hidden * hidden) * 0.3989422804014327
                slope_ref[j, rows] = (share + hidden * bell).astype(BF16)
        for j, rows, active in actives:
            acc_ref[rows] += dot(active, wr_refs[j][...])

        @pl.when(at == 0)
        def _():
            for j, rows, active in actives:
                cross_ref[ACTIVE + j, rows] = active

        @pl.when(at == 1)
        def _():
            for j, rows, active in actives:
                active_ref[j, rows] = active

    @pl.when(phase == per - 1)
    def _():
        out = acc_ref[...] + rb_ref[own]
        branch_feed_ref[...] = out.astype(BF16)
        add_branch(out, fscale_ref[own])

    @pl.when(t == pl.num_programs(0) - 1)
    def _():
        send_pieces(me_ref[0], images, total_ref, piece_refs)


def send_pieces(me, images, rows_ref, piece_refs):
    sections = len(piece_refs)
    width = D // sections
    turned = [rows_ref[RP * n : RP * n + RP].T for n in range(images)]
    for own in range(sections):

        @pl.when(me == own)
        def _():
            for distance, piece in enumerate(piece_refs):
                at = width * (own ^ distance)
                for n in range(images):
                    piece[n] = turned[n][at : at + width, :ROWS].astype(BF16)


def pieces_shape(images, sections):
    return [jax.ShapeDtypeStruct((images, D // sections, ROWS), BF16)] * sections


def forward(images, sections, me, order, tokens, cotangent, w, tables):
    m = images * RP
    mc = (images - 1) * RP + CP
    wide = QUAD * HEAD
    steps = HEADS // QUAD
    per = steps + 2
    deep = FF // sections
    half = sections // 2
    layer = lambda t: t // per
    phase = lambda t: lax.rem(t, per)

    def att_at(t):
        inside = phase(t) < steps
        more = layer(t) + 1 < LAYERS
        l = jnp.where(inside, layer(t), jnp.minimum(layer(t) + 1, LAYERS - 1))
        return l, jnp.where(inside, phase(t), jnp.where(more, 0, steps - 1))

    def feed_at(t):
        return layer(t), jnp.maximum(phase(t) - steps, 0)

    def third(which):
        def index(t, *_):
            l, g = att_at(t)
            return l, 0, which * steps + g

        return pl.BlockSpec((None, D, wide), index)

    def att_in(block, place):
        return pl.BlockSpec(block, lambda t, *_: place(*att_at(t)))

    def feed_in(block, place, j):
        return pl.BlockSpec(block, lambda t, me, order: place(layer(t), order[feed_at(t)[1] * half + j]))

    def att_out(block, place):
        return pl.BlockSpec(block, lambda t, *_: place(layer(t), jnp.minimum(phase(t), steps - 1)))

    per_layer = lambda *block: pl.BlockSpec((None,) + block, lambda t, *_: (layer(t),) + (0,) * len(block))
    row = whole(LAYERS, D)
    mine = pl.BlockSpec((images, ROWS, D), lambda t, me, order: (me[0], 0, 0))
    shape = lambda *s, dtype=BF16: jax.ShapeDtypeStruct(s, dtype)
    results = run(
        functools.partial(forward_kernel, images, steps, sections),
        grid=(LAYERS * per,),
        prefetch=[me, order],
        in_specs=[
            mine, mine, row, row, third(0), third(1), third(2), row, row,
            whole(2 * images, LAYERS * HEADS, SPAN),
            att_in((None, wide, D), lambda l, g: (l, g, 0)),
            row, row, row, row,
            whole(LAYERS, FF),
            row, row, whole(m, 1), whole(images, 1, CP), whole(images, RP, CP),
        ]
        + [feed_in((None, D, deep), lambda l, f: (l, 0, f), j) for j in range(half)]
        + [feed_in((None, deep, D), lambda l, f: (l, f, 0), j) for j in range(half)],
        out_specs=[
            per_layer(ACTIVE + half, m, D),
            per_layer(half, m, deep),
            att_out((None, m, wide), lambda l, g: (l, 0, g)),
            att_out((None, mc, wide), lambda l, g: (l, 0, g)),
            att_out((None, mc, wide), lambda l, g: (l, 0, g)),
            att_out((None, images, QUAD, RP, CP), lambda l, g: (l, 0, g, 0, 0)),
            per_layer(m, D),
            pl.BlockSpec((None, half, m, deep), lambda t, *_: feed_at(t) + (0, 0)),
            per_layer(m, D),
        ]
        + [whole(images, D // sections, ROWS)] * sections,
        out_shape=[
            shape(LAYERS, ACTIVE + half, m, D), shape(LAYERS, half, m, deep),
            shape(LAYERS, m, D), shape(LAYERS, mc, D), shape(LAYERS, mc, D), shape(LAYERS, images, HEADS, RP, CP),
            shape(LAYERS, m, D), shape(LAYERS, sections, m, deep), shape(LAYERS, m, D),
        ]
        + pieces_shape(images, sections),
        scratch=[
            pltpu.VMEM((m, D), BF16), pltpu.VMEM((m, D), F32), pltpu.VMEM((m, D), F32),
            pltpu.VMEM((images * QUAD, RP, CP), F32), pltpu.VMEM((m, D), BF16), pltpu.VMEM((m, wide), BF16),
        ],
        name="forward",
        operands=[
            tokens, cotangent, w.attention_gain, w.attention_shift, w.input_projection, w.input_projection,
            w.input_projection, w.query_bias, w.value_bias, tables.rows, w.output_projection,
            w.output_bias, w.attention_scale, w.forward_gain, w.forward_shift,
            w.hidden_bias, w.return_bias, w.forward_scale, tables.live,
            tables.mask, tables.upper,
        ] + [w.hidden_weight] * half + [w.return_weight] * half,
    )
    return results[0], Kept(*results[1:-sections]), results[-sections:]


def layer_block(layer, *block):
    return pl.BlockSpec((None,) + block, lambda *_: (layer,) + (0,) * len(block))


def feed_steps(step, gain, bg_rows, out_ref, u_ref, live_ref, branch_ref, slope_ref, wh_refs, wr_refs,
               next_ref, small_ref, hb_ref, send_ref, keep_ref, ng_ref):
    @pl.when(step == 0)
    def _():
        ng_ref[...] = jnp.zeros_like(ng_ref)

    grads = []
    for j, wr_ref in enumerate(wr_refs):
        grad = dot(out_ref[...], wr_ref[...], NT) * slope_ref[j].astype(F32)
        grads.append(grad.astype(BF16))
        hb_ref[j] = column_sum(grads[j].astype(F32))
    for grad, wh_ref in zip(grads, wh_refs):
        ng_ref[...] += dot(grad, wh_ref[...], NT)

    @pl.when(step == 0)
    def _():
        for j, grad in enumerate(grads):
            send_ref[j] = grad

    @pl.when(step == 1)
    def _():
        for j, grad in enumerate(grads):
            keep_ref[j] = grad

    @pl.when(step == 1)
    def _():
        bg_rows()
        bg = next_ref[...]
        whitened, inverse = norm_stats(u_ref[...].astype(F32))
        ng = ng_ref[...]
        small_ref[...] = jnp.zeros_like(small_ref)
        small_ref[0:1] = column_sum(ng * whitened)
        small_ref[1:2] = column_sum(ng)
        small_ref[2:3] = column_sum(out_ref[...].astype(F32))
        small_ref[3:4] = column_sum(bg * branch_ref[...].astype(F32) * live_ref[...])
        next_ref[...] = bg + norm_back(ng, whitened, inverse, gain)


def feed_refs(refs, rest):
    half = (len(refs) - rest) // 2
    return refs[:half], refs[half : 2 * half], refs[2 * half :]


def feed_blocks(layer, m, sections, at):
    wide = FF // sections
    half = sections // 2
    hidden = lambda j: pl.BlockSpec((None, D, wide), lambda t, me, order: (layer, 0, order[at(t) * half + j]))
    returned = lambda j: pl.BlockSpec((None, wide, D), lambda t, me, order: (layer, order[at(t) * half + j], 0))
    slope = pl.BlockSpec((None, half, m, wide), lambda t, *_: (layer, at(t), 0, 0))
    return [slope] + [hidden(j) for j in range(half)] + [returned(j) for j in range(half)]


def first_chain_kernel(images, me_ref, order_ref, cot_ref, out_ref, u_ref, gain_ref, live_ref, branch_ref, slope_ref,
                       *refs):
    wh_refs, wr_refs, (next_ref, small_ref, hb_ref, keep_ref, send_ref, ng_ref) = feed_refs(refs, 6)

    def bg_rows():
        next_ref[...] = jnp.zeros_like(next_ref)
        for n in range(images):
            next_ref[RP * n : RP * n + ROWS] = cot_ref[n].astype(F32)

    feed_steps(
        pl.program_id(0), gain_ref[LAYERS - 1 : LAYERS], bg_rows, out_ref, u_ref, live_ref,
        branch_ref, slope_ref, wh_refs, wr_refs, next_ref, small_ref, hb_ref, send_ref, keep_ref, ng_ref,
    )


def slot(layer, index, m):
    return pl.BlockSpec((None, None, m, D), lambda *_: (layer, index, 0, 0))


def first_chain(images, sections, me, order, cotangent, cross, kept, w, tables):
    layer = LAYERS - 1
    m = images * RP
    wide = FF // sections
    sends = sections // 2
    shape = jax.ShapeDtypeStruct
    return run(
        functools.partial(first_chain_kernel, images),
        grid=(2,),
        in_specs=[
            pl.BlockSpec((images, ROWS, D), lambda i, me, order: (me[0], 0, 0)),
            slot(layer, OUT_FEED, m), slot(layer, IN_FEED, m), whole(LAYERS, D), whole(m, 1), layer_block(layer, m, D),
            *feed_blocks(layer, m, sections, lambda i: i),
        ],
        out_specs=[
            whole(m, D), whole(8, D),
            pl.BlockSpec((sends, 1, wide), lambda i, *_: (i, 0, 0)),
            whole(sends, m, wide),
            whole(sends, m, wide),
        ],
        out_shape=[
            shape((m, D), F32), shape((8, D), F32), shape((sections, 1, wide), F32), shape((sends, m, wide), BF16),
            shape((sends, m, wide), BF16),
        ],
        scratch=[pltpu.VMEM((m, D), F32)],
        prefetch=[me, order],
        operands=[
            cotangent, cross, cross, w.forward_gain, tables.live, kept.branch_feed, kept.slope,
        ] + [w.hidden_weight] * sends + [w.return_weight] * sends,
        name="first_chain",
    )


def by_first_bit(total, own, send_ref, keep_ref):
    pairs, rows, width = keep_ref.shape
    blocks = total.astype(BF16).reshape(pairs, 2, rows, width)
    even, odd = blocks[:, 0], blocks[:, 1]

    @pl.when(own == 0)
    def _():
        keep_ref[...] = even
        send_ref[...] = odd

    @pl.when(own == 1)
    def _():
        keep_ref[...] = odd
        send_ref[...] = even


def store_halves(totals, own, a_send_ref, a_keep_ref, b_send_ref, b_keep_ref):
    last = pl.program_id(0) == pl.num_programs(0) - 1
    for j, total in enumerate(totals):
        half = total.shape[1] // 2
        left = total[:, :half].astype(BF16)

        @pl.when(last)
        def _():
            a_keep_ref[j] = left

        @pl.when(jnp.logical_not(last))
        def _():
            a_send_ref[j] = left

        by_first_bit(total[:, half:], own, b_send_ref.at[j], b_keep_ref.at[j])


def halves_out(count, sends, rows):
    half = D // 2
    pairs = D // (2 * rows)
    piece = pl.BlockSpec((count, None, pairs, rows, half), lambda i, *_: (0, i, 0, 0, 0))
    specs = [whole(count, D, half), whole(count, D, half), piece, piece]
    shapes = [jax.ShapeDtypeStruct((count, D, half), BF16)] * 2
    return specs, shapes + [jax.ShapeDtypeStruct((count, sends, pairs, rows, half), BF16)] * 2


def turned_norm(u_ref, gain, shift):
    whitened, _ = norm_stats(u_ref[...].astype(F32))
    return (whitened * gain + shift).astype(BF16).T


def feed_keep_kernel(layer, returned, hidden, own_ref, *refs):
    ins, out_refs, turned_ref = refs[:-5], refs[-5:-1], refs[-1]
    first = pl.program_id(0) == 0
    totals = []
    if returned:
        out_ref, out_got_ref, active_ref, active_got_ref, *ins = ins

        @pl.when(first)
        def _():
            turned_ref[0] = out_ref[...].T
            turned_ref[1] = out_got_ref[...].T

        totals.append(dot(turned_ref[0], active_ref[...]) + dot(turned_ref[1], active_got_ref[...]))
    if hidden:
        u_ref, u_got_ref, gain_ref, shift_ref, hg_ref, hg_got_ref = ins
        at = 2 * returned

        @pl.when(first)
        def _():
            gain, shift = gain_ref[layer : layer + 1], shift_ref[layer : layer + 1]
            turned_ref[at] = turned_norm(u_ref, gain, shift)
            turned_ref[at + 1] = turned_norm(u_got_ref, gain, shift)

        totals.append(dot(turned_ref[at], hg_ref[...]) + dot(turned_ref[at + 1], hg_got_ref[...]))
    store_halves(totals, own_ref[0], *out_refs)


def feed_keep(layer, own, rows, cross, cross_got, kept, w, after, returned=None, hidden=None):
    wide = FF // lax.axis_size(SECTION)
    sends, m = kept.active.shape[1:3]
    count = (returned is not None) + (hidden is not None)
    halves, out_shape = halves_out(count, sends, rows)
    specs, operands = [], []
    if returned:
        specs += [
            *returned[2:],
            pl.BlockSpec((None, None, m, wide), lambda i, own: (layer, i, 0, 0)),
            pl.BlockSpec((None, None, m, wide), lambda i, own: (layer, ACTIVE + i, 0, 0)),
        ]
        operands += [*returned[:2], kept.active, cross_got]
    if hidden:
        block = pl.BlockSpec((None, m, wide), lambda i, own: (i, 0, 0))
        specs += [slot(layer, IN_FEED, m)] * 2 + [whole(LAYERS, D)] * 2 + [block] * 2
        operands += [cross, cross_got, w.forward_gain, w.forward_shift, *hidden]
    return run(
        functools.partial(feed_keep_kernel, layer, returned is not None, hidden is not None),
        grid=(sends,),
        in_specs=specs,
        out_specs=halves,
        out_shape=out_shape,
        scratch=[pltpu.VMEM((2 * count, D, m), BF16)],
        prefetch=[own],
        operands=operands,
        after=after,
        name="feed_keep",
    )


def attention_steps(
    step, images, sections, me, gain, scale, finish, u_ref, bg_ref, live_ref, q_ref, k_ref, v_ref, w_ref, branch_ref,
    wq_ref, wk_ref, wv_ref, wo_ref, next_ref, send_ref, keep_ref, sg_ref, bias_ref, small_ref,
    ng_ref, out_ref, wg_ref, parts_ref,
):
    steps = HEADS // QUAD
    sends = sections // 2

    @pl.when(step == 0)
    def _():
        out_ref[...] = (bg_ref[...] * scale * live_ref[...]).astype(BF16)
        ng_ref[...] = jnp.zeros_like(ng_ref)

    att_grad = dot(out_ref[...], wo_ref[...], NT).astype(BF16)
    masks = head_masks()
    lanes_of = lambda pair: slice(128 * pair, 128 * pair + 128)
    for n in range(images):
        for h in range(QUAD):
            lanes = lanes_of(h // 2)
            chosen = att_grad[RP * n : RP * n + RP, lanes] * masks[h % 2]
            wg_ref[QUAD * n + h] = dot(chosen, v_ref[RP * n : RP * n + CP, lanes], NT)
    for n in range(images):
        for row in range(0, RP, 16):
            probs = w_ref[n, :, row : row + 16].astype(F32)
            product = wg_ref[QUAD * n : QUAD * n + QUAD, row : row + 16] * probs
            grad = product - probs * jnp.sum(product, axis=2, keepdims=True)
            sg_ref[n, :, row : row + 16] = grad.astype(BF16)
    grads = [[], [], []]
    for n in range(images):
        here = [[], [], []]
        for pair in range(QUAD // 2):
            lanes = lanes_of(pair)
            rows = slice(RP * n, RP * n + RP)
            kn, qn, an = k_ref[RP * n : RP * n + CP, lanes], q_ref[rows, lanes], att_grad[rows, lanes]
            one, two = (n, 2 * pair), (n, 2 * pair + 1)
            dq = dot(sg_ref[one], kn * masks[0]) + dot(sg_ref[two], kn * masks[1])
            dk = dot(sg_ref[one], qn * masks[0], TN) + dot(sg_ref[two], qn * masks[1], TN)
            dv = dot(w_ref[n, 2 * pair], an * masks[0], TN) + dot(w_ref[n, 2 * pair + 1], an * masks[1], TN)
            here[0].append((dq.astype(BF16).astype(F32) * 0.125).astype(BF16))
            here[1].append(dk[:RP].astype(BF16))
            here[2].append(dv[:RP].astype(BF16))
        for i in range(3):
            grads[i].append(jnp.concatenate(here[i], axis=1))
    gq, gk, gv = (jnp.concatenate(each, axis=0) for each in grads)
    wide = QUAD * HEAD
    for i, each in enumerate((gq, gk, gv)):
        for g in range(steps):

            @pl.when(step == g)
            def _():
                parts_ref[:, i * D + g * wide : i * D + g * wide + wide] = each
    bias_ref[0] = column_sum(gq.astype(F32))
    bias_ref[1] = column_sum(gv.astype(F32))
    ng_ref[...] += dot(gq, wq_ref[...], NT) + dot(gk, wk_ref[...], NT) + dot(gv, wv_ref[...], NT)

    @pl.when(step == steps - 1)
    def _():
        whitened, inverse = norm_stats(u_ref[...].astype(F32))
        ng = ng_ref[...]
        bg = bg_ref[...]
        next_ref[...] = bg + norm_back(ng, whitened, inverse, gain)
        small_ref[...] = jnp.zeros_like(small_ref)
        small_ref[0:1] = column_sum(ng * whitened)
        small_ref[1:2] = column_sum(ng)
        small_ref[2:3] = column_sum(out_ref[...].astype(F32))
        small_ref[3:4] = column_sum(bg * branch_ref[...].astype(F32) * live_ref[...])
        part, each = 3 * D // sections, D // sections
        for own in range(sections):

            @pl.when(me == own)
            def _():
                for s in range(sections):
                    place = sends - 1 - ((s // 2) ^ (own // 2))
                    target = (keep_ref if s % 2 == own % 2 else send_ref).at[place]
                    target[:, :part] = parts_ref[:, part * s : part * s + part]
                    target[:, part:] = out_ref[:, each * s : each * s + each]
        finish()


def middle_chain_kernel(
    images, sections, me_ref, order_ref, u_ref, bg_ref, gain_ref, scale_ref, fgain_ref, fscale_ref, live_ref, q_ref,
    k_ref, v_ref, w_ref, branch_ref, wq_ref, wk_ref, wv_ref, wo_ref, u_feed_ref, branch_feed_ref, slope_ref, *refs,
):
    wh_refs, wr_refs, refs = feed_refs(refs, 14)
    next_ref, send_ref, keep_ref, sg_ref, bias_ref, small_ref, feed_small_ref, hb_ref, hg_keep_ref, hg_send_ref = refs[:10]
    ng_ref, out_ref, wg_ref, parts_ref = refs[10:]
    t = pl.program_id(0)
    steps = HEADS // QUAD
    att, feed = slice(LAYERS - 1, LAYERS), slice(LAYERS - 2, LAYERS - 1)
    out_rows_ref = hg_send_ref.at[sections // 2]

    def finish():
        out_rows_ref[...] = (next_ref[...] * fscale_ref[feed] * live_ref[...]).astype(BF16)

    @pl.when(t < steps)
    def _():
        attention_steps(
            t, images, sections, me_ref[0], gain_ref[att], scale_ref[att], finish, u_ref, bg_ref, live_ref, q_ref, k_ref,
            v_ref, w_ref, branch_ref, wq_ref, wk_ref, wv_ref, wo_ref, next_ref, send_ref, keep_ref, sg_ref,
            bias_ref, small_ref, ng_ref, out_ref, wg_ref, parts_ref,
        )

    @pl.when(t >= steps)
    def _():
        feed_steps(
            t - steps, fgain_ref[feed], lambda: None, out_rows_ref, u_feed_ref, live_ref, branch_feed_ref,
            slope_ref, wh_refs, wr_refs, next_ref, feed_small_ref, hb_ref, hg_send_ref, hg_keep_ref, ng_ref,
        )


def attention_specs(layer, images, at):
    m = images * RP
    mc = (images - 1) * RP + CP
    wide = QUAD * HEAD
    steps = HEADS // QUAD
    block = lambda count: pl.BlockSpec((None, count, wide), lambda t, *_: (layer, 0, at(t)))
    third = lambda which: pl.BlockSpec((None, D, wide), lambda t, *_: (layer, 0, which * steps + at(t)))
    return [
        block(m), block(mc), block(mc),
        pl.BlockSpec((None, images, QUAD, RP, CP), lambda t, *_: (layer, 0, at(t), 0, 0)),
        layer_block(layer, m, D), third(0), third(1), third(2),
        pl.BlockSpec((None, wide, D), lambda t, *_: (layer, at(t), 0)),
    ]


def attention_out(images, sections, at):
    m = images * RP
    sends = sections // 2
    shape = jax.ShapeDtypeStruct
    specs = [
        whole(m, D), whole(sends, m, D), whole(sends, m, D),
        pl.BlockSpec((images, QUAD, RP, CP), lambda t, *_: (0, at(t), 0, 0)),
        pl.BlockSpec((2, 1, QUAD * HEAD), lambda t, *_: (0, 0, at(t))), whole(8, D),
    ]
    shapes = [
        shape((m, D), F32), shape((sends, m, D), BF16), shape((sends, m, D), BF16),
        shape((images, HEADS, RP, CP), BF16), shape((2, 1, D), F32), shape((8, D), F32),
    ]
    return specs, shapes


def attention_scratch(images):
    m = images * RP
    return [
        pltpu.VMEM((m, D), F32), pltpu.VMEM((m, D), BF16), pltpu.VMEM((images * QUAD, RP, CP), F32),
        pltpu.VMEM((m, 3 * D), BF16),
    ]


def attention_operands(kept, w, tables):
    return [
        kept.q, kept.k, kept.v, kept.w, kept.branch_att, w.input_projection, w.input_projection, w.input_projection,
        w.output_projection,
    ]


def middle_chain(images, sections, me, order, bg, cross, kept, w, tables, after):
    m = images * RP
    wide = FF // sections
    sends = sections // 2
    steps = HEADS // QUAD
    late = lambda t: jnp.maximum(t - steps, 0)
    early = lambda t: jnp.minimum(t, steps - 1)
    shape = jax.ShapeDtypeStruct
    out_specs, out_shape = attention_out(images, sections, early)
    return run(
        functools.partial(middle_chain_kernel, images, sections),
        grid=(steps + 2,),
        prefetch=[me, order],
        in_specs=[slot(LAYERS - 1, IN_ATT, m), whole(m, D)] + [whole(LAYERS, D)] * 4 + [whole(m, 1)]
        + attention_specs(LAYERS - 1, images, early)
        + [
            slot(LAYERS - 2, IN_FEED, m), layer_block(LAYERS - 2, m, D),
            *feed_blocks(LAYERS - 2, m, sections, late),
        ],
        out_specs=out_specs + [
            whole(8, D), pl.BlockSpec((sends, 1, wide), lambda t, *_: (late(t), 0, 0)),
            whole(sends, m, wide), whole(sends + 1, m, wide),
        ],
        out_shape=out_shape + [
            shape((8, D), F32), shape((sections, 1, wide), F32), shape((sends, m, wide), BF16),
            shape((sends + 1, m, wide), BF16),
        ],
        scratch=attention_scratch(images),
        operands=[cross, bg, w.attention_gain, w.attention_scale, w.forward_gain, w.forward_scale, tables.live]
        + attention_operands(kept, w, tables)
        + [cross, kept.branch_feed, kept.slope] + [w.hidden_weight] * sends + [w.return_weight] * sends,
        after=after,
        name="middle_chain",
    )


def last_chain_kernel(images, sections, me_ref, u_ref, bg_ref, gain_ref, scale_ref, live_ref, *refs):
    first = 9 + sections
    ins, early_refs, outs, piece_refs, scratch = (
        refs[:9], refs[9:first], refs[first : first + 6], refs[first + 6 : first + 6 + sections], refs[-4:]
    )
    next_ref = outs[0]

    def finish():
        for early_ref, piece_ref in zip(early_refs, piece_refs):
            piece_ref[0] = early_ref[...]
        send_pieces(me_ref[0], images, next_ref, [piece.at[1] for piece in piece_refs])

    attention_steps(
        pl.program_id(0), images, sections, me_ref[0], gain_ref[0:1], scale_ref[0:1], finish, u_ref, bg_ref, live_ref,
        *ins, *outs, *scratch,
    )


def last_chain(images, sections, me, bg, cross, kept, w, tables, after, early):
    m = images * RP
    at = lambda t: t
    out_specs, out_shape = attention_out(images, sections, at)
    return run(
        functools.partial(last_chain_kernel, images, sections),
        grid=(HEADS // QUAD,),
        prefetch=[me],
        in_specs=[slot(0, IN_ATT, m), whole(m, D)] + [whole(LAYERS, D)] * 2 + [whole(m, 1)]
        + attention_specs(0, images, at) + [whole(*piece.shape) for piece in early],
        out_specs=out_specs + [whole(2, *piece.shape) for piece in early],
        out_shape=out_shape + [jax.ShapeDtypeStruct((2,) + piece.shape, BF16) for piece in early],
        scratch=attention_scratch(images),
        operands=[cross, bg, w.attention_gain, w.attention_scale, tables.live, *attention_operands(kept, w, tables), *early],
        after=after,
        name="last_chain",
    )


def table_rows_kernel(images, sg_ref, upper_ref, rows_ref):
    for n in range(images):
        for h in range(QUAD):
            sums = [None, None]
            for g in range(0, 16, 2):
                blocks = [(g, 0)] + ([(g + 16, 1)] if 8 * (g + 16) < RP else [])
                loaded = {}
                for start, _ in blocks:
                    both = sg_ref[n, h, 8 * start : 8 * start + 16].astype(F32)
                    above = jnp.where(upper_ref[n, 8 * start : 8 * start + 16] > 0.0, both, 0.0)
                    loaded[start] = (above, both - above)
                for u in range(2):
                    for i in range(2):
                        cut = lambda s, k: loaded[s][u][8 * i : 8 * i + 8, 128 * k : 128 * k + 128]
                        zero = jnp.zeros((8, 128), F32)
                        tiles = [cut(g, 0), cut(g, 1), zero, zero]
                        if len(blocks) > 1:
                            tiles = [tiles[0] + cut(g + 16, 1), tiles[1], zero, cut(g + 16, 0)]
                        block = jnp.concatenate(tiles, axis=1)
                        if g + i:
                            block = pltpu.roll(block, SPAN - 8 * (g + i), 1)
                        sums[u] = block if sums[u] is None else sums[u] + block
            for u in range(2):
                rows_ref[2 * n + u, pl.ds(pl.program_id(0) * QUAD + h, 1)] = straighten(sums[u])


def table_rows(images, sg, tables, after):
    shape = (2 * images, HEADS, SPAN)
    return run(
        functools.partial(table_rows_kernel, images),
        grid=(HEADS // QUAD,),
        in_specs=[pl.BlockSpec((images, QUAD, RP, CP), lambda g: (0, g, 0, 0)), whole(images, RP, CP)],
        out_specs=[whole(*shape)],
        out_shape=[jax.ShapeDtypeStruct(shape, F32)],
        operands=[sg, tables.upper],
        after=after,
        name="table_rows",
    )[0]


def attention_product(nt, at, grads):
    first = 3 * D // (4 * 128) * 128
    low = lax.broadcasted_iota(jnp.int32, (1, 128), 1) < HEAD
    left = dot(nt, grads[:, : first + 128])
    right = dot(at, grads[:, first:])
    middle = jnp.where(low, left[:, first:], right[:, :128])
    return jnp.concatenate([left[:, :first], middle, right[:, 128:]], axis=1)


def attention_keep_kernel(layer, own_ref, u_ref, u_got_ref, att_ref, att_got_ref, gain_ref, shift_ref, grads_ref, *refs):
    got_ref, out_refs, (nt_ref, at_ref) = refs[0], refs[1:5], refs[5:]

    @pl.when(pl.program_id(0) == 0)
    def _():
        gain, shift = gain_ref[layer : layer + 1], shift_ref[layer : layer + 1]
        for i, (u, att) in enumerate(((u_ref, att_ref), (u_got_ref, att_got_ref))):
            nt_ref[i] = turned_norm(u, gain, shift)
            at_ref[i] = att[...].T

    total = attention_product(nt_ref[0], at_ref[0], grads_ref[...])
    total += attention_product(nt_ref[1], at_ref[1], got_ref[...])
    store_halves([total], own_ref[0], *out_refs)


def attention_keep(layer, own, rows, cross, cross_got, grads, got, w, after):
    sends, m, _ = grads.shape
    out_specs, out_shape = halves_out(1, sends, rows)
    return run(
        functools.partial(attention_keep_kernel, layer),
        grid=(sends,),
        in_specs=[
            slot(layer, IN_ATT, m), slot(layer, IN_ATT, m), slot(layer, ATTENDED, m), slot(layer, ATTENDED, m),
            whole(LAYERS, D), whole(LAYERS, D),
        ] + [pl.BlockSpec((None, m, D), lambda i, own: (i, 0, 0))] * 2,
        out_specs=out_specs,
        out_shape=out_shape,
        scratch=[pltpu.VMEM((2, D, m), BF16), pltpu.VMEM((2, D, m), BF16)],
        prefetch=[own],
        operands=[cross, cross_got, cross, cross_got, w.attention_gain, w.attention_shift, grads, got],
        after=after,
        name="attention_keep",
    )


def flip(value, axis, bit):
    count = lax.axis_size(axis)
    return lax.ppermute(value, axis, [(i, i ^ bit) for i in range(count)])


def wide_names():
    return [(WIDE, 1 << i) for i in reversed(range(lax.axis_size(WIDE).bit_length() - 1))]


def own_bit(axis, bit):
    return (lax.axis_index(axis) // bit) % 2


ACROSS = (SECTION, 2)


class Chunk:
    def __init__(self, keep, received, lead, names, order, rows):
        self.width = keep.shape[-1]
        self.rows = rows
        shape = keep.shape[:1] + (2,) * len(names) + (rows, self.width)
        self.terms = [(array.reshape(shape), lead, tuple(names)) for array in (keep, received)]
        self.left = tuple(names)
        self.done = ()
        self.order = list(order)

    def arrived(self):
        return [self.terms[-1][0]]


class Small:
    def __init__(self, keep, received):
        self.terms = [keep, received]
        self.order = [ACROSS] + list(reversed(wide_names()))


def combine(groups, mine, after, name, writer=None, out_shape=None, small=None, held=()):
    all_names = wide_names()
    specs, operands, counts, out_specs, shapes = [], [], [], [], []
    rows = groups[0][0].rows if groups else 0
    split = 2 if rows % 32 == 0 and writer is None else 1
    rows = rows // split
    for group in groups:
        for chunk in group:
            stage = None if writer else chunk.order[0]
            for array, lead, names in chunk.terms:
                fixed = [n in chunk.done or n == stage for n in names]
                block = (None,) + tuple(None if f else 2 for f in fixed) + (rows, chunk.width)

                def index(i, mine_ref, lead=lead, names=names, fixed=fixed, stage=stage):
                    at = []
                    for n, f in zip(names, fixed):
                        own = 1 if n == ACROSS else mine_ref[all_names.index(n)]
                        at.append((1 - own if n == stage else own) if f else 0)
                    return (lead, *at, i, 0)

                specs.append(pl.BlockSpec(block, index))
                operands.append(array)
            counts.append(len(chunk.terms))
        if writer is None:
            chunk = group[0]
            dims = (len(group),) + (2,) * (len(chunk.left) - 1)
            shapes.append(jax.ShapeDtypeStruct(dims + (chunk.rows, chunk.width), BF16))
            out_specs.append(
                pl.BlockSpec(dims + (rows, chunk.width), lambda i, mine_ref, n=len(dims): (0,) * n + (i, 0))
            )
    if writer:
        shapes = out_shape
        out_specs = [whole(*s.shape) for s in shapes]

    if small:
        specs += [whole(*term.shape) for term in small.terms]
        operands += small.terms
        shape = small.terms[0].shape[-2:]
        shapes += [jax.ShapeDtypeStruct(shape, F32)] * (1 + (small.order[0] == ACROSS))
        out_specs += [whole(*shape)] * (len(shapes) - len(out_specs))

    def kernel(mine_ref, *refs):
        ins, outs = refs[: len(operands)], refs[len(operands) :]
        if small:
            value = ins[-2][...] + ins[-1][...]
            if small.order[0] == ACROSS:
                outs[-2][...], outs[-1][...] = value[0], value[1]
            else:
                outs[-1][...] = value
        totals, at = [], 0
        for count in counts:
            total = ins[at][...].astype(F32)
            for ref in ins[at + 1 : at + count]:
                total = total + ref[...].astype(F32)
            totals.append(total)
            at += count
        if writer:
            writer(outs, totals)
            return
        for group, out in zip(groups, outs):
            for j in range(len(group)):
                out[j] = totals.pop(0).astype(BF16)

    results = run(
        kernel, grid=(split,), in_specs=specs, out_specs=out_specs, out_shape=shapes,
        prefetch=[mine], operands=operands, after=list(after), held=held, name=name,
    )
    if writer:
        return results
    held_count = len(held)
    results, held = results[: len(results) - held_count], results[len(results) - held_count :]
    if small:
        stage = small.order[0]
        small.order = small.order[1:]
        small.terms = [results[-1], flip(results[-2] if stage == ACROSS else results[-1], *stage)]
    for group, sent in zip(groups, results):
        stage = group[0].order[0]
        got = flip(sent, *stage)
        for j, chunk in enumerate(group):
            chunk.order = chunk.order[1:]
            chunk.done = chunk.done + (stage,)
            chunk.left = tuple(n for n in chunk.left if n != stage)
            chunk.terms = chunk.terms + [(got, j, chunk.left)]
    return (results, held) if held else results


def pack_kernel(sections, me_ref, index_ref, rows0_ref, rows1_ref, a0_ref, a1_ref, f0_ref, f1_ref, b0_ref, b1_ref,
                h0_ref, h1_ref, send_ref, keep_ref, sum_ref):
    step = pl.program_id(0)

    @pl.when(step == 0)
    def _():
        sum_ref[...] = jnp.zeros_like(sum_ref)

    chosen = (lax.broadcasted_iota(jnp.int32, (TABLE, SPAN), 0) == index_ref[...]).astype(F32).astype(BF16)
    rows = jnp.concatenate([rows0_ref[...], rows1_ref[...]], axis=0)
    high = rows.astype(BF16)
    low = (rows - high.astype(F32)).astype(BF16)
    sum_ref[...] += dot(high, chosen, NT) + dot(low, chosen, NT)
    each = D // sections
    heads = HEADS // sections
    sends = sections // 2
    tiles = TABLE // 256
    layers = ((a0_ref, f0_ref, b0_ref, h0_ref), (a1_ref, f1_ref, b1_ref, h1_ref))

    def fill(own):
        for s in range(sections):
            place = sends - 1 - ((s // 2) ^ (own // 2))
            ref = (keep_ref if s % 2 == own % 2 else send_ref).at[place]
            lanes = slice(each * s, each * s + each)
            for layer, (a_ref, f_ref, b_ref, h_ref) in enumerate(layers):
                at = layer * SMALL
                ref[at : at + 4, 0:each] = a_ref[0:4, lanes]
                ref[at + 4 : at + 8, 0:each] = f_ref[0:4, lanes]
                for i in range(2):
                    ref[at + 8 + i : at + 9 + i, 0:each] = b_ref[i, :, lanes]
                where = place + (sends if s % 2 == own % 2 else 0)
                for j in range(FF // sections // 256):
                    ref[at + 10 + j : at + 11 + j] = h_ref[where, :, 256 * j : 256 * j + 256]
                for k in range(heads):
                    row = layer * HEADS + s * heads + k
                    for j in range(tiles):
                        to = at + 13 + k * tiles + j
                        ref[to : to + 1] = sum_ref[row : row + 1, 256 * j : 256 * j + 256]

    @pl.when(step == pl.num_programs(0) - 1)
    def _():
        send_ref[...] = jnp.zeros_like(send_ref)
        keep_ref[...] = jnp.zeros_like(keep_ref)
        for own in range(sections):
            pl.when(me_ref[0] == own)(functools.partial(fill, own))


def pack(me, sections, index, rows, att, feed, bias, hidden, after):
    places = index.shape[0]
    row = pl.BlockSpec((None, HEADS, SPAN), lambda i, me: (i, 0, 0))
    hidden_wide = FF // sections
    shape = (sections // 2, LAYERS * SMALL, 256)
    return run(
        functools.partial(pack_kernel, sections),
        grid=(places,),
        prefetch=[me],
        in_specs=[pl.BlockSpec((None, 1, SPAN), lambda i, me: (i, 0, 0)), row, row]
        + [whole(8, D)] * 4 + [whole(2, 1, D)] * 2 + [whole(sections, 1, hidden_wide)] * 2,
        out_specs=[whole(*shape)] * 2,
        out_shape=[jax.ShapeDtypeStruct(shape, F32)] * 2,
        scratch=[pltpu.VMEM((LAYERS * HEADS, TABLE), F32)],
        operands=[index, *rows, *att, *feed, *bias, *hidden],
        after=after,
        name="pack",
    )


def unpack_kernel(keep_ref, got_ref, *out_refs):
    *vector_refs, hidden_ref, table_ref, small_ref = out_refs
    small_ref[...] = keep_ref[...] + got_ref[...]
    each = vector_refs[0].shape[1]
    heads = table_ref.shape[0]
    tiles = TABLE // 256
    for layer in range(LAYERS):
        at = layer * SMALL
        for i, ref in enumerate(vector_refs):
            ref[layer : layer + 1] = small_ref[at + i : at + i + 1, 0:each]
        for j in range(hidden_ref.shape[1] // 256):
            hidden_ref[layer : layer + 1, 256 * j : 256 * j + 256] = small_ref[at + 10 + j : at + 11 + j]
        for k in range(heads):
            row = at + 13 + k * tiles
            line = jnp.concatenate([small_ref[r : r + 1] for r in range(row, row + tiles)], axis=1)
            table_ref[k, layer : layer + 1] = line[:, :REL]


def unpack(small, sections, after):
    shape = jax.ShapeDtypeStruct
    out_shape = [shape((LAYERS, D // sections), F32)] * 10
    out_shape += [shape((LAYERS, FF // sections), F32), shape((HEADS // sections, LAYERS, REL), F32)]
    return run(
        unpack_kernel, grid=(1,), in_specs=[whole(LAYERS * SMALL, 256)] * 2, out_specs=[whole(*s.shape) for s in out_shape],
        out_shape=out_shape, operands=small.terms, scratch=[pltpu.VMEM((LAYERS * SMALL, 256), F32)], after=after,
        name="unpack",
    )


def assemble_kernel(me_ref, *refs):
    *piece_refs, output_ref, grad_ref = refs
    images = piece_refs[0].shape[1]
    for distance, piece in enumerate(piece_refs):
        rows = pl.ds((me_ref[0] ^ distance) * images, images)
        output_ref[rows] = piece[0]
        grad_ref[rows] = piece[1]


def assemble(me, pieces, after):
    sections = len(pieces)
    _, images, width, rows = pieces[0].shape
    shape = (sections * images, width, rows)
    return run(
        assemble_kernel, grid=(1,), prefetch=[me], in_specs=[whole(*pieces[0].shape)] * sections,
        out_specs=[whole(*shape)] * 2, out_shape=[jax.ShapeDtypeStruct(shape, BF16)] * 2,
        operands=pieces, after=after, name="assemble",
    )


def on_device(
    tokens, cotangent, patch_grids, attention_gain, attention_shift, input_projection, query_bias, value_bias,
    relative_table, output_projection, output_bias, attention_scale, forward_gain, forward_shift, hidden_weight,
    hidden_bias, return_weight, return_bias, forward_scale,
):
    sections = lax.axis_size(SECTION)
    me = lax.axis_index(SECTION).astype(jnp.int32)
    me_row = me.reshape(1)
    images = tokens.shape[0] // sections
    m = images * RP
    rows = D // lax.axis_size(WIDE)
    w = Weights(
        attention_gain, attention_shift, input_projection, query_bias, value_bias, output_projection, output_bias,
        attention_scale, forward_gain, forward_shift, hidden_weight, hidden_bias, return_weight, return_bias,
        forward_scale,
    )
    grids = lax.dynamic_slice_in_dim(patch_grids, me * images, images, 0)
    height, width = grids[:, 0:1], grids[:, 1:2]
    place = lax.broadcasted_iota(jnp.int32, (images, CP), 1)
    live = place < height * width
    column = place % width
    turn = lax.broadcasted_iota(jnp.int32, (images, SPAN), 1)
    gap = jnp.where(turn < CP, -turn, SPAN - turn)
    b = jnp.mod(gap, width)
    a = (gap - b) // width
    entry = lambda p, q: jnp.clip(p + HMAX - 1, 0, 2 * HMAX - 2) * QW + jnp.clip(q + WMAX - 1, 0, QW - 1)
    index = jnp.stack([entry(a, b), entry(a + 1, b - width)], axis=1).reshape(2 * images, 1, SPAN)
    table = jnp.transpose(relative_table, (0, 2, 1)).reshape(LAYERS * HEADS, REL)
    table = jnp.pad(table, ((0, 0), (0, TABLE - REL)))
    tables = Tables(
        live[:, :RP].reshape(m, 1).astype(F32),
        jnp.where(live, 0.0, -1e9).astype(F32).reshape(images, 1, CP),
        (column[:, :RP, None] >= column[:, None, :]).astype(F32),
        bias_rows(table, index),
    )
    high, core = me // 2, me % 2
    order = jnp.stack([2 * (1 - high) + 1 - core, 2 * high + 1 - core, 2 * (1 - high) + core, 2 * high + core])
    cross, kept, pieces = forward(images, sections, me_row, order, tokens, cotangent, w, tables)

    names = wide_names()
    mine_bits = jnp.stack([own_bit(*name) for name in names]).astype(jnp.int32)
    own = own_bit(WIDE, 1).astype(jnp.int32).reshape(1)
    first = names[-1]
    core_flip = lambda sent: flip(sent, SECTION, 1)

    def launch(a_send, a_keep, b_send, b_keep):
        a_got, b_got = flip(a_send, *ACROSS), flip(b_send, *first)
        across = [ACROSS] + names[:-1]
        chunks = []
        for j in range(a_keep.shape[0]):
            chunks.append((
                Chunk(a_keep, a_got, j, names, list(reversed(names)), rows),
                Chunk(b_keep, b_got, j, across, [ACROSS] + list(reversed(names[:-1])), rows),
            ))
        left, right = zip(*chunks)
        return list(left), list(right), [a_got, b_got]

    def step(groups, after, name, small=None, held=()):
        return combine(groups, mine_bits, after, name, small=small, held=held)

    def finish(groups, after, name, writer, out_shape):
        while any(group[0].order for group in groups):
            after = step([group for group in groups if group[0].order], after, name)
        return combine(groups, mine_bits, after, name, writer, out_shape)

    cross_got = core_flip(cross)
    spec = slot(1, OUT_FEED, m)
    bg, feed_small1, hidden1, hg, sent = first_chain(images, sections, me_row, order, cotangent, cross, kept, w, tables)
    out = feed_keep(
        1, own, rows, cross, cross_got, kept, w, [bg], returned=(cross, cross_got, spec, spec),
        hidden=(hg, core_flip(sent)),
    )
    a1, b1, launched = launch(*out)
    bg, grads_sent, grads, sg1, *small1, feed_small0, hidden0, hg, sent = middle_chain(
        images, sections, me_row, order, bg, cross, kept, w, tables, out[1:2]
    )
    grads_sent, sent = hold([grads_sent, sent], [bg, *launched])
    grads_got = core_flip(grads_sent)
    sent_got = core_flip(sent)
    last = step([a1, b1], [grads_sent], "second")
    spec = pl.BlockSpec((None, m, D), lambda *_: (sections // 2, 0, 0))
    out = feed_keep(
        0, own, rows, cross, cross_got, kept, w, last, returned=(sent, sent_got, spec, spec), hidden=(hg, sent_got)
    )
    a0, b0, _ = launch(*out)
    last = step([a1 + b1], [*out[1:2], grads_got], "third")
    a_send, a_keep, b_send, b_keep = attention_keep(1, own, rows, cross, cross_got, grads, grads_got, w, last)
    pa1, pb1, launched = launch(a_send, a_keep, b_send, b_keep)
    last = [b_keep]
    bg, grads0_sent, grads0, sg0, biases, small0, *pieces = last_chain(
        images, sections, me_row, bg, cross, kept, w, tables, last, pieces
    )
    pieces = [pieces[0]] + [flip(pieces[d], SECTION, d) for d in range(1, sections)]
    rows1 = table_rows(images, sg1, tables, [bg])
    last, (grads0_sent,) = step([a0 + pa1, b0 + pb1, a1 + b1], [rows1], "second", held=[grads0_sent])
    grads0_got = core_flip(grads0_sent)
    (a_keep,) = hold([a_keep], [grads0_got])
    a_send, a_keep, b_send, b_keep = attention_keep(0, own, rows, cross, cross_got, grads0, grads0_got, w, [a_keep])
    rows0 = table_rows(images, sg0, tables, [a_keep])
    last, (a_send, b_send) = step([a0 + b0], [rows0, *a1[0].arrived(), *b1[0].arrived()], "third", held=[a_send, b_send])
    pa0, pb0, _ = launch(a_send, a_keep, b_send, b_keep)
    core_sent, core_kept = pack(
        me_row, sections, index, (rows0, rows1), (small0, small1[1]), (feed_small0, feed_small1),
        (biases, small1[0]), (hidden0, hidden1), last,
    )
    small = Small(core_kept, core_flip(core_sent))
    last = step([a0 + b0, pa1 + pb1], [core_kept], "fourth", small)
    last = step([pa0, pb0], last, "second", small)
    last = step([pa0 + pb0, pa1 + pb1], [*last, *a0[0].arrived()], "third", small)

    def write_feed(outs, totals):
        for layer in range(LAYERS):
            ra, ha, rb, hb = totals[4 * layer : 4 * layer + 4]
            half = D // 2
            outs[0][layer, :, :half] = ha
            outs[0][layer, :, half:] = hb
            outs[1][layer, :, :half] = ra
            outs[1][layer, :, half:] = rb

    def write_attention(outs, totals):
        part = 3 * D // sections
        for layer in range(LAYERS):
            left, right = totals[2 * layer], totals[2 * layer + 1]
            outs[0][layer, :, : D // 2] = left
            outs[0][layer, :, D // 2 :] = right[:, : part - D // 2]
            outs[1][layer] = right[:, part - D // 2 :]

    shape = lambda *s: jax.ShapeDtypeStruct(s, F32)
    wide = FF // sections
    hidden_grad, return_grad = finish(
        [a0 + b0, a1 + b1], last, "last", write_feed, [shape(LAYERS, rows, wide)] * 2
    )
    last = step([pa0 + pb0], [hidden_grad], "fourth", small)
    layer_output, input_grad = assemble(me_row, pieces, last)
    projection_grad, out_grad = finish(
        [pa0 + pb0, pa1 + pb1], [layer_output], "last", write_attention,
        [shape(LAYERS, rows, 3 * D // sections), shape(LAYERS, rows, D // sections)],
    )
    while small.order:
        last = combine([], mine_bits, [], "more", small=small)
    vectors = unpack(small, sections, [out_grad])
    gain, shift, out_shift, scale, fgain, fshift, return_shift, fscale, query, value, hidden_shift, table_grad = vectors
    return (
        jnp.swapaxes(layer_output, 1, 2), jnp.swapaxes(input_grad, 1, 2), gain, shift, projection_grad, query, value, jnp.transpose(table_grad, (1, 2, 0)), out_grad, out_shift, scale,
        fgain, fshift, hidden_grad, hidden_shift, jnp.swapaxes(return_grad, 1, 2), return_shift, fscale,
    )


def solution(mesh):
    three, two = P(WIDE, None, SECTION), P(None, SECTION)
    weight = P(None, WIDE, SECTION)
    return jax.shard_map(
        on_device,
        mesh=mesh,
        in_specs=(P(WIDE, None, None), P(WIDE, None, None), P(WIDE, None)) + (P(),) * 16,
        out_specs=(
            three, three, two, two, weight, two, two, P(None, None, SECTION), weight, two, two, two, two,
            weight, two, P(None, SECTION, WIDE), two, two,
        ),
        check_vma=False,
    )
```
